32 devices in a mesh: expert: 32 (over z, y, x, core), mp: 1.
Axes of the slice: x: 2, y: 2, z: 4, core: 2. Of those that a mesh axis runs over, the one named last changes fastest.
Arguments:
- hidden_state: bfloat16 [4096, 2048], P('expert', 'mp'), as said below
- context: bfloat16 [4096, 2048], P('expert', 'mp'), may hold values from -6 to 6
- out_proj: bfloat16 [2048, 2048], P('mp', 'expert'), may hold values from -0.125 to 0.125
- norm_gain: bfloat16 [2048], P('mp'), may hold values from 0.25 to 1.75
- router_weight: float32 [2048, 32], P('mp'), as said below
- expert_in: bfloat16 [32, 2048, 2, 1408], P('expert', None, None, 'mp'), may hold values from -0.125 to 0.125
- expert_out: bfloat16 [32, 1408, 2048], P('expert', 'mp'), may hold values from -0.15625 to 0.15625
- shared_in: bfloat16 [2048, 2, 2816], P('expert', None, 'mp'), may hold values from -0.125 to 0.125
- shared_out: bfloat16 [2816, 2048], P('mp', 'expert'), may hold values from -0.109375 to 0.109375
- route_ids: int32 [4096, 6], P('expert'), may hold values from 0 to 31, all different within a row; in each aligned block of 128 rows (0 to 127, 128 to 255, ...) at most 40 rows name the same one
Outputs:
- output: float32 [4096, 2048], P('expert', 'mp')
The draws below stay inside these ranges and needn't reach their ends.
Inputs may be any that keep to these rules, and one draw needn't show every extreme that they name: `route_ids`: each row names 6 different experts; among the rows of one index of the expert axis no expert is named by more than 40 rows. `router_weight`: finite float32 router columns; no range is promised. `hidden_state`: finite values; no range is promised.
All inputs are finite; a program needn't handle non-finite values.
Results may differ from the reference program's by a relative error of at most 0.0025.
Values may be sent and summed in bfloat16 or wider, within the bound.
No kernel may reach another device: no remote copies, remote signals or barrier semaphores. Data moves between devices by JAX's collectives and lax.ppermute only.
A program may use at most 128 MiB of HBM per device.

```python
import math
import jax
import jax.numpy as jnp
import numpy as np
from jax import lax

D = 2048
FFE = 1408
TOP = 6
TOK_DEV = 128
EXPERTS = 32
FFS = 2816
CAP = 40
TOKENS = 4096
N_MP = 1


def draw_router_weight(key, part):
    values = jax.random.normal(jax.random.fold_in(key, 11), (D, EXPERTS), jnp.float32)
    return values * (0.4 / math.sqrt(D))


def draw_hidden_state(key, part):
    column = jnp.arange(D, dtype=jnp.float32) / (D - 1)
    scales = jnp.exp(math.log(0.4) + column * (math.log(3.0) - math.log(0.4)))
    values = jnp.clip(jax.random.normal(key, (TOKENS, D), jnp.float32), -6.0, 6.0)
    return (values * scales[None, :]).astype(jnp.bfloat16)


def block_scale(rng, dims, cuts, smallest, largest):
    def one(dim, shards_of):
        heights = jax.random.uniform(jax.random.fold_in(jax.random.fold_in(rng, 6), dim), (shards_of,), jnp.float32, smallest / len(cuts), largest / len(cuts))
        return jnp.repeat(jnp.exp(heights), dims[dim] // shards_of).reshape((-1,) + (1,) * (len(dims) - dim - 1))

    gain = one(*cuts[0])
    for cut in cuts[1:]:
        gain = gain * one(*cut)
    return gain


def assign_block(key, own, number, rows, amount, top, reach, skew):
    order = jax.random.permutation(key, amount)
    crowded, usual = shares(amount, rows * top, reach, skew, True), shares(amount, rows * top, reach, skew, False)
    places = jnp.arange(amount)

    def named(lengths, offset_by):
        used = int((lengths > 0).sum())
        fixed = max(1, used // 4)
        shifted = fixed + (places - fixed + offset_by * (used - fixed)) % max(1, amount - fixed)
        return jnp.zeros((amount,), jnp.int32).at[order[jnp.where(places < fixed, places, shifted)]].set(jnp.asarray(lengths, jnp.int32))

    lengths = jnp.where(number % 4 == 0, named(crowded, number // 4), named(usual, number - number // 4 - 1))
    mixed = jax.random.permutation(jax.random.fold_in(own, 3), amount)
    giver, sink = mixed[0:amount // 2 * 2:2], mixed[1:amount // 2 * 2:2]
    slack = jnp.minimum(lengths[giver] - 1, reach - lengths[sink]) // 2
    slack = jnp.where((giver == order[0]) | (sink == order[0]) | (lengths[sink] == 0), 0, jnp.maximum(slack, 0))
    shifted = jax.random.randint(jax.random.fold_in(own, 4), (amount // 2,), 0, 1 << 20) % (slack + 1)
    lengths = lengths.at[giver].add(-shifted).at[sink].add(shifted)
    items = jnp.searchsorted(jnp.cumsum(lengths), jnp.arange(rows * top), side="right").astype(jnp.int32)
    table = items.reshape(top, rows).T
    table = table[jax.random.permutation(jax.random.fold_in(own, 1), rows)]
    offset_by = jax.random.randint(jax.random.fold_in(own, 2), (rows, 1), 0, top)
    return jnp.take_along_axis(table, (jnp.arange(top)[None, :] + offset_by) % top, axis=1)


def shares(number_of, total, bound, slope, full):
    loads = [(1 << 20) // math.isqrt(grade ** slope) + 1 for grade in range(1, number_of + 1)]
    largest = bound if full else min(bound, max(-(-total // number_of), total * loads[0] // sum(loads)))
    least = 1 if total - largest >= number_of - 1 else 0
    holding, rest = [largest] + [least] * (number_of - 1), total - largest - least * (number_of - 1)
    while rest > 0:
        candidates = [i for i in range(1, number_of) if holding[i] < largest] or [i for i in range(1, number_of) if holding[i] < bound]
        whole, remaining = sum([loads[i] for i in candidates]), rest
        for i in candidates:
            addition = min(bound - holding[i], max(1, remaining * loads[i] // whole), rest)
            holding[i] = holding[i] + addition
            rest = rest - addition
    return np.array(holding)


def gaussian(key, extent, spread, reach, pieces=(), kind=jnp.bfloat16):
    array = spread * jax.random.normal(key, extent, jnp.float32)
    if pieces:
        array = array * block_scale(key, extent, pieces, -0.22, 0.18)
    return jnp.clip(array, -reach, reach).astype(kind)


def setup_inputs(seed: int = 0) -> dict:
    streams_of = jax.random.split(jax.random.key(seed), 11)
    hidden_state = draw_hidden_state(jax.random.fold_in(streams_of[10], 71), 0)
    context = gaussian(streams_of[1], (TOKENS, D), 1.0, 6.0, ((0, 32),))
    out_proj = gaussian(streams_of[2], (D, D), D ** -0.5, 0.125, ((1, 32),))
    norm_gain = jnp.clip(1.0 + 0.15 * jax.random.normal(streams_of[3], (D,), jnp.float32), 0.25, 1.75).astype(jnp.bfloat16)
    router_weight = draw_router_weight(jax.random.fold_in(streams_of[10], 71), 0)
    expert_in = gaussian(streams_of[5], (EXPERTS, D, 2, FFE), D ** -0.5, 0.125, ((0, 32),))
    expert_out = gaussian(streams_of[6], (EXPERTS, FFE, D), FFE ** -0.5, 0.15625, ((0, 32),))
    shared_in = gaussian(streams_of[7], (D, 2, FFS), D ** -0.5, 0.125, ((0, 32),))
    shared_out = gaussian(streams_of[8], (FFS, D), FFS ** -0.5, 0.109375, ((1, 32),))
    route_ids_keys = jax.random.split(jax.random.fold_in(streams_of[9], 1), TOKENS // TOK_DEV)
    route_ids_turns = jax.random.permutation(jax.random.fold_in(streams_of[9], 3), TOKENS // TOK_DEV)
    route_ids = jax.vmap(lambda own, number: assign_block(jax.random.fold_in(streams_of[9], 2), own, number, TOK_DEV, EXPERTS, TOP, CAP, 2))(route_ids_keys, route_ids_turns).reshape((TOKENS, TOP))
    return {"hidden_state": hidden_state, "context": context, "out_proj": out_proj, "norm_gain": norm_gain, "router_weight": router_weight, "expert_in": expert_in, "expert_out": expert_out, "shared_in": shared_in, "shared_out": shared_out, "route_ids": route_ids}


def reference(hidden_state, context, out_proj, norm_gain, router_weight, expert_in, expert_out, shared_in, shared_out, route_ids):
    attn = jnp.dot(context, out_proj, preferred_element_type=jnp.float32)
    mixed = hidden_state.astype(jnp.float32) + attn
    inverse = lax.rsqrt(lax.optimization_barrier(jnp.mean(mixed * mixed, axis=1, keepdims=True)) + 1e-06)
    normed32 = mixed * inverse * norm_gain.astype(jnp.float32)
    normed = normed32.astype(jnp.bfloat16)
    logits = jnp.dot(normed32, router_weight, precision=lax.Precision.HIGHEST)
    chosen = jnp.take_along_axis(logits, route_ids, axis=1)
    gates = jax.nn.softmax(chosen, axis=1)
    both = jnp.dot(normed, shared_in.reshape(D, 2 * FFS), preferred_element_type=jnp.float32).reshape(-1, 2, FFS)
    shared_hidden = (jax.nn.silu(both[:, 0]) * both[:, 1]).astype(jnp.bfloat16)
    shared = jnp.dot(shared_hidden, shared_out, preferred_element_type=jnp.float32)
    blocks = TOKENS // TOK_DEV
    flat = route_ids.reshape(blocks, TOK_DEV * TOP)
    onehot = (flat[:, :, None] == jnp.arange(EXPERTS, dtype=jnp.int32)[None, None, :]).astype(jnp.int32)
    position = lax.optimization_barrier(jnp.sum(onehot * jnp.cumsum(onehot, axis=1), axis=2)) - 1
    row_of = (jnp.arange(TOK_DEV * TOP, dtype=jnp.int32) // TOP)[None, :] + (jnp.arange(blocks, dtype=jnp.int32) * TOK_DEV)[:, None]
    block_of = jnp.broadcast_to(jnp.arange(blocks, dtype=jnp.int32)[:, None], flat.shape)
    table = jnp.zeros((EXPERTS, blocks, CAP), jnp.int32).at[flat, block_of, position].set(row_of)
    weight_table = jnp.zeros((EXPERTS, blocks, CAP), jnp.float32).at[flat, block_of, position].set(gates.reshape(blocks, TOK_DEV * TOP))
    quarter = FFE // N_MP

    def one_expert(routed, expert):
        rows = table[expert].reshape(-1)
        weights = weight_table[expert].reshape(-1)
        taken = normed[rows]
        inner = jnp.dot(taken, expert_in[expert].reshape(D, 2 * FFE), preferred_element_type=jnp.float32).reshape(-1, 2, FFE)
        hidden = (jax.nn.silu(inner[:, 0]) * inner[:, 1]).astype(jnp.bfloat16)
        parts = jnp.einsum('sqf,qfd->qsd', hidden.reshape(-1, N_MP, quarter).astype(jnp.float32), expert_out[expert].reshape(N_MP, quarter, D).astype(jnp.float32))
        rounded = lax.optimization_barrier(parts.astype(jnp.bfloat16))
        total = lax.optimization_barrier(jnp.sum(rounded.astype(jnp.float32), axis=0))
        total = lax.optimization_barrier(total.astype(jnp.bfloat16)).astype(jnp.float32)
        routed = routed.at[rows].add(weights[:, None] * total)
        return (routed, None)
    routed, _ = lax.scan(one_expert, jnp.zeros((TOKENS, D), jnp.float32), jnp.arange(EXPERTS, dtype=jnp.int32))
    return mixed + routed + shared
```

```python
import functools

import jax
import jax.numpy as jnp
from jax import lax
from jax.experimental import pallas as pl
from jax.experimental.pallas import tpu as pltpu
from jax.sharding import PartitionSpec as P

LANES = 128
LAYER = 8


def capacity_of(rows, top, experts):
    return max(2, min(rows, rows * top // experts * 5 // 3))


def general(
    hidden_state,
    context,
    out_proj,
    norm_gain,
    router_weight,
    expert_in,
    expert_out,
    shared_in,
    shared_out,
    route_ids,
):
    rows_here, top = route_ids.shape
    experts = router_weight.shape[1]
    width = out_proj.shape[0] * lax.axis_size("mp")
    capacity = capacity_of(rows_here, top, experts)
    partial_attn = jnp.dot(
        context,
        lax.all_gather(out_proj, "expert", axis=1, tiled=True),
        preferred_element_type=jnp.float32,
    )
    attn = lax.psum_scatter(partial_attn, "mp", scatter_dimension=1, tiled=True)
    mixed = hidden_state.astype(jnp.float32) + attn
    gain = norm_gain.astype(jnp.float32)
    squares = lax.psum(jnp.sum(mixed * mixed, axis=1), "mp")
    inverse = lax.rsqrt(squares / width + 1e-06)[:, None]
    normed32 = mixed * inverse * gain
    logits = lax.psum(jnp.dot(normed32, router_weight, precision=lax.Precision.HIGHEST), "mp")
    normed = normed32.astype(jnp.bfloat16)
    gates = jax.nn.softmax(jnp.take_along_axis(logits, route_ids, axis=1), axis=1)
    full_rows = lax.all_gather(normed, "mp", axis=1, tiled=True)
    shared_width = shared_in.shape[2]
    piece = lax.all_gather(shared_in, "expert", axis=0, tiled=True)
    shared_both = jnp.dot(
        full_rows,
        piece.reshape(piece.shape[0], 2 * shared_width),
        preferred_element_type=jnp.float32,
    )
    shared_both = shared_both.reshape(rows_here, 2, shared_width)
    shared_hidden = (jax.nn.silu(shared_both[:, 0]) * shared_both[:, 1]).astype(jnp.bfloat16)
    shared_part = jnp.dot(
        shared_hidden,
        lax.all_gather(shared_out, "expert", axis=1, tiled=True),
        preferred_element_type=jnp.float32,
    )
    flat = route_ids.reshape(-1)
    onehot = (flat[:, None] == jnp.arange(experts, dtype=jnp.int32)[None, :]).astype(jnp.int32)
    position = jnp.sum(onehot * jnp.cumsum(onehot, axis=0), axis=1) - 1
    slot_of = flat * capacity + position
    source = (
        jnp.zeros((experts * capacity,), jnp.int32)
        .at[slot_of]
        .set(jnp.arange(flat.shape[0], dtype=jnp.int32) // top)
    )
    filled = jnp.zeros((experts * capacity,), jnp.bool_).at[slot_of].set(True)
    outgoing = jnp.where(filled[:, None], normed[source], jnp.zeros((), jnp.bfloat16)).reshape(
        experts, capacity, normed.shape[1]
    )
    quarter = expert_in.shape[3]
    weights_in = expert_in[0].reshape(width, 2 * quarter)
    incoming = lax.all_to_all(outgoing, "expert", split_axis=0, concat_axis=0, tiled=True)
    sources = incoming.shape[0]
    items = incoming.shape[1]
    gathered = lax.all_gather(incoming, "mp", axis=2, tiled=True).reshape(sources * items, width)
    inner = jnp.dot(gathered, weights_in, preferred_element_type=jnp.float32).reshape(
        -1, 2, quarter
    )
    hidden = (jax.nn.silu(inner[:, 0]) * inner[:, 1]).astype(jnp.bfloat16)
    partial_out = jnp.dot(hidden, expert_out[0], preferred_element_type=jnp.float32).astype(
        jnp.bfloat16
    )
    partial_out = partial_out.reshape(sources, items, width)
    result = lax.all_to_all(partial_out, "expert", split_axis=0, concat_axis=0, tiled=True)
    picked = result.reshape(experts * capacity, result.shape[2])[slot_of]
    slot_total = lax.psum_scatter(
        lax.optimization_barrier(picked).astype(jnp.float32).astype(jnp.bfloat16),
        "mp",
        scatter_dimension=1,
        tiled=True,
    )
    expert_sum = lax.optimization_barrier(slot_total).astype(jnp.float32)
    expert_sum = expert_sum.reshape(rows_here, top, expert_sum.shape[1])
    routed = jnp.sum(gates[:, :, None] * expert_sum, axis=1)
    shared = lax.psum_scatter(shared_part, "mp", scatter_dimension=1, tiled=True)
    return mixed + routed + shared


def swap(x, bit):
    n = lax.axis_size("expert")
    return lax.ppermute(x, "expert", [(i, i ^ bit) for i in range(n)])


def turn(x, layers):
    n = lax.axis_size("expert")
    return lax.ppermute(x, "expert", [(i, (i + LAYER * layers) % n) for i in range(n)])


def silu(v):
    return v / (1.0 + jnp.exp(-v))


def chunk_kernel(
    cap,
    idx_ref,
    gate_ref,
    wsi_ref,
    wso_ref,
    l0,
    r0,
    l1,
    r1,
    sl0,
    sr0,
    sl1,
    sr1,
    win_ref,
    wout_ref,
    keep_ref,
    send_ref,
    xs,
    win_v,
    wout_v,
    pick,
    place,
    gate_col,
    rows_v,
    hid_v,
    hs_v,
    y_v,
    keep_v,
    send_v,
    x_sem,
    w_sem,
    o_sem,
):
    rows = l0.shape[0] // 2
    wide, half = xs.shape[1], xs.shape[1] // 2
    slots = 8 * cap
    tiles = win_ref.shape[0]
    part = 4 * rows

    copies = []

    def fetch(src, lo, n, row, col):
        k = len(copies)
        c = pltpu.make_async_copy(
            src.at[pl.ds(lo, n)], xs.at[pl.ds(row, n), pl.ds(col, half)], x_sem.at[k]
        )
        c.start()
        copies.append(c)

    for base, (a0, b0, a1, b1) in enumerate(((l0, r0, l1, r1), (sl0, sr0, sl1, sr1))):
        at = base * part
        fetch(a0, 0, 2 * rows, at, 0)
        fetch(b0, 0, 2 * rows, at + 2 * rows, 0)
        fetch(a1, 0, rows, at, half)
        fetch(a1, rows, rows, at + 2 * rows, half)
        fetch(b1, 0, rows, at + rows, half)
        fetch(b1, rows, rows, at + 3 * rows, half)
    weights = []
    for t in range(tiles):
        c = pltpu.make_async_copy(win_ref.at[t], win_v.at[t], w_sem.at[t])
        c.start()
        weights.append(c)
    last = pltpu.make_async_copy(wout_ref, wout_v, w_sem.at[tiles])
    last.start()

    g = jnp.concatenate([gate_ref[pl.ds(idx_ref[p], 1), :] for p in range(8)], axis=0)
    chosen = g > 0.0
    r_io = lax.broadcasted_iota(jnp.int32, (rows, rows), 0)
    c_io = lax.broadcasted_iota(jnp.int32, (rows, rows), 1)
    upto = jnp.where(r_io <= c_io, 1.0, 0.0).astype(jnp.bfloat16)
    count = jnp.dot(
        jnp.where(chosen, 1.0, 0.0).astype(jnp.bfloat16), upto, preferred_element_type=jnp.float32
    ).astype(jnp.int32)
    first = lax.broadcasted_iota(jnp.int32, (8, rows), 0) * cap
    slot = jnp.where(chosen, first + count - 1, -1)
    eye = r_io == c_io
    slot_rows = lax.broadcasted_iota(jnp.int32, (slots, rows), 0)
    slot_cols = lax.broadcasted_iota(jnp.int32, (rows, slots), 1)
    for p in range(8):
        row = slot[p : p + 1, :]
        pick[:, pl.ds(p * rows, rows)] = jnp.where(slot_rows == row, 1.0, 0.0).astype(jnp.bfloat16)
        col = jnp.sum(jnp.where(eye, row, 0), axis=1, keepdims=True)
        place[pl.ds(p * rows, rows), :] = jnp.where(slot_cols == col, 1.0, 0.0).astype(jnp.bfloat16)
        gcol = jnp.sum(jnp.where(eye, g[p : p + 1, :], 0.0), axis=1, keepdims=True)
        gate_col[pl.ds(p * rows, rows), :] = jnp.broadcast_to(gcol, (rows, LANES))

    for c in copies:
        c.wait()

    step = min(512, wide)
    for n in range(0, wide, step):
        rows_v[:, pl.ds(n, step)] = jnp.dot(
            pick[...], xs[:, pl.ds(n, step)], preferred_element_type=jnp.float32
        ).astype(jnp.bfloat16)
    hp = hs_v.shape[1]
    for m in range(0, 8 * rows, 2 * rows):
        both = jnp.dot(xs[pl.ds(m, 2 * rows), :], wsi_ref[...], preferred_element_type=jnp.float32)
        hs_v[pl.ds(m, 2 * rows), :] = (silu(both[:, :hp]) * both[:, hp:]).astype(jnp.bfloat16)

    tile = win_v.shape[2] // 2
    for t in range(tiles):
        weights[t].wait()
        both = jnp.dot(rows_v[...], win_v[t], preferred_element_type=jnp.float32)
        hid_v[:, pl.ds(t * tile, tile)] = (silu(both[:, :tile]) * both[:, tile:]).astype(
            jnp.bfloat16
        )
    last.wait()
    for n in range(0, wide, step):
        y_v[:, pl.ds(n, step)] = jnp.dot(
            hid_v[...], wout_v[:, pl.ds(n, step)], preferred_element_type=jnp.float32
        ).astype(jnp.bfloat16)
    step = min(256, half)
    outs = []
    for n in range(0, wide, step):
        routed = jnp.dot(place[...], y_v[:, pl.ds(n, step)], preferred_element_type=jnp.float32)
        shared = jnp.dot(hs_v[...], wso_ref[:, pl.ds(n, step)], preferred_element_type=jnp.float32)
        total = routed * gate_col[:, 0:1] + shared
        keep_v[:, pl.ds(n, step)] = total[:part]
        send_v[:, pl.ds(n, step)] = total[part:].astype(jnp.bfloat16)
        if (n + step) % half == 0:
            k = len(outs)
            cols = pl.ds(n + step - half, half)
            for c in (
                pltpu.make_async_copy(send_v.at[:, cols], send_ref.at[:, cols], o_sem.at[k]),
                pltpu.make_async_copy(keep_v.at[:, cols], keep_ref.at[:, cols], o_sem.at[k + 1]),
            ):
                c.start()
                outs.append(c)
    for c in outs:
        c.wait()


def chunk_work(idx, gates, wsi, wso, pieces, win, wout, cap):
    rows = pieces[0].shape[0] // 2
    wide = pieces[0].shape[1] * 2
    tiles, _, tile2 = win.shape
    hidden = wout.shape[0]
    slots = 8 * cap
    hp = wso.shape[0]
    bf, f32 = jnp.bfloat16, jnp.float32
    vmem = pl.BlockSpec(memory_space=pltpu.VMEM)
    hbm = pl.BlockSpec(memory_space=pl.ANY)
    flops = 2 * (
        2 * slots * 8 * rows * wide
        + slots * hidden * wide * 3
        + 8 * rows * wide * 3 * hp
    )
    return pl.pallas_call(
        functools.partial(chunk_kernel, cap),
        out_shape=(
            jax.ShapeDtypeStruct((4 * rows, wide), f32),
            jax.ShapeDtypeStruct((4 * rows, wide), bf),
        ),
        in_specs=[pl.BlockSpec(memory_space=pltpu.SMEM), vmem, vmem, vmem] + [hbm] * 10,
        out_specs=(hbm, hbm),
        scratch_shapes=[
            pltpu.VMEM((8 * rows, wide), bf),
            pltpu.VMEM((tiles, wide, tile2), bf),
            pltpu.VMEM((hidden, wide), bf),
            pltpu.VMEM((slots, 8 * rows), bf),
            pltpu.VMEM((8 * rows, slots), bf),
            pltpu.VMEM((8 * rows, LANES), f32),
            pltpu.VMEM((slots, wide), bf),
            pltpu.VMEM((slots, hidden), bf),
            pltpu.VMEM((8 * rows, hp), bf),
            pltpu.VMEM((slots, wide), bf),
            pltpu.VMEM((4 * rows, wide), f32),
            pltpu.VMEM((4 * rows, wide), bf),
            pltpu.SemaphoreType.DMA((12,)),
            pltpu.SemaphoreType.DMA((tiles + 1,)),
            pltpu.SemaphoreType.DMA((4,)),
        ],
        compiler_params=pltpu.CompilerParams(vmem_limit_bytes=56 * 1024 * 1024),
        cost_estimate=pl.CostEstimate(
            flops=flops, bytes_accessed=40 * 1024 * 1024, transcendentals=slots * hidden
        ),
    )(idx, gates, wsi, wso, *pieces, win, wout)


def spread(block):
    half = block.shape[1] // 2
    h0, h1 = block[:, :half], block[:, half:]
    l0 = jnp.concatenate([h0, swap(h0, 2)], axis=0)
    l1 = jnp.concatenate([h1, swap(h1, 4)], axis=0)
    r0 = swap(l0, 4)
    r1 = swap(l1, 2)
    mine = (l0, r0, l1, r1)
    return mine + tuple(swap(p, 1) for p in mine)


def collect(keep, send):
    bf, f32 = jnp.bfloat16, jnp.float32
    rows, wide = keep.shape[0] // 4, keep.shape[1]
    half = wide // 2
    both = keep + swap(send, 1).astype(f32)
    low, high = both[:, :half], both[:, half:]
    low = low[: 2 * rows] + swap(low[2 * rows :].astype(bf), 4).astype(f32)
    far = jnp.concatenate([high[rows : 2 * rows], high[3 * rows :]], axis=0)
    near = jnp.concatenate([high[:rows], high[2 * rows : 3 * rows]], axis=0)
    high = near + swap(far.astype(bf), 2).astype(f32)
    low = low[:rows] + swap(low[rows:].astype(bf), 2).astype(f32)
    high = high[:rows] + swap(high[rows:].astype(bf), 4).astype(f32)
    return jnp.concatenate([low, high], axis=1)


def whole_rows(
    hidden_state,
    context,
    out_proj,
    norm_gain,
    router_weight,
    expert_in,
    expert_out,
    shared_in,
    shared_out,
    route_ids,
):
    bf, f32 = jnp.bfloat16, jnp.float32
    n = lax.axis_size("expert")
    layers = n // LAYER
    me = lax.axis_index("expert")
    rows, top = route_ids.shape
    experts = router_weight.shape[1]
    width = out_proj.shape[0]
    cap = capacity_of(rows, top, experts)

    hidden = expert_out.shape[1]
    tile = LANES if hidden % LANES == 0 else hidden
    win = (
        expert_in[0]
        .reshape(width, 2, hidden // tile, tile)
        .transpose(2, 0, 1, 3)
        .reshape(hidden // tile, width, 2 * tile)
    )
    wout = expert_out[0]

    shared_width = shared_in.shape[2]
    own = shared_width // n
    depth = shared_in.shape[0]
    three = jnp.concatenate([shared_in, shared_out.T[:, None, :]], axis=1)
    three = three.reshape(depth * 3, n, own).transpose(1, 0, 2)
    three = lax.all_to_all(three, "expert", split_axis=0, concat_axis=0, tiled=True)
    three = three.reshape(width, 3, own)
    hp = -(-own // LANES) * LANES
    three = jnp.pad(three, ((0, 0), (0, 0), (0, hp - own)))
    wsi = three[:, :2].reshape(width, 2 * hp)
    wso = three[:, 2].T

    attn = jnp.dot(
        context,
        lax.all_gather(out_proj, "expert", axis=1, tiled=True),
        preferred_element_type=f32,
    )
    mixed = hidden_state.astype(f32) + attn
    inverse = lax.rsqrt(jnp.mean(mixed * mixed, axis=1, keepdims=True) + 1e-06)
    normed32 = mixed * inverse * norm_gain.astype(f32)
    normed = normed32.astype(bf)
    logits = jnp.dot(normed32, router_weight, precision=lax.Precision.HIGHEST)
    named = jnp.any(
        route_ids[:, :, None] == jnp.arange(experts, dtype=jnp.int32)[None, None, :], axis=1
    )
    highest = jnp.max(jnp.where(named, logits, -jnp.inf), axis=1, keepdims=True)
    raised = jnp.where(named, jnp.exp(logits - highest), 0.0)
    gates = raised / jnp.sum(raised, axis=1, keepdims=True)
    all_gates = lax.all_gather(gates.T, "expert", axis=0)
    own_gates = lax.dynamic_index_in_dim(all_gates, me, axis=1, keepdims=False)

    low = me % LAYER
    order = jnp.array([2 * (p % 4) + p // 4 for p in range(8)], jnp.int32)
    total = mixed
    blocks = [normed] + [turn(normed, k) for k in range(1, layers)]
    for k in list(range(1, layers)) + [0]:
        idx = (me // LAYER - k) % layers * LAYER + jnp.bitwise_xor(low, order)
        keep, send = chunk_work(
            idx.astype(jnp.int32), own_gates, wsi, wso, spread(blocks[k]), win, wout, cap
        )
        part = collect(keep, send)
        if k:
            part = turn(part.astype(bf), layers - k).astype(f32)
        total = total + part
    return total


def solution(mesh):
    n, mp = mesh.shape["expert"], mesh.shape["mp"]
    per_device = whole_rows if mp == 1 and n % LAYER == 0 else general
    return jax.shard_map(
        per_device,
        mesh=mesh,
        in_specs=(
            P("expert", "mp"),
            P("expert", "mp"),
            P("mp", "expert"),
            P("mp"),
            P("mp", None),
            P("expert", None, None, "mp"),
            P("expert", "mp", None),
            P("expert", None, "mp"),
            P("mp", "expert"),
            P("expert", None),
        ),
        out_specs=P("expert", "mp"),
        check_vma=False,
    )
```

```python
import functools

import jax
import jax.numpy as jnp
from jax import lax
from jax.experimental import pallas as pl
from jax.experimental.pallas import tpu as pltpu
from jax.sharding import PartitionSpec as P

LANES = 128
LAYER = 8


def capacity_of(rows, top, experts):
    return max(2, min(rows, rows * top // experts * 5 // 3))


def general(
    hidden_state,
    context,
    out_proj,
    norm_gain,
    router_weight,
    expert_in,
    expert_out,
    shared_in,
    shared_out,
    route_ids,
):
    rows_here, top = route_ids.shape
    experts = router_weight.shape[1]
    width = out_proj.shape[0] * lax.axis_size("mp")
    capacity = capacity_of(rows_here, top, experts)
    partial_attn = jnp.dot(
        context,
        lax.all_gather(out_proj, "expert", axis=1, tiled=True),
        preferred_element_type=jnp.float32,
    )
    attn = lax.psum_scatter(partial_attn, "mp", scatter_dimension=1, tiled=True)
    mixed = hidden_state.astype(jnp.float32) + attn
    gain = norm_gain.astype(jnp.float32)
    squares = lax.psum(jnp.sum(mixed * mixed, axis=1), "mp")
    inverse = lax.rsqrt(squares / width + 1e-06)[:, None]
    normed32 = mixed * inverse * gain
    logits = lax.psum(jnp.dot(normed32, router_weight, precision=lax.Precision.HIGHEST), "mp")
    normed = normed32.astype(jnp.bfloat16)
    gates = jax.nn.softmax(jnp.take_along_axis(logits, route_ids, axis=1), axis=1)
    full_rows = lax.all_gather(normed, "mp", axis=1, tiled=True)
    shared_width = shared_in.shape[2]
    piece = lax.all_gather(shared_in, "expert", axis=0, tiled=True)
    shared_both = jnp.dot(
        full_rows,
        piece.reshape(piece.shape[0], 2 * shared_width),
        preferred_element_type=jnp.float32,
    )
    shared_both = shared_both.reshape(rows_here, 2, shared_width)
    shared_hidden = (jax.nn.silu(shared_both[:, 0]) * shared_both[:, 1]).astype(jnp.bfloat16)
    shared_part = jnp.dot(
        shared_hidden,
        lax.all_gather(shared_out, "expert", axis=1, tiled=True),
        preferred_element_type=jnp.float32,
    )
    flat = route_ids.reshape(-1)
    onehot = (flat[:, None] == jnp.arange(experts, dtype=jnp.int32)[None, :]).astype(jnp.int32)
    position = jnp.sum(onehot * jnp.cumsum(onehot, axis=0), axis=1) - 1
    slot_of = flat * capacity + position
    source = (
        jnp.zeros((experts * capacity,), jnp.int32)
        .at[slot_of]
        .set(jnp.arange(flat.shape[0], dtype=jnp.int32) // top)
    )
    filled = jnp.zeros((experts * capacity,), jnp.bool_).at[slot_of].set(True)
    outgoing = jnp.where(filled[:, None], normed[source], jnp.zeros((), jnp.bfloat16)).reshape(
        experts, capacity, normed.shape[1]
    )
    quarter = expert_in.shape[3]
    weights_in = expert_in[0].reshape(width, 2 * quarter)
    incoming = lax.all_to_all(outgoing, "expert", split_axis=0, concat_axis=0, tiled=True)
    sources = incoming.shape[0]
    items = incoming.shape[1]
    gathered = lax.all_gather(incoming, "mp", axis=2, tiled=True).reshape(sources * items, width)
    inner = jnp.dot(gathered, weights_in, preferred_element_type=jnp.float32).reshape(
        -1, 2, quarter
    )
    hidden = (jax.nn.silu(inner[:, 0]) * inner[:, 1]).astype(jnp.bfloat16)
    partial_out = jnp.dot(hidden, expert_out[0], preferred_element_type=jnp.float32).astype(
        jnp.bfloat16
    )
    partial_out = partial_out.reshape(sources, items, width)
    result = lax.all_to_all(partial_out, "expert", split_axis=0, concat_axis=0, tiled=True)
    picked = result.reshape(experts * capacity, result.shape[2])[slot_of]
    slot_total = lax.psum_scatter(
        lax.optimization_barrier(picked).astype(jnp.float32).astype(jnp.bfloat16),
        "mp",
        scatter_dimension=1,
        tiled=True,
    )
    expert_sum = lax.optimization_barrier(slot_total).astype(jnp.float32)
    expert_sum = expert_sum.reshape(rows_here, top, expert_sum.shape[1])
    routed = jnp.sum(gates[:, :, None] * expert_sum, axis=1)
    shared = lax.psum_scatter(shared_part, "mp", scatter_dimension=1, tiled=True)
    return mixed + routed + shared


def swap(x, bit):
    n = lax.axis_size("expert")
    return lax.ppermute(x, "expert", [(i, i ^ bit) for i in range(n)])


def turn(x, layers):
    n = lax.axis_size("expert")
    return lax.ppermute(x, "expert", [(i, (i + LAYER * layers) % n) for i in range(n)])


def silu(v):
    return v / (1.0 + jnp.exp(-v))


def chunk_kernel(
    cap,
    unused,
    idx_ref,
    gate_ref,
    three_ref,
    l0,
    r0,
    l1,
    r1,
    sl0,
    sr0,
    sl1,
    sr1,
    win_ref,
    wout_ref,
    *rest,
):
    (
        keep_ref,
        send_ref,
        xs,
        wsi_v,
        wso_v,
        win_v,
        wout_v,
        pick,
        place,
        gate_col,
        rows_v,
        hid_v,
        hs_v,
        y_v,
        keep_v,
        send_v,
        x_sem,
        w_sem,
        o_sem,
    ) = rest[unused:]
    rows = l0.shape[0] // 2
    wide, half = xs.shape[1], xs.shape[1] // 2
    slots = 8 * cap
    tiles = win_v.shape[0]
    tile = win_v.shape[3] // 2
    hp = hs_v.shape[1]
    part = 4 * rows

    copies = []

    def fetch(src, dst):
        c = pltpu.make_async_copy(src, dst, x_sem.at[len(copies)])
        c.start()
        copies.append(c)

    def fetch_rows(src, lo, n, row, col):
        fetch(src.at[pl.ds(lo, n)], xs.at[pl.ds(row, n), pl.ds(col, half)])

    for base, (a0, b0, a1, b1) in enumerate(((l0, r0, l1, r1), (sl0, sr0, sl1, sr1))):
        at = base * part
        fetch_rows(a0, 0, 2 * rows, at, 0)
        fetch_rows(b0, 0, 2 * rows, at + 2 * rows, 0)
        fetch_rows(a1, 0, rows, at, half)
        fetch_rows(a1, rows, rows, at + 2 * rows, half)
        fetch_rows(b1, 0, rows, at + rows, half)
        fetch_rows(b1, rows, rows, at + 3 * rows, half)
    fetch(three_ref.at[:, 0], wsi_v.at[:, :, pl.ds(0, hp)])
    fetch(three_ref.at[:, 1], wsi_v.at[:, :, pl.ds(hp, hp)])
    fetch(three_ref.at[:, 2], wso_v)

    g = jnp.concatenate([gate_ref[pl.ds(idx_ref[p], 1), :] for p in range(8)], axis=0)
    chosen = g > 0.0
    r_io = lax.broadcasted_iota(jnp.int32, (rows, rows), 0)
    c_io = lax.broadcasted_iota(jnp.int32, (rows, rows), 1)
    upto = jnp.where(r_io <= c_io, 1.0, 0.0).astype(jnp.bfloat16)
    count = jnp.dot(
        jnp.where(chosen, 1.0, 0.0).astype(jnp.bfloat16), upto, preferred_element_type=jnp.float32
    ).astype(jnp.int32)
    first = lax.broadcasted_iota(jnp.int32, (8, rows), 0) * cap
    slot = jnp.where(chosen, first + count - 1, -1)
    eye = r_io == c_io
    slot_rows = lax.broadcasted_iota(jnp.int32, (slots, rows), 0)
    slot_cols = lax.broadcasted_iota(jnp.int32, (rows, slots), 1)
    for p in range(8):
        row = slot[p : p + 1, :]
        pick[:, pl.ds(p * rows, rows)] = jnp.where(slot_rows == row, 1.0, 0.0).astype(jnp.bfloat16)
        col = jnp.sum(jnp.where(eye, row, 0), axis=1, keepdims=True)
        place[pl.ds(p * rows, rows), :] = jnp.where(slot_cols == col, 1.0, 0.0).astype(jnp.bfloat16)
        gcol = jnp.sum(jnp.where(eye, g[p : p + 1, :], 0.0), axis=1, keepdims=True)
        gate_col[pl.ds(p * rows, rows), :] = jnp.broadcast_to(gcol, (rows, LANES))

    for c in copies:
        c.wait()

    weights = []
    for t in range(tiles):
        for h in range(2):
            c = pltpu.make_async_copy(
                win_ref.at[:, h, :, pl.ds(t * tile, tile)],
                win_v.at[t, :, :, pl.ds(h * tile, tile)],
                w_sem.at[2 * t + h],
            )
            c.start()
            weights.append(c)
    last = pltpu.make_async_copy(wout_ref, wout_v, w_sem.at[2 * tiles])
    last.start()

    step = min(512, wide)
    for n in range(0, wide, step):
        rows_v[:, pl.ds(n, step)] = jnp.dot(
            pick[...], xs[:, pl.ds(n, step)], preferred_element_type=jnp.float32
        ).astype(jnp.bfloat16)
    wsi = wsi_v[...].reshape(wide, 2 * hp)
    for m in range(0, 8 * rows, 2 * rows):
        both = jnp.dot(xs[pl.ds(m, 2 * rows), :], wsi, preferred_element_type=jnp.float32)
        hs_v[pl.ds(m, 2 * rows), :] = (silu(both[:, :hp]) * both[:, hp:]).astype(jnp.bfloat16)

    for t in range(tiles):
        weights[2 * t].wait()
        weights[2 * t + 1].wait()
        both = jnp.dot(
            rows_v[...], win_v[t].reshape(wide, 2 * tile), preferred_element_type=jnp.float32
        )
        hid_v[:, pl.ds(t * tile, tile)] = (silu(both[:, :tile]) * both[:, tile:]).astype(
            jnp.bfloat16
        )
    last.wait()
    for n in range(0, wide, step):
        y_v[:, pl.ds(n, step)] = jnp.dot(
            hid_v[...], wout_v[:, pl.ds(n, step)], preferred_element_type=jnp.float32
        ).astype(jnp.bfloat16)
    step = min(256, half)
    depth = wso_v.shape[1]
    outs = []
    for n in range(0, wide, step):
        routed = jnp.dot(place[...], y_v[:, pl.ds(n, step)], preferred_element_type=jnp.float32)
        if step % depth == 0:
            down = wso_v[pl.ds(n // depth, step // depth)].reshape(step, hp)
        else:
            down = wso_v[...].reshape(wide, hp)[n : n + step]
        shared = lax.dot_general(
            hs_v[...], down, (((1,), (1,)), ((), ())), preferred_element_type=jnp.float32
        )
        total = routed * gate_col[:, 0:1] + shared
        keep_v[:, pl.ds(n, step)] = total[:part]
        send_v[:, pl.ds(n, step)] = total[part:].astype(jnp.bfloat16)
        if (n + step) % half == 0:
            k = len(outs)
            cols = pl.ds(n + step - half, half)
            for c in (
                pltpu.make_async_copy(send_v.at[:, cols], send_ref.at[:, cols], o_sem.at[k]),
                pltpu.make_async_copy(keep_v.at[:, cols], keep_ref.at[:, cols], o_sem.at[k + 1]),
            ):
                c.start()
                outs.append(c)
    for c in outs:
        c.wait()


def chunk_work(idx, gates, three, pieces, win, wout, cap, after):
    rows = pieces[0].shape[0] // 2
    wide = pieces[0].shape[1] * 2
    hidden = wout.shape[0]
    tile = LANES if hidden % LANES == 0 else hidden
    tiles = hidden // tile
    slots = 8 * cap
    depth, hp = three.shape[2:]
    bf, f32 = jnp.bfloat16, jnp.float32
    vmem = pl.BlockSpec(memory_space=pltpu.VMEM)
    hbm = pl.BlockSpec(memory_space=pl.ANY)
    flops = 2 * (
        2 * slots * 8 * rows * wide + slots * hidden * wide * 3 + 8 * rows * wide * 3 * hp
    )
    return pl.pallas_call(
        functools.partial(chunk_kernel, cap, len(after)),
        out_shape=(
            jax.ShapeDtypeStruct((4 * rows, wide), f32),
            jax.ShapeDtypeStruct((4 * rows, wide), bf),
        ),
        in_specs=[pl.BlockSpec(memory_space=pltpu.SMEM), vmem] + [hbm] * (11 + len(after)),
        out_specs=(hbm, hbm),
        scratch_shapes=[
            pltpu.VMEM((8 * rows, wide), bf),
            pltpu.VMEM((wide // depth, depth, 2 * hp), bf),
            pltpu.VMEM((wide // depth, depth, hp), bf),
            pltpu.VMEM((tiles,) + (win.shape[0], win.shape[2], 2 * tile), bf),
            pltpu.VMEM((hidden, wide), bf),
            pltpu.VMEM((slots, 8 * rows), bf),
            pltpu.VMEM((8 * rows, slots), bf),
            pltpu.VMEM((8 * rows, LANES), f32),
            pltpu.VMEM((slots, wide), bf),
            pltpu.VMEM((slots, hidden), bf),
            pltpu.VMEM((8 * rows, hp), bf),
            pltpu.VMEM((slots, wide), bf),
            pltpu.VMEM((4 * rows, wide), f32),
            pltpu.VMEM((4 * rows, wide), bf),
            pltpu.SemaphoreType.DMA((15,)),
            pltpu.SemaphoreType.DMA((2 * tiles + 1,)),
            pltpu.SemaphoreType.DMA((4,)),
        ],
        compiler_params=pltpu.CompilerParams(vmem_limit_bytes=56 * 1024 * 1024),
        cost_estimate=pl.CostEstimate(
            flops=flops, bytes_accessed=40 * 1024 * 1024, transcendentals=slots * hidden
        ),
    )(idx, gates, three, *pieces, win, wout, *after)


def spread(block):
    half = block.shape[1] // 2
    h0, h1 = block[:, :half], block[:, half:]
    l0 = jnp.concatenate([h0, swap(h0, 2)], axis=0)
    l1 = jnp.concatenate([h1, swap(h1, 4)], axis=0)
    r0 = swap(l0, 4)
    r1 = swap(l1, 2)
    mine = (l0, r0, l1, r1)
    return mine + tuple(swap(p, 1) for p in mine)


def add_core(keep, send):
    bf, f32 = jnp.bfloat16, jnp.float32
    rows, half = keep.shape[0] // 4, keep.shape[1] // 2
    both = keep + swap(send, 1).astype(f32)
    low, high = both[:, :half], both[:, half:]
    near = (low[: 2 * rows], jnp.concatenate([high[:rows], high[2 * rows : 3 * rows]], axis=0))
    far = (low[2 * rows :], jnp.concatenate([high[rows : 2 * rows], high[3 * rows :]], axis=0))
    return near, tuple(v.astype(bf) for v in far)


def add_first(near, far):
    bf, f32 = jnp.bfloat16, jnp.float32
    rows = near[0].shape[0] // 2
    low = near[0] + swap(far[0], 4).astype(f32)
    high = near[1] + swap(far[1], 2).astype(f32)
    return (low[:rows], high[:rows]), (low[rows:].astype(bf), high[rows:].astype(bf))


def add_second(near, far):
    f32 = jnp.float32
    low = near[0] + swap(far[0], 2).astype(f32)
    high = near[1] + swap(far[1], 4).astype(f32)
    return jnp.concatenate([low, high], axis=1)


def attention(context, out_proj, before):
    n = lax.axis_size("expert")
    odd = lax.axis_index("expert") % 2 == 1
    half = out_proj.shape[0] // 2

    def halves(lo, hi):
        return jnp.where(odd, hi, lo), jnp.where(odd, lo, hi)

    mine, other = halves(out_proj[:half], out_proj[half:])
    got = swap(other, 1)
    pair = jnp.concatenate(halves(mine, got), axis=1)
    groups = [list(range(c, n, 2)) for c in range(2)]
    weights = lax.all_gather(pair, "expert", axis=1, tiled=True, axis_index_groups=groups)
    mine, other = halves(context[:, :half], context[:, half:])
    rows = jnp.concatenate([mine, swap(other, 1)], axis=0)
    rows, before = lax.optimization_barrier((rows, before))
    parts = jnp.dot(rows, weights, preferred_element_type=jnp.float32)
    here = context.shape[0]
    return parts[:here] + swap(parts[here:], 1), before


def whole_rows(
    hidden_state,
    context,
    out_proj,
    norm_gain,
    router_weight,
    expert_in,
    expert_out,
    shared_in,
    shared_out,
    route_ids,
):
    bf, f32 = jnp.bfloat16, jnp.float32
    n = lax.axis_size("expert")
    layers = n // LAYER
    me = lax.axis_index("expert")
    rows, top = route_ids.shape
    experts = router_weight.shape[1]
    width = out_proj.shape[0]
    cap = capacity_of(rows, top, experts)

    group = 16
    win = expert_in[0].reshape(width // group, group, 2, -1).transpose(0, 2, 1, 3)
    wout = expert_out[0]

    own = shared_in.shape[2] // n
    depth = shared_in.shape[0]
    hp = -(-own // LANES) * LANES
    three = jnp.concatenate([shared_in.transpose(1, 0, 2), shared_out.T[None]], axis=0)
    three = three.reshape(3, depth, n, own)
    three = jnp.pad(three, ((0, 0), (0, 0), (0, 0), (0, hp - own))).transpose(2, 0, 1, 3)
    three = lax.all_to_all(three, "expert", split_axis=0, concat_axis=0, tiled=True)

    attn, win = attention(context, out_proj, win)
    mixed = hidden_state.astype(f32) + attn
    inverse = lax.rsqrt(jnp.mean(mixed * mixed, axis=1, keepdims=True) + 1e-06)
    normed32 = mixed * inverse * norm_gain.astype(f32)
    normed = normed32.astype(bf)
    logits = jnp.dot(normed32, router_weight, precision=lax.Precision.HIGHEST)
    named = jnp.any(
        route_ids[:, :, None] == jnp.arange(experts, dtype=jnp.int32)[None, None, :], axis=1
    )
    highest = jnp.max(jnp.where(named, logits, -jnp.inf), axis=1, keepdims=True)
    raised = jnp.where(named, jnp.exp(logits - highest), 0.0)
    gates = raised / jnp.sum(raised, axis=1, keepdims=True)
    own_gates = lax.all_to_all(gates.T, "expert", split_axis=0, concat_axis=0, tiled=True)

    low = me % LAYER
    order = jnp.array([2 * (p % 4) + p // 4 for p in range(8)], jnp.int32)
    far_first = sorted(range(layers), key=lambda k: (k != 0, -min(k, layers - k)))
    blocks = {k: turn(normed, k) if k else normed for k in far_first}
    pieces = {k: spread(blocks[k]) for k in far_first}
    total = mixed
    ready, cored, once = [], [], []
    for i, k in enumerate(far_first):
        idx = (me // LAYER - k) % layers * LAYER + jnp.bitwise_xor(low, order)
        after = [ready[-1][1]] if ready else []
        if i >= 2:
            cored.append(add_core(*ready[i - 2]))
            after += cored[i - 2][1]
        if i >= 3:
            once.append(add_first(*cored[i - 3]))
            after += once[i - 3][1]
        ready.append(
            chunk_work(
                idx.astype(jnp.int32), own_gates, three, pieces[k], win, wout, cap, after
            )
        )
    for i, k in enumerate(far_first):
        if i >= len(cored):
            cored.append(add_core(*ready[i]))
        if i >= len(once):
            once.append(add_first(*cored[i]))
        part = add_second(*once[i])
        if k:
            part = turn(part.astype(bf), layers - k).astype(f32)
        total = total + part
    return total


def solution(mesh):
    n, mp = mesh.shape["expert"], mesh.shape["mp"]
    per_device = whole_rows if mp == 1 and n % LAYER == 0 else general
    return jax.shard_map(
        per_device,
        mesh=mesh,
        in_specs=(
            P("expert", "mp"),
            P("expert", "mp"),
            P("mp", "expert"),
            P("mp"),
            P("mp", None),
            P("expert", None, None, "mp"),
            P("expert", "mp", None),
            P("expert", None, "mp"),
            P("mp", "expert"),
            P("expert", None),
        ),
        out_specs=P("expert", "mp"),
        check_vma=False,
    )
```

```python
import functools

import jax
import jax.numpy as jnp
from jax import lax
from jax.experimental import pallas as pl
from jax.experimental.pallas import tpu as pltpu
from jax.sharding import PartitionSpec as P

LANES = 128
GROUP = 2
LAYER = 8


def capacity_of(rows, top, experts):
    return max(2, min(rows, rows * top // experts * 5 // 3))


def general(
    hidden_state,
    context,
    out_proj,
    norm_gain,
    router_weight,
    expert_in,
    expert_out,
    shared_in,
    shared_out,
    route_ids,
):
    rows_here, top = route_ids.shape
    experts = router_weight.shape[1]
    width = out_proj.shape[0] * lax.axis_size("mp")
    capacity = capacity_of(rows_here, top, experts)
    partial_attn = jnp.dot(
        context,
        lax.all_gather(out_proj, "expert", axis=1, tiled=True),
        preferred_element_type=jnp.float32,
    )
    attn = lax.psum_scatter(partial_attn, "mp", scatter_dimension=1, tiled=True)
    mixed = hidden_state.astype(jnp.float32) + attn
    gain = norm_gain.astype(jnp.float32)
    squares = lax.psum(jnp.sum(mixed * mixed, axis=1), "mp")
    inverse = lax.rsqrt(squares / width + 1e-06)[:, None]
    normed32 = mixed * inverse * gain
    logits = lax.psum(jnp.dot(normed32, router_weight, precision=lax.Precision.HIGHEST), "mp")
    normed = normed32.astype(jnp.bfloat16)
    gates = jax.nn.softmax(jnp.take_along_axis(logits, route_ids, axis=1), axis=1)
    full_rows = lax.all_gather(normed, "mp", axis=1, tiled=True)
    shared_width = shared_in.shape[2]
    piece = lax.all_gather(shared_in, "expert", axis=0, tiled=True)
    shared_both = jnp.dot(
        full_rows,
        piece.reshape(piece.shape[0], 2 * shared_width),
        preferred_element_type=jnp.float32,
    )
    shared_both = shared_both.reshape(rows_here, 2, shared_width)
    shared_hidden = (jax.nn.silu(shared_both[:, 0]) * shared_both[:, 1]).astype(jnp.bfloat16)
    shared_part = jnp.dot(
        shared_hidden,
        lax.all_gather(shared_out, "expert", axis=1, tiled=True),
        preferred_element_type=jnp.float32,
    )
    flat = route_ids.reshape(-1)
    onehot = (flat[:, None] == jnp.arange(experts, dtype=jnp.int32)[None, :]).astype(jnp.int32)
    position = jnp.sum(onehot * jnp.cumsum(onehot, axis=0), axis=1) - 1
    slot_of = flat * capacity + position
    source = (
        jnp.zeros((experts * capacity,), jnp.int32)
        .at[slot_of]
        .set(jnp.arange(flat.shape[0], dtype=jnp.int32) // top)
    )
    filled = jnp.zeros((experts * capacity,), jnp.bool_).at[slot_of].set(True)
    outgoing = jnp.where(filled[:, None], normed[source], jnp.zeros((), jnp.bfloat16)).reshape(
        experts, capacity, normed.shape[1]
    )
    quarter = expert_in.shape[3]
    weights_in = expert_in[0].reshape(width, 2 * quarter)
    incoming = lax.all_to_all(outgoing, "expert", split_axis=0, concat_axis=0, tiled=True)
    sources = incoming.shape[0]
    items = incoming.shape[1]
    gathered = lax.all_gather(incoming, "mp", axis=2, tiled=True).reshape(sources * items, width)
    inner = jnp.dot(gathered, weights_in, preferred_element_type=jnp.float32).reshape(
        -1, 2, quarter
    )
    hidden = (jax.nn.silu(inner[:, 0]) * inner[:, 1]).astype(jnp.bfloat16)
    partial_out = jnp.dot(hidden, expert_out[0], preferred_element_type=jnp.float32).astype(
        jnp.bfloat16
    )
    partial_out = partial_out.reshape(sources, items, width)
    result = lax.all_to_all(partial_out, "expert", split_axis=0, concat_axis=0, tiled=True)
    picked = result.reshape(experts * capacity, result.shape[2])[slot_of]
    slot_total = lax.psum_scatter(
        lax.optimization_barrier(picked).astype(jnp.float32).astype(jnp.bfloat16),
        "mp",
        scatter_dimension=1,
        tiled=True,
    )
    expert_sum = lax.optimization_barrier(slot_total).astype(jnp.float32)
    expert_sum = expert_sum.reshape(rows_here, top, expert_sum.shape[1])
    routed = jnp.sum(gates[:, :, None] * expert_sum, axis=1)
    shared = lax.psum_scatter(shared_part, "mp", scatter_dimension=1, tiled=True)
    return mixed + routed + shared


def swap(x, bit):
    n = lax.axis_size("expert")
    return lax.ppermute(x, "expert", [(i, i ^ bit) for i in range(n)])


def turn(x, layers):
    n = lax.axis_size("expert")
    return lax.ppermute(x, "expert", [(i, (i + LAYER * layers) % n) for i in range(n)])


def silu(v):
    return v / (1.0 + jnp.exp(-v))


def spread(block):
    half = block.shape[1] // 2
    h0, h1 = block[:, :half], block[:, half:]
    l0 = jnp.concatenate([h0, swap(h0, 2)], axis=0)
    l1 = jnp.concatenate([h1, swap(h1, 4)], axis=0)
    return l0, swap(l0, 4), l1, swap(l1, 2)


class Copies:
    def __init__(self, sems):
        self.sems, self.all = sems, []

    def start(self, src, dst):
        c = pltpu.make_async_copy(src, dst, self.sems.at[len(self.all)])
        c.start()
        self.all.append(c)

    def wait(self):
        for c in self.all:
            c.wait()


def fetch_pieces(copies, pieces, rows, count, place):
    l0, r0, l1, r1 = pieces
    for h, (near, far, first, second) in enumerate(((l0, r0, 1, 2), (l1, r1, 2, 1))):
        for piece, base in ((near, 0), (far, second)):
            for a, q in enumerate((base, base + first)):
                for i in range(count):
                    copies.start(piece.at[pl.ds((a * count + i) * rows, rows)], place(i, q, h))


def slots_of(gate_ref, idx_ref, expert, blocks, cap, rows):
    g = jnp.concatenate([gate_ref[pl.ds(idx_ref[expert, p], 1), :] for p in blocks], axis=0)
    chosen = g > 0.0
    r_io = lax.broadcasted_iota(jnp.int32, (rows, rows), 0)
    c_io = lax.broadcasted_iota(jnp.int32, (rows, rows), 1)
    upto = jnp.where(r_io <= c_io, 1.0, 0.0).astype(jnp.bfloat16)
    count = jnp.dot(
        jnp.where(chosen, 1.0, 0.0).astype(jnp.bfloat16), upto, preferred_element_type=jnp.float32
    ).astype(jnp.int32)
    first = lax.broadcasted_iota(jnp.int32, (len(blocks), rows), 0) * cap
    return g, jnp.where(chosen, first + count - 1, -1)


def steps(total, most):
    step = min(most, total)
    return [(n, step) for n in range(0, total, step)]


def attention_kernel(count, groups, idx_ref, mine_ref, other_ref, *rest):
    pieces, (keep_ref, send_ref, w_v, sems) = rest[: 4 * groups], rest[4 * groups :]
    rows = pieces[0].shape[0] // (2 * count)
    half = w_v.shape[1] // 2
    copies = Copies(sems)
    for g in range(groups):

        def place(i, q, h, g=g):
            chip = idx_ref[(g * count + i) * 4 + q]
            return w_v.at[pl.ds(pl.multiple_of(chip * rows, rows), rows), pl.ds(h * half, half)]

        fetch_pieces(copies, pieces[4 * g : 4 * g + 4], rows, count, place)
    copies.wait()
    both = jnp.concatenate([mine_ref[...], other_ref[...]], axis=0)
    here = mine_ref.shape[0]
    for n, step in steps(w_v.shape[0], 512):
        part = lax.dot_general(
            both,
            w_v[pl.ds(n, step), :],
            (((1,), (1,)), ((), ())),
            preferred_element_type=jnp.float32,
        )
        keep_ref[:, pl.ds(n, step)] = part[:here]
        send_ref[:, pl.ds(n, step)] = part[here:]


def pick_kernel(cap, count, unused, idx_ref, gate_ref, *rest):
    pieces, (mine_ref, other_ref, xs, pick, out_v, x_sem, o_sem) = rest[:4], rest[4 + unused :]
    rows = pieces[0].shape[0] // (2 * count)
    wide, half = xs.shape[1], xs.shape[1] // 2
    copies = Copies(x_sem)
    fetch_pieces(
        copies,
        pieces,
        rows,
        count,
        lambda i, q, h: xs.at[pl.ds((4 * i + q) * rows, rows), pl.ds(h * half, half)],
    )
    slots = 4 * cap
    numbers = lax.broadcasted_iota(jnp.int32, (slots, rows), 0)
    for i in range(count):
        for e in range(2):
            _, slot = slots_of(gate_ref, idx_ref, e, range(4 * i, 4 * i + 4), cap, rows)
            for q in range(4):
                pick[i, pl.ds(e * slots, slots), pl.ds(q * rows, rows)] = jnp.where(
                    numbers == slot[q : q + 1, :], 1.0, 0.0
                ).astype(jnp.bfloat16)
    copies.wait()
    outs = Copies(o_sem)
    for i in range(count):
        for n, step in steps(wide, 512):
            out_v[i, :, pl.ds(n, step)] = jnp.dot(
                pick[i],
                xs[pl.ds(4 * i * rows, 4 * rows), pl.ds(n, step)],
                preferred_element_type=jnp.float32,
            ).astype(jnp.bfloat16)
        outs.start(out_v.at[i, pl.ds(slots, slots)], other_ref.at[pl.ds(i * slots, slots)])
        outs.start(out_v.at[i, pl.ds(0, slots)], mine_ref.at[pl.ds(i * slots, slots)])
    outs.wait()


def shared_kernel(count, unused, three_ref, theirs_ref, *rest):
    pieces, (hs_ref, xs, w_v, x_sem) = rest[:4], rest[4 + unused :]
    rows = pieces[0].shape[0] // (2 * count)
    wide, half = xs.shape[1], xs.shape[1] // 2
    hp = three_ref.shape[3]
    copies = Copies(x_sem)
    for e, ref in enumerate((three_ref, theirs_ref)):
        for h in range(2):
            copies.start(ref.at[:, h], w_v.at[:, :, pl.ds((2 * h + e) * hp, hp)])
    fetch_pieces(
        copies,
        pieces,
        rows,
        count,
        lambda i, q, h: xs.at[pl.ds((4 * i + q) * rows, rows), pl.ds(h * half, half)],
    )
    copies.wait()
    w = w_v[...].reshape(wide, 4 * hp)
    for m, step in steps(4 * count * rows, 2 * rows):
        both = jnp.dot(xs[pl.ds(m, step), :], w, preferred_element_type=jnp.float32)
        hs_ref[pl.ds(m, step), :] = (silu(both[:, : 2 * hp]) * both[:, 2 * hp :]).astype(
            jnp.bfloat16
        )


def expert_kernel(unused, mine_ref, other_ref, win_ref, wout_ref, *rest):
    mine_out, other_out, win_v, wout_v, hid_v, y_v, w_sem, o_sem = rest[unused:]
    slots, wide = mine_ref.shape
    tiles, tile = win_v.shape[0], win_v.shape[3] // 2
    copies = Copies(w_sem)
    for t in range(tiles):
        for h in range(2):
            copies.start(
                win_ref.at[:, h, :, pl.ds(t * tile, tile)],
                win_v.at[t, :, :, pl.ds(h * tile, tile)],
            )
    copies.start(wout_ref, wout_v)
    x = jnp.concatenate([mine_ref[...], other_ref[...]], axis=0)
    for t in range(tiles):
        copies.all[2 * t].wait()
        copies.all[2 * t + 1].wait()
        both = jnp.dot(x, win_v[t].reshape(wide, 2 * tile), preferred_element_type=jnp.float32)
        hid_v[:, pl.ds(t * tile, tile)] = (silu(both[:, :tile]) * both[:, tile:]).astype(
            jnp.bfloat16
        )
    copies.all[2 * tiles].wait()
    for n, step in steps(wide, 512):
        y_v[:, pl.ds(n, step)] = jnp.dot(
            hid_v[...], wout_v[:, pl.ds(n, step)], preferred_element_type=jnp.float32
        ).astype(jnp.bfloat16)
    outs = Copies(o_sem)
    outs.start(y_v.at[pl.ds(slots, slots)], other_out)
    outs.start(y_v.at[pl.ds(0, slots)], mine_out)
    outs.wait()


def place_kernel(cap, count, unused, idx_ref, gate_ref, mine_ref, other_ref, hs_ref, *rest):
    three_ref, theirs_ref = rest[:2]
    near_low, far_low, near_high, far_high, w_v, place, gate_col, w_sem = rest[2 + unused :]
    rows = hs_ref.shape[0] // (4 * count)
    wide, half = mine_ref.shape[1], near_low.shape[1]
    hp = three_ref.shape[3]
    slots = 4 * cap
    copies = Copies(w_sem)
    for e, ref in enumerate((three_ref, theirs_ref)):
        copies.start(ref.at[:, 2], w_v.at[:, :, pl.ds(e * hp, hp)])
    r_io = lax.broadcasted_iota(jnp.int32, (rows, rows), 0)
    c_io = lax.broadcasted_iota(jnp.int32, (rows, rows), 1)
    eye = r_io == c_io
    numbers = lax.broadcasted_iota(jnp.int32, (rows, slots), 1)
    for i in range(count):
        for e in range(2):
            g, slot = slots_of(gate_ref, idx_ref, e, range(4 * i, 4 * i + 4), cap, rows)
            for q in range(4):
                at = pl.ds(q * rows, rows)
                col = jnp.sum(jnp.where(eye, slot[q : q + 1, :], 0), axis=1, keepdims=True)
                place[i, e, at, :] = jnp.where(numbers == col, 1.0, 0.0).astype(jnp.bfloat16)
                gcol = jnp.sum(jnp.where(eye, g[q : q + 1, :], 0.0), axis=1, keepdims=True)
                gate_col[i, e, at, :] = jnp.broadcast_to(gcol, (rows, LANES))
    copies.wait()
    depth = w_v.shape[1]
    f32 = jnp.float32
    for i in range(count):
        span = pl.ds(i * slots, slots)
        for n, step in steps(wide, min(256, half)):
            cols = pl.ds(n, step)
            if step % depth == 0:
                down = w_v[pl.ds(n // depth, step // depth)].reshape(step, 2 * hp)
            else:
                down = w_v[...].reshape(wide, 2 * hp)[n : n + step]
            total = lax.dot_general(
                hs_ref[pl.ds(4 * i * rows, 4 * rows), :],
                down,
                (((1,), (1,)), ((), ())),
                preferred_element_type=f32,
            )
            for e, ref in enumerate((mine_ref, other_ref)):
                y = jnp.dot(place[i, e], ref[span, cols], preferred_element_type=f32)
                total = total + gate_col[i, e][:, 0:1] * y
            if n < half:
                near, far, order, at = near_low, far_low, (0, 1, 2, 3), pl.ds(n, step)
            else:
                near, far, order, at = near_high, far_high, (0, 2, 1, 3), pl.ds(n - half, step)
            for a in range(2):
                to = pl.ds((a * count + i) * rows, rows)
                q = order[a] * rows
                near[to, at] = total[q : q + rows]
                q = order[2 + a] * rows
                far[to, at] = total[q : q + rows].astype(far.dtype)


def call(body, out_shape, in_specs, args, scratch, flops, moved, after=(), outs_in_vmem=True):
    vmem = pl.BlockSpec(memory_space=pltpu.VMEM)
    hbm = pl.BlockSpec(memory_space=pl.ANY)
    kinds = {"s": pl.BlockSpec(memory_space=pltpu.SMEM), "v": vmem, "h": hbm}
    return pl.pallas_call(
        body,
        out_shape=out_shape,
        in_specs=[kinds[k] for k in in_specs] + [hbm] * len(after),
        out_specs=tuple([vmem if outs_in_vmem else hbm] * len(out_shape)),
        scratch_shapes=scratch,
        compiler_params=pltpu.CompilerParams(vmem_limit_bytes=48 * 1024 * 1024),
        cost_estimate=pl.CostEstimate(flops=flops, bytes_accessed=moved, transcendentals=0),
    )(*args, *after)


def attention(context, out_proj, groups, before):
    bf, f32 = jnp.bfloat16, jnp.float32
    me = lax.axis_index("expert")
    layers = lax.axis_size("expert") // LAYER
    odd = me % 2 == 1
    wide = context.shape[1]
    half = wide // 2

    def halves(lo, hi):
        return jnp.where(odd, hi, lo), jnp.where(odd, lo, hi)

    turned = out_proj.T
    mine, other = halves(turned[:, :half], turned[:, half:])
    pair = jnp.concatenate(halves(mine, swap(other, 1)), axis=0)
    mine, other = halves(context[:, :half], context[:, half:])
    got = swap(other, 1)
    blocks = {k: turn(pair, k) if k else pair for g in groups for k in g}
    pieces, chips = [], []
    for g in groups:
        pieces += spread(jnp.concatenate([blocks[k] for k in g], axis=0))
        for k in g:
            layer = (me // LAYER - k) % layers
            chips += [layer * (LAYER // 2) + jnp.bitwise_xor(me % LAYER // 2, q) for q in range(4)]
    mine, before = lax.optimization_barrier((mine, before))
    count, here = len(groups[0]), context.shape[0]
    keep, send = call(
        functools.partial(attention_kernel, count, len(groups)),
        [jax.ShapeDtypeStruct((here, wide), f32)] * 2,
        "svv" + "h" * len(pieces),
        (jnp.stack(chips).astype(jnp.int32), mine, got, *pieces),
        [
            pltpu.VMEM((out_proj.shape[1] * lax.axis_size("expert"), half), bf),
            pltpu.SemaphoreType.DMA((8 * count * len(groups),)),
        ],
        4 * here * wide * half,
        2 * wide * half,
    )
    return keep + swap(send, 1), before


def whole_rows(
    hidden_state,
    context,
    out_proj,
    norm_gain,
    router_weight,
    expert_in,
    expert_out,
    shared_in,
    shared_out,
    route_ids,
):
    bf, f32 = jnp.bfloat16, jnp.float32
    n = lax.axis_size("expert")
    layers = n // LAYER
    me = lax.axis_index("expert")
    odd = me % 2
    rows, top = route_ids.shape
    experts = router_weight.shape[1]
    wide = out_proj.shape[0]
    half = wide // 2
    cap = capacity_of(rows, top, experts)
    count = GROUP if layers % GROUP == 0 else 1
    near_first = sorted(range(layers), key=lambda k: (min(k, layers - k), k))
    groups = [near_first[i : i + count] for i in range(0, layers, count)]

    pack = 16
    win = expert_in[0].reshape(wide // pack, pack, 2, -1).transpose(0, 2, 1, 3)
    wout = expert_out[0]
    hidden = wout.shape[0]
    tile = LANES if hidden % LANES == 0 else hidden

    own = shared_in.shape[2] // n
    depth = shared_in.shape[0]
    hp = -(-own // LANES) * LANES
    three = jnp.concatenate([shared_in.transpose(1, 0, 2), shared_out.T[None]], axis=0)
    three = three.reshape(3, depth, n, own)
    three = jnp.pad(three, ((0, 0), (0, 0), (0, 0), (0, hp - own))).transpose(2, 0, 1, 3)
    three = lax.all_to_all(three, "expert", split_axis=0, concat_axis=0, tiled=True)

    attn, (win, three) = attention(context, out_proj, groups, (win, three))
    theirs = swap(three, 1)
    mixed = hidden_state.astype(f32) + attn
    inverse = lax.rsqrt(jnp.mean(mixed * mixed, axis=1, keepdims=True) + 1e-06)
    normed32 = mixed * inverse * norm_gain.astype(f32)
    normed = normed32.astype(bf)
    logits = jnp.dot(normed32, router_weight, precision=lax.Precision.HIGHEST)
    named = jnp.any(
        route_ids[:, :, None] == jnp.arange(experts, dtype=jnp.int32)[None, None, :], axis=1
    )
    highest = jnp.max(jnp.where(named, logits, -jnp.inf), axis=1, keepdims=True)
    raised = jnp.where(named, jnp.exp(logits - highest), 0.0)
    gates = raised / jnp.sum(raised, axis=1, keepdims=True)
    gates = jnp.repeat(gates.T.reshape(n // 2, 2, rows), 2, axis=0)
    gates = lax.all_to_all(gates, "expert", split_axis=0, concat_axis=0, tiled=True)
    gates = gates.reshape(2 * n, rows)

    blocks = {k: turn(normed, k) if k else normed for k in near_first}
    slots = 4 * cap * count
    span = 4 * count * rows
    sds = jax.ShapeDtypeStruct
    xs = pltpu.VMEM((span, wide), bf)
    x_copies = 8 * count
    total = mixed
    placed, once = [], []

    def add_first(near_low, far_low, near_high, far_high):
        keep = near_low.shape[0] // 2
        low = near_low + swap(far_low, 4).astype(f32)
        high = near_high + swap(far_high, 2).astype(f32)
        return low[:keep], low[keep:].astype(bf), high[:keep], high[keep:].astype(bf)

    for g in groups:
        pieces = spread(jnp.concatenate([blocks[k] for k in g], axis=0))
        source = [
            (me // LAYER - k) % layers * LAYER + jnp.bitwise_xor(me % LAYER, 2 * q)
            for k in g
            for q in range(4)
        ]
        source = jnp.stack(source).astype(jnp.int32)
        idx = jnp.stack([2 * source + odd, 2 * source + 1 - odd]).astype(jnp.int32)
        after = [placed[-1][1]] if placed else []
        picked, lent = call(
            functools.partial(pick_kernel, cap, count, len(after)),
            [sds((slots, wide), bf)] * 2,
            "svhhhh",
            (idx, gates, *pieces),
            [
                xs,
                pltpu.VMEM((count, 8 * cap, 4 * rows), bf),
                pltpu.VMEM((count, 8 * cap, wide), bf),
                pltpu.SemaphoreType.DMA((x_copies,)),
                pltpu.SemaphoreType.DMA((2 * count,)),
            ],
            4 * slots * 4 * rows * wide,
            4 * span * wide,
            after,
            False,
        )
        borrowed = swap(lent, 1)
        (hs,) = call(
            functools.partial(shared_kernel, count, 1),
            [sds((span, 2 * hp), bf)],
            "hhhhhh",
            (three, theirs, *pieces),
            [
                xs,
                pltpu.VMEM((n, depth, 4 * hp), bf),
                pltpu.SemaphoreType.DMA((x_copies + 4,)),
            ],
            8 * span * wide * hp,
            4 * span * wide,
            [lent],
        )
        done, back = call(
            functools.partial(expert_kernel, 1),
            [sds((slots, wide), bf)] * 2,
            "vvhh",
            (picked, borrowed, win, wout),
            [
                pltpu.VMEM((hidden // tile, wide // pack, pack, 2 * tile), bf),
                pltpu.VMEM((hidden, wide), bf),
                pltpu.VMEM((2 * slots, hidden), bf),
                pltpu.VMEM((2 * slots, wide), bf),
                pltpu.SemaphoreType.DMA((2 * (hidden // tile) + 1,)),
                pltpu.SemaphoreType.DMA((2,)),
            ],
            12 * slots * wide * hidden,
            6 * wide * hidden,
            [hs],
            False,
        )
        after = []
        if placed:
            once.append(add_first(*placed[-1]))
            after = [once[-1][1], once[-1][3]]
        placed.append(
            call(
                functools.partial(place_kernel, cap, count, len(after)),
                [sds((2 * count * rows, half), t) for t in (f32, bf, f32, bf)],
                "svvvvhh",
                (idx, gates, done, swap(back, 1), hs, three, theirs),
                [
                    pltpu.VMEM((n, depth, 2 * hp), bf),
                    pltpu.VMEM((count, 2, 4 * rows, 4 * cap), bf),
                    pltpu.VMEM((count, 2, 4 * rows, LANES), f32),
                    pltpu.SemaphoreType.DMA((2,)),
                ],
                4 * span * wide * (4 * cap + hp),
                8 * span * wide,
                after,
            )
        )
    once.append(add_first(*placed[-1]))
    for g, (low, far_low, high, far_high) in zip(groups, once):
        low = low + swap(far_low, 2).astype(f32)
        high = high + swap(far_high, 4).astype(f32)
        both = jnp.concatenate([low, high], axis=1)
        for i, k in enumerate(g):
            part = both[i * rows : (i + 1) * rows]
            if k:
                part = turn(part.astype(bf), layers - k).astype(f32)
            total = total + part
    return total


def solution(mesh):
    n, mp = mesh.shape["expert"], mesh.shape["mp"]
    per_device = whole_rows if mp == 1 and n % LAYER == 0 else general
    return jax.shard_map(
        per_device,
        mesh=mesh,
        in_specs=(
            P("expert", "mp"),
            P("expert", "mp"),
            P("mp", "expert"),
            P("mp"),
            P("mp", None),
            P("expert", None, None, "mp"),
            P("expert", "mp", None),
            P("expert", None, "mp"),
            P("mp", "expert"),
            P("expert", None),
        ),
        out_specs=P("expert", "mp"),
        check_vma=False,
    )
```

```python
import functools

import jax
import jax.numpy as jnp
from jax import lax
from jax.experimental import pallas as pl
from jax.experimental.pallas import tpu as pltpu
from jax.sharding import PartitionSpec as P

LANES = 128
LAYER = 8


def capacity_of(rows, top, experts):
    return max(2, min(rows, rows * top // experts * 5 // 3))


def general(
    hidden_state,
    context,
    out_proj,
    norm_gain,
    router_weight,
    expert_in,
    expert_out,
    shared_in,
    shared_out,
    route_ids,
):
    rows_here, top = route_ids.shape
    experts = router_weight.shape[1]
    width = out_proj.shape[0] * lax.axis_size("mp")
    capacity = capacity_of(rows_here, top, experts)
    partial_attn = jnp.dot(
        context,
        lax.all_gather(out_proj, "expert", axis=1, tiled=True),
        preferred_element_type=jnp.float32,
    )
    attn = lax.psum_scatter(partial_attn, "mp", scatter_dimension=1, tiled=True)
    mixed = hidden_state.astype(jnp.float32) + attn
    gain = norm_gain.astype(jnp.float32)
    squares = lax.psum(jnp.sum(mixed * mixed, axis=1), "mp")
    inverse = lax.rsqrt(squares / width + 1e-06)[:, None]
    normed32 = mixed * inverse * gain
    logits = lax.psum(jnp.dot(normed32, router_weight, precision=lax.Precision.HIGHEST), "mp")
    normed = normed32.astype(jnp.bfloat16)
    gates = jax.nn.softmax(jnp.take_along_axis(logits, route_ids, axis=1), axis=1)
    full_rows = lax.all_gather(normed, "mp", axis=1, tiled=True)
    shared_width = shared_in.shape[2]
    piece = lax.all_gather(shared_in, "expert", axis=0, tiled=True)
    shared_both = jnp.dot(
        full_rows,
        piece.reshape(piece.shape[0], 2 * shared_width),
        preferred_element_type=jnp.float32,
    )
    shared_both = shared_both.reshape(rows_here, 2, shared_width)
    shared_hidden = (jax.nn.silu(shared_both[:, 0]) * shared_both[:, 1]).astype(jnp.bfloat16)
    shared_part = jnp.dot(
        shared_hidden,
        lax.all_gather(shared_out, "expert", axis=1, tiled=True),
        preferred_element_type=jnp.float32,
    )
    flat = route_ids.reshape(-1)
    onehot = (flat[:, None] == jnp.arange(experts, dtype=jnp.int32)[None, :]).astype(jnp.int32)
    position = jnp.sum(onehot * jnp.cumsum(onehot, axis=0), axis=1) - 1
    slot_of = flat * capacity + position
    source = (
        jnp.zeros((experts * capacity,), jnp.int32)
        .at[slot_of]
        .set(jnp.arange(flat.shape[0], dtype=jnp.int32) // top)
    )
    filled = jnp.zeros((experts * capacity,), jnp.bool_).at[slot_of].set(True)
    outgoing = jnp.where(filled[:, None], normed[source], jnp.zeros((), jnp.bfloat16)).reshape(
        experts, capacity, normed.shape[1]
    )
    quarter = expert_in.shape[3]
    weights_in = expert_in[0].reshape(width, 2 * quarter)
    incoming = lax.all_to_all(outgoing, "expert", split_axis=0, concat_axis=0, tiled=True)
    sources = incoming.shape[0]
    items = incoming.shape[1]
    gathered = lax.all_gather(incoming, "mp", axis=2, tiled=True).reshape(sources * items, width)
    inner = jnp.dot(gathered, weights_in, preferred_element_type=jnp.float32).reshape(
        -1, 2, quarter
    )
    hidden = (jax.nn.silu(inner[:, 0]) * inner[:, 1]).astype(jnp.bfloat16)
    partial_out = jnp.dot(hidden, expert_out[0], preferred_element_type=jnp.float32).astype(
        jnp.bfloat16
    )
    partial_out = partial_out.reshape(sources, items, width)
    result = lax.all_to_all(partial_out, "expert", split_axis=0, concat_axis=0, tiled=True)
    picked = result.reshape(experts * capacity, result.shape[2])[slot_of]
    slot_total = lax.psum_scatter(
        lax.optimization_barrier(picked).astype(jnp.float32).astype(jnp.bfloat16),
        "mp",
        scatter_dimension=1,
        tiled=True,
    )
    expert_sum = lax.optimization_barrier(slot_total).astype(jnp.float32)
    expert_sum = expert_sum.reshape(rows_here, top, expert_sum.shape[1])
    routed = jnp.sum(gates[:, :, None] * expert_sum, axis=1)
    shared = lax.psum_scatter(shared_part, "mp", scatter_dimension=1, tiled=True)
    return mixed + routed + shared


def swap(x, bit):
    n = lax.axis_size("expert")
    return lax.ppermute(x, "expert", [(i, i ^ bit) for i in range(n)])


def turn(x, layers):
    n = lax.axis_size("expert")
    return lax.ppermute(x, "expert", [(i, (i + LAYER * layers) % n) for i in range(n)])


def silu(v):
    return v / (1.0 + jnp.exp(-v))


def spread_first(block):
    half = block.shape[1] // 2
    h0, h1 = block[:, :half], block[:, half:]
    return jnp.concatenate([h0, swap(h0, 2)], axis=0), jnp.concatenate([h1, swap(h1, 4)], axis=0)


def spread_second(l0, l1):
    return l0, swap(l0, 4), l1, swap(l1, 2)


def tie(x, *others):
    return lax.optimization_barrier((x, *others))[0]


class Copies:
    def __init__(self, sems):
        self.sems, self.all = sems, []

    def start(self, src, dst):
        c = pltpu.make_async_copy(src, dst, self.sems.at[len(self.all)])
        c.start()
        self.all.append(c)

    def wait(self):
        for c in self.all:
            c.wait()


def fetch_pieces(copies, pieces, rows, place):
    for i in range(len(pieces) // 4):
        l0, r0, l1, r1 = pieces[4 * i : 4 * i + 4]
        for h, (near, far, first, second) in enumerate(((l0, r0, 1, 2), (l1, r1, 2, 1))):
            for piece, base in ((near, 0), (far, second)):
                for a, q in enumerate((base, base + first)):
                    copies.start(piece.at[pl.ds(a * rows, rows)], place(i, q, h))


def slots_of(gate_ref, idx_ref, expert, blocks, cap, rows):
    g = jnp.concatenate([gate_ref[pl.ds(idx_ref[expert, p], 1), :] for p in blocks], axis=0)
    chosen = g > 0.0
    r_io = lax.broadcasted_iota(jnp.int32, (rows, rows), 0)
    c_io = lax.broadcasted_iota(jnp.int32, (rows, rows), 1)
    upto = jnp.where(r_io <= c_io, 1.0, 0.0).astype(jnp.bfloat16)
    count = jnp.dot(
        jnp.where(chosen, 1.0, 0.0).astype(jnp.bfloat16), upto, preferred_element_type=jnp.float32
    ).astype(jnp.int32)
    first = lax.broadcasted_iota(jnp.int32, (len(blocks), rows), 0) * cap
    return g, jnp.where(chosen, first + count - 1, -1)


def steps(total, most):
    step = min(most, total)
    return [(n, step) for n in range(0, total, step)]


def attention_kernel(groups, rows, idx_ref, mine_ref, other_ref, *rest):
    pieces, (keep_ref, send_ref, w_v, sems) = rest[: 4 * groups], rest[4 * groups :]
    half = w_v.shape[1] // 2
    count = pieces[0].shape[0] // (2 * rows)
    copies = Copies(sems)
    for g in range(groups):
        l0, r0, l1, r1 = pieces[4 * g : 4 * g + 4]
        for h, (near, far, first, second) in enumerate(((l0, r0, 1, 2), (l1, r1, 2, 1))):
            for piece, base in ((near, 0), (far, second)):
                for a, q in enumerate((base, base + first)):
                    for i in range(count):
                        chip = idx_ref[(g * count + i) * 4 + q]
                        to = pl.ds(pl.multiple_of(chip * rows, rows), rows)
                        copies.start(
                            piece.at[pl.ds((a * count + i) * rows, rows)],
                            w_v.at[to, pl.ds(h * half, half)],
                        )
    copies.wait()
    both = jnp.concatenate([mine_ref[...], other_ref[...]], axis=0)
    here = mine_ref.shape[0]
    for n, step in steps(w_v.shape[0], 512):
        part = lax.dot_general(
            both,
            w_v[pl.ds(n, step), :],
            (((1,), (1,)), ((), ())),
            preferred_element_type=jnp.float32,
        )
        keep_ref[:, pl.ds(n, step)] = part[:here]
        send_ref[:, pl.ds(n, step)] = part[here:]


def pick_kernel(cap, count, unused, idx_ref, gate_ref, *rest):
    pieces = rest[: 4 * count]
    mine_ref, other_ref, xs, pick, out_v, x_sem, o_sem = rest[4 * count + unused :]
    rows = pieces[0].shape[0] // 2
    wide, half = xs.shape[1], xs.shape[1] // 2
    copies = Copies(x_sem)
    fetch_pieces(
        copies,
        pieces,
        rows,
        lambda i, q, h: xs.at[pl.ds((4 * i + q) * rows, rows), pl.ds(h * half, half)],
    )
    slots = 4 * cap
    numbers = lax.broadcasted_iota(jnp.int32, (slots, rows), 0)
    for i in range(count):
        for e in range(2):
            _, slot = slots_of(gate_ref, idx_ref, e, range(4 * i, 4 * i + 4), cap, rows)
            for q in range(4):
                pick[i, pl.ds(e * slots, slots), pl.ds(q * rows, rows)] = jnp.where(
                    numbers == slot[q : q + 1, :], 1.0, 0.0
                ).astype(jnp.bfloat16)
    copies.wait()
    outs = Copies(o_sem)
    for i in range(count):
        for n, step in steps(wide, 512):
            out_v[i, :, pl.ds(n, step)] = jnp.dot(
                pick[i],
                xs[pl.ds(4 * i * rows, 4 * rows), pl.ds(n, step)],
                preferred_element_type=jnp.float32,
            ).astype(jnp.bfloat16)
        outs.start(out_v.at[i, pl.ds(slots, slots)], other_ref.at[pl.ds(i * slots, slots)])
        outs.start(out_v.at[i, pl.ds(0, slots)], mine_ref.at[pl.ds(i * slots, slots)])
    outs.wait()


def shared_kernel(count, unused, three_ref, theirs_ref, *rest):
    pieces, (hs_ref, xs, w_v, x_sem) = rest[: 4 * count], rest[4 * count + unused :]
    rows = pieces[0].shape[0] // 2
    wide, half = xs.shape[1], xs.shape[1] // 2
    hp = three_ref.shape[3]
    copies = Copies(x_sem)
    for e, ref in enumerate((three_ref, theirs_ref)):
        for h in range(2):
            copies.start(ref.at[:, h], w_v.at[:, :, pl.ds((2 * h + e) * hp, hp)])
    fetch_pieces(
        copies,
        pieces,
        rows,
        lambda i, q, h: xs.at[pl.ds((4 * i + q) * rows, rows), pl.ds(h * half, half)],
    )
    copies.wait()
    w = w_v[...].reshape(wide, 4 * hp)
    for m, step in steps(4 * count * rows, 2 * rows):
        both = jnp.dot(xs[pl.ds(m, step), :], w, preferred_element_type=jnp.float32)
        hs_ref[pl.ds(m, step), :] = (silu(both[:, : 2 * hp]) * both[:, 2 * hp :]).astype(
            jnp.bfloat16
        )


def expert_kernel(unused, mine_ref, other_ref, win_ref, wout_ref, *rest):
    mine_out, other_out, x_v, win_v, wout_v, hid_v, y_v, x_sem, w_sem, o_sem = rest[unused:]
    slots, wide = mine_ref.shape
    tiles, tile = win_v.shape[0], win_v.shape[3] // 2
    rows = Copies(x_sem)
    rows.start(mine_ref, x_v.at[pl.ds(0, slots)])
    rows.start(other_ref, x_v.at[pl.ds(slots, slots)])
    copies = Copies(w_sem)
    for t in range(tiles):
        for h in range(2):
            copies.start(
                win_ref.at[:, h, :, pl.ds(t * tile, tile)],
                win_v.at[t, :, :, pl.ds(h * tile, tile)],
            )
    copies.start(wout_ref, wout_v)
    rows.wait()
    here = 0
    for t in range(tiles):
        if t == here:
            here = min(2 * here + 1, tiles)
            for c in copies.all[2 * t : 2 * here]:
                c.wait()
        both = jnp.dot(
            x_v[...], win_v[t].reshape(wide, 2 * tile), preferred_element_type=jnp.float32
        )
        hid_v[:, pl.ds(t * tile, tile)] = (silu(both[:, :tile]) * both[:, tile:]).astype(
            jnp.bfloat16
        )
    copies.all[2 * tiles].wait()
    outs = Copies(o_sem)
    for n, step in steps(wide, 512):
        y_v[:, pl.ds(n, step)] = jnp.dot(
            hid_v[...], wout_v[:, pl.ds(n, step)], preferred_element_type=jnp.float32
        ).astype(jnp.bfloat16)
    outs.start(y_v.at[pl.ds(slots, slots)], other_out)
    outs.start(y_v.at[pl.ds(0, slots)], mine_out)
    outs.wait()


def place_kernel(cap, count, unused, idx_ref, gate_ref, mine_ref, other_ref, hs_ref, *rest):
    three_ref, theirs_ref = rest[:2]
    refs, rest = rest[2 + unused : 6 + unused], rest[6 + unused :]
    bufs, (w_v, place, gate_col, w_sem, o_sem) = rest[:4], rest[4:]
    near_low, far_low, near_high, far_high = bufs
    rows = hs_ref.shape[0] // (4 * count)
    wide, half = mine_ref.shape[1], near_low.shape[1]
    hp = three_ref.shape[3]
    slots = 4 * cap
    copies = Copies(w_sem)
    for e, ref in enumerate((three_ref, theirs_ref)):
        copies.start(ref.at[:, 2], w_v.at[:, :, pl.ds(e * hp, hp)])
    r_io = lax.broadcasted_iota(jnp.int32, (rows, rows), 0)
    c_io = lax.broadcasted_iota(jnp.int32, (rows, rows), 1)
    eye = r_io == c_io
    numbers = lax.broadcasted_iota(jnp.int32, (rows, slots), 1)
    for i in range(count):
        for e in range(2):
            g, slot = slots_of(gate_ref, idx_ref, e, range(4 * i, 4 * i + 4), cap, rows)
            for q in range(4):
                at = pl.ds(q * rows, rows)
                col = jnp.sum(jnp.where(eye, slot[q : q + 1, :], 0), axis=1, keepdims=True)
                place[i, e, at, :] = jnp.where(numbers == col, 1.0, 0.0).astype(jnp.bfloat16)
                gcol = jnp.sum(jnp.where(eye, g[q : q + 1, :], 0.0), axis=1, keepdims=True)
                gate_col[i, e, at, :] = jnp.broadcast_to(gcol, (rows, LANES))
    copies.wait()
    depth = w_v.shape[1]
    f32 = jnp.float32
    outs = Copies(o_sem)
    for n, step in steps(wide, min(256, half)):
        cols = pl.ds(n, step)
        if step % depth == 0:
            down = w_v[pl.ds(n // depth, step // depth)].reshape(step, 2 * hp)
        else:
            down = w_v[...].reshape(wide, 2 * hp)[n : n + step]
        for i in range(count):
            total = lax.dot_general(
                hs_ref[pl.ds(4 * i * rows, 4 * rows), :],
                down,
                (((1,), (1,)), ((), ())),
                preferred_element_type=f32,
            )
            for e, ref in enumerate((mine_ref, other_ref)):
                y = jnp.dot(
                    place[i, e], ref[pl.ds(i * slots, slots), cols], preferred_element_type=f32
                )
                total = total + gate_col[i, e][:, 0:1] * y
            if n < half:
                near, far, order, at = near_low, far_low, (0, 1, 2, 3), pl.ds(n, step)
            else:
                near, far, order, at = near_high, far_high, (0, 2, 1, 3), pl.ds(n - half, step)
            for a in range(2):
                to = pl.ds((a * count + i) * rows, rows)
                q = order[a] * rows
                near[to, at] = total[q : q + rows]
                q = order[2 + a] * rows
                far[to, at] = total[q : q + rows].astype(far.dtype)
        if (n + step) % half == 0:
            k = 2 * (n // half)
            outs.start(bufs[k + 1], refs[k + 1])
            outs.start(bufs[k], refs[k])
    outs.wait()


def call(body, out_shape, in_specs, args, scratch, flops, moved, after=(), outs_in_vmem=True):
    vmem = pl.BlockSpec(memory_space=pltpu.VMEM)
    hbm = pl.BlockSpec(memory_space=pl.ANY)
    kinds = {"s": pl.BlockSpec(memory_space=pltpu.SMEM), "v": vmem, "h": hbm}
    return pl.pallas_call(
        body,
        out_shape=out_shape,
        in_specs=[kinds[k] for k in in_specs] + [hbm] * len(after),
        out_specs=tuple([vmem if outs_in_vmem else hbm] * len(out_shape)),
        scratch_shapes=scratch,
        compiler_params=pltpu.CompilerParams(vmem_limit_bytes=48 * 1024 * 1024),
        cost_estimate=pl.CostEstimate(flops=flops, bytes_accessed=moved, transcendentals=0),
    )(*args, *after)


def attention(context, out_proj, order, before, exchange):
    bf, f32 = jnp.bfloat16, jnp.float32
    me = lax.axis_index("expert")
    layers = lax.axis_size("expert") // LAYER
    odd = me % 2 == 1
    wide = context.shape[1]
    half = wide // 2

    def halves(lo, hi):
        return jnp.where(odd, hi, lo), jnp.where(odd, lo, hi)

    turned = out_proj.T
    mine, other = halves(turned[:, :half], turned[:, half:])
    pair = jnp.concatenate(halves(mine, swap(other, 1)), axis=0)
    mine, other = halves(context[:, :half], context[:, half:])
    got = swap(other, 1)
    cut = pair.shape[0]
    twos = [order[i : i + 2] for i in range(0, layers, 2)]
    firsts = [
        spread_first(jnp.concatenate([turn(pair, k) if k else pair for k in two], axis=0))
        for two in twos
    ]
    exchange = lax.all_to_all(
        tie(exchange, *firsts[-1]), "expert", split_axis=0, concat_axis=0, tiled=True
    )
    pieces, chips = [], []
    for two, first in zip(twos, firsts):
        pieces += spread_second(*first)
        for k in two:
            layer = (me // LAYER - k) % layers
            chips += [layer * (LAYER // 2) + jnp.bitwise_xor(me % LAYER // 2, q) for q in range(4)]
    mine, before = lax.optimization_barrier((mine, before))
    here = context.shape[0]
    keep, send = call(
        functools.partial(attention_kernel, len(twos), cut),
        [jax.ShapeDtypeStruct((here, wide), f32)] * 2,
        "svv" + "h" * len(pieces),
        (jnp.stack(chips).astype(jnp.int32), mine, got, *pieces),
        [
            pltpu.VMEM((out_proj.shape[1] * lax.axis_size("expert"), half), bf),
            pltpu.SemaphoreType.DMA((8 * layers,)),
        ],
        4 * here * wide * half,
        2 * wide * half,
    )
    return keep + swap(send, 1), before, exchange


def whole_rows(
    hidden_state,
    context,
    out_proj,
    norm_gain,
    router_weight,
    expert_in,
    expert_out,
    shared_in,
    shared_out,
    route_ids,
):
    bf, f32 = jnp.bfloat16, jnp.float32
    n = lax.axis_size("expert")
    layers = n // LAYER
    me = lax.axis_index("expert")
    odd = me % 2
    rows, top = route_ids.shape
    experts = router_weight.shape[1]
    wide = out_proj.shape[0]
    half = wide // 2
    cap = capacity_of(rows, top, experts)
    order = list(range(layers))
    groups = [g for g in ([0], order[1:-1], order[-1:]) if g] if layers > 1 else [[0]]

    pack = 16
    win = expert_in[0].reshape(wide // pack, pack, 2, -1).transpose(0, 2, 1, 3)
    wout = expert_out[0]
    hidden = wout.shape[0]
    tile = LANES if hidden % LANES == 0 else hidden

    own = shared_in.shape[2] // n
    depth = shared_in.shape[0]
    hp = -(-own // LANES) * LANES
    three = jnp.concatenate([shared_in.transpose(1, 0, 2), shared_out.T[None]], axis=0)
    three = three.reshape(3, depth, n, own)
    three = jnp.pad(three, ((0, 0), (0, 0), (0, 0), (0, hp - own))).transpose(2, 0, 1, 3)

    attn, win, three = attention(context, out_proj, order, win, three)
    attn, three = lax.optimization_barrier((attn, three))
    theirs = swap(three, 1)
    mixed = hidden_state.astype(f32) + attn
    inverse = lax.rsqrt(jnp.mean(mixed * mixed, axis=1, keepdims=True) + 1e-06)
    normed32 = mixed * inverse * norm_gain.astype(f32)
    normed = normed32.astype(bf)
    logits = jnp.dot(normed32, router_weight, precision=lax.Precision.HIGHEST)
    named = jnp.any(
        route_ids[:, :, None] == jnp.arange(experts, dtype=jnp.int32)[None, None, :], axis=1
    )
    highest = jnp.max(jnp.where(named, logits, -jnp.inf), axis=1, keepdims=True)
    raised = jnp.where(named, jnp.exp(logits - highest), 0.0)
    gates = raised / jnp.sum(raised, axis=1, keepdims=True)
    gates = jnp.repeat(gates.T.reshape(n // 2, 2, rows), 2, axis=0)
    gates = lax.all_to_all(gates, "expert", split_axis=0, concat_axis=0, tiled=True)
    gates = gates.reshape(2 * n, rows)

    blocks = {0: normed}
    for k in order[1:]:
        blocks[k] = turn(tie(normed, blocks[k - 1]) if k > 1 else normed, k)
    sds = jax.ShapeDtypeStruct
    total = mixed
    firsts, placed, once = {}, [], []

    def add_first(near_low, far_low, near_high, far_high):
        keep = near_low.shape[0] // 2
        low = near_low + swap(far_low, 4).astype(f32)
        high = near_high + swap(far_high, 2).astype(f32)
        return low[:keep], low[keep:].astype(bf), high[:keep], high[keep:].astype(bf)

    def first(k, *others):
        if k not in firsts:
            firsts[k] = spread_first(tie(blocks[k], *others) if others else blocks[k])
        return firsts[k]

    for at, g in enumerate(groups):
        count = len(g)
        slots = 4 * cap * count
        span = 4 * count * rows
        xs = pltpu.VMEM((span, wide), bf)
        pieces = []
        for k in g:
            pieces += spread_second(*first(k))
        source = [
            (me // LAYER - k) % layers * LAYER + jnp.bitwise_xor(me % LAYER, 2 * q)
            for k in g
            for q in range(4)
        ]
        source = jnp.stack(source).astype(jnp.int32)
        idx = jnp.stack([2 * source + odd, 2 * source + 1 - odd]).astype(jnp.int32)
        after = [placed[-1][1]] if placed else []
        picked, lent = call(
            functools.partial(pick_kernel, cap, count, len(after)),
            [sds((slots, wide), bf)] * 2,
            "sv" + "h" * len(pieces),
            (idx, gates, *pieces),
            [
                xs,
                pltpu.VMEM((count, 8 * cap, 4 * rows), bf),
                pltpu.VMEM((count, 8 * cap, wide), bf),
                pltpu.SemaphoreType.DMA((8 * count,)),
                pltpu.SemaphoreType.DMA((2 * count,)),
            ],
            4 * slots * 4 * rows * wide,
            4 * span * wide,
            after,
            False,
        )
        borrowed = swap(lent, 1)
        (hs,) = call(
            functools.partial(shared_kernel, count, 1),
            [sds((span, 2 * hp), bf)],
            "hh" + "h" * len(pieces),
            (three, theirs, *pieces),
            [
                xs,
                pltpu.VMEM((n, depth, 4 * hp), bf),
                pltpu.SemaphoreType.DMA((8 * count + 4,)),
            ],
            8 * span * wide * hp,
            4 * span * wide,
            [lent],
        )
        after = [hs]
        if at + 1 < len(groups):
            after += first(groups[at + 1][0])
        done, back = call(
            functools.partial(expert_kernel, len(after)),
            [sds((slots, wide), bf)] * 2,
            "hhhh",
            (picked, borrowed, win, wout),
            [
                pltpu.VMEM((2 * slots, wide), bf),
                pltpu.VMEM((hidden // tile, wide // pack, pack, 2 * tile), bf),
                pltpu.VMEM((hidden, wide), bf),
                pltpu.VMEM((2 * slots, hidden), bf),
                pltpu.VMEM((2 * slots, wide), bf),
                pltpu.SemaphoreType.DMA((2,)),
                pltpu.SemaphoreType.DMA((2 * (hidden // tile) + 1,)),
                pltpu.SemaphoreType.DMA((2,)),
            ],
            12 * slots * wide * hidden,
            6 * wide * hidden,
            after,
            False,
        )
        if at == 0:
            for k in order[2:]:
                first(k, back)
        after = []
        if placed:
            once.append(add_first(*placed[-1]))
            after = [once[-1][1], once[-1][3]]
        placed.append(
            call(
                functools.partial(place_kernel, cap, count, len(after)),
                [sds((2 * count * rows, half), t) for t in (f32, bf, f32, bf)],
                "svvvvhh",
                (idx, gates, done, swap(back, 1), hs, three, theirs),
                [pltpu.VMEM((2 * count * rows, half), t) for t in (f32, bf, f32, bf)]
                + [
                    pltpu.VMEM((n, depth, 2 * hp), bf),
                    pltpu.VMEM((count, 2, 4 * rows, 4 * cap), bf),
                    pltpu.VMEM((count, 2, 4 * rows, LANES), f32),
                    pltpu.SemaphoreType.DMA((2,)),
                    pltpu.SemaphoreType.DMA((4,)),
                ],
                4 * span * wide * (4 * cap + hp),
                8 * span * wide,
                after,
                False,
            )
        )
    once.append(add_first(*placed[-1]))
    for g, (low, far_low, high, far_high) in zip(groups, once):
        low = low + swap(far_low, 2).astype(f32)
        high = high + swap(far_high, 4).astype(f32)
        both = jnp.concatenate([low, high], axis=1)
        for i, k in enumerate(g):
            part = both[i * rows : (i + 1) * rows]
            if k:
                part = turn(part.astype(bf), layers - k).astype(f32)
            total = total + part
    return total


def solution(mesh):
    n, mp = mesh.shape["expert"], mesh.shape["mp"]
    per_device = whole_rows if mp == 1 and n % LAYER == 0 else general
    return jax.shard_map(
        per_device,
        mesh=mesh,
        in_specs=(
            P("expert", "mp"),
            P("expert", "mp"),
            P("mp", "expert"),
            P("mp"),
            P("mp", None),
            P("expert", None, None, "mp"),
            P("expert", "mp", None),
            P("expert", None, "mp"),
            P("mp", "expert"),
            P("expert", None),
        ),
        out_specs=P("expert", "mp"),
        check_vma=False,
    )
```

```python
import functools

import jax
import jax.numpy as jnp
from jax import lax
from jax.experimental import pallas as pl
from jax.experimental.pallas import tpu as pltpu
from jax.sharding import PartitionSpec as P

LANES = 128
LAYER = 8


def capacity_of(rows, top, experts):
    return max(2, min(rows, rows * top // experts * 5 // 3))


def general(
    hidden_state,
    context,
    out_proj,
    norm_gain,
    router_weight,
    expert_in,
    expert_out,
    shared_in,
    shared_out,
    route_ids,
):
    rows_here, top = route_ids.shape
    experts = router_weight.shape[1]
    width = out_proj.shape[0] * lax.axis_size("mp")
    capacity = capacity_of(rows_here, top, experts)
    partial_attn = jnp.dot(
        context,
        lax.all_gather(out_proj, "expert", axis=1, tiled=True),
        preferred_element_type=jnp.float32,
    )
    attn = lax.psum_scatter(partial_attn, "mp", scatter_dimension=1, tiled=True)
    mixed = hidden_state.astype(jnp.float32) + attn
    gain = norm_gain.astype(jnp.float32)
    squares = lax.psum(jnp.sum(mixed * mixed, axis=1), "mp")
    inverse = lax.rsqrt(squares / width + 1e-06)[:, None]
    normed32 = mixed * inverse * gain
    logits = lax.psum(jnp.dot(normed32, router_weight, precision=lax.Precision.HIGHEST), "mp")
    normed = normed32.astype(jnp.bfloat16)
    gates = jax.nn.softmax(jnp.take_along_axis(logits, route_ids, axis=1), axis=1)
    full_rows = lax.all_gather(normed, "mp", axis=1, tiled=True)
    shared_width = shared_in.shape[2]
    piece = lax.all_gather(shared_in, "expert", axis=0, tiled=True)
    shared_both = jnp.dot(
        full_rows,
        piece.reshape(piece.shape[0], 2 * shared_width),
        preferred_element_type=jnp.float32,
    )
    shared_both = shared_both.reshape(rows_here, 2, shared_width)
    shared_hidden = (jax.nn.silu(shared_both[:, 0]) * shared_both[:, 1]).astype(jnp.bfloat16)
    shared_part = jnp.dot(
        shared_hidden,
        lax.all_gather(shared_out, "expert", axis=1, tiled=True),
        preferred_element_type=jnp.float32,
    )
    flat = route_ids.reshape(-1)
    onehot = (flat[:, None] == jnp.arange(experts, dtype=jnp.int32)[None, :]).astype(jnp.int32)
    position = jnp.sum(onehot * jnp.cumsum(onehot, axis=0), axis=1) - 1
    slot_of = flat * capacity + position
    source = (
        jnp.zeros((experts * capacity,), jnp.int32)
        .at[slot_of]
        .set(jnp.arange(flat.shape[0], dtype=jnp.int32) // top)
    )
    filled = jnp.zeros((experts * capacity,), jnp.bool_).at[slot_of].set(True)
    outgoing = jnp.where(filled[:, None], normed[source], jnp.zeros((), jnp.bfloat16)).reshape(
        experts, capacity, normed.shape[1]
    )
    quarter = expert_in.shape[3]
    weights_in = expert_in[0].reshape(width, 2 * quarter)
    incoming = lax.all_to_all(outgoing, "expert", split_axis=0, concat_axis=0, tiled=True)
    sources = incoming.shape[0]
    items = incoming.shape[1]
    gathered = lax.all_gather(incoming, "mp", axis=2, tiled=True).reshape(sources * items, width)
    inner = jnp.dot(gathered, weights_in, preferred_element_type=jnp.float32).reshape(
        -1, 2, quarter
    )
    hidden = (jax.nn.silu(inner[:, 0]) * inner[:, 1]).astype(jnp.bfloat16)
    partial_out = jnp.dot(hidden, expert_out[0], preferred_element_type=jnp.float32).astype(
        jnp.bfloat16
    )
    partial_out = partial_out.reshape(sources, items, width)
    result = lax.all_to_all(partial_out, "expert", split_axis=0, concat_axis=0, tiled=True)
    picked = result.reshape(experts * capacity, result.shape[2])[slot_of]
    slot_total = lax.psum_scatter(
        lax.optimization_barrier(picked).astype(jnp.float32).astype(jnp.bfloat16),
        "mp",
        scatter_dimension=1,
        tiled=True,
    )
    expert_sum = lax.optimization_barrier(slot_total).astype(jnp.float32)
    expert_sum = expert_sum.reshape(rows_here, top, expert_sum.shape[1])
    routed = jnp.sum(gates[:, :, None] * expert_sum, axis=1)
    shared = lax.psum_scatter(shared_part, "mp", scatter_dimension=1, tiled=True)
    return mixed + routed + shared


def swap(x, bit):
    n = lax.axis_size("expert")
    return lax.ppermute(x, "expert", [(i, i ^ bit) for i in range(n)])


def silu(v):
    return v / (1.0 + jnp.exp(-v))


def spread_first(block, rows):
    half = block.shape[1] // 2
    h0, h1 = block[:, :half], block[:rows, half:]
    return jnp.concatenate([h0, swap(h0, 2)], axis=0), jnp.concatenate([h1, swap(h1, 4)], axis=0)


def spread_second(l0, l1):
    return l0, swap(l0, 4), l1, swap(l1, 2)


def along_z(block, layers):
    blocks = [block]
    for k in range(1, layers):
        low = k & -k
        blocks.append(swap(blocks[k - low], LAYER * low))
    return blocks


def tie(x, *others):
    return lax.optimization_barrier((x, *others))[0]


class Copies:
    def __init__(self, sems):
        self.sems, self.all = sems, []

    def start(self, src, dst):
        c = pltpu.make_async_copy(src, dst, self.sems.at[len(self.all)])
        c.start()
        self.all.append(c)

    def wait(self):
        for c in self.all:
            c.wait()


PIECES = ((0, 0, (0, 1)), (1, 0, (2, 3)), (2, 1, (0, 2)), (3, 1, (1, 3)))


def fetch_rows(copies, pieces, rows, xs):
    half = xs.shape[1] // 2
    for n, h, chips in PIECES:
        stride = pieces[n].shape[0] // 2
        for a, q in enumerate(chips):
            copies.start(
                pieces[n].at[pl.ds(a * stride, rows)],
                xs.at[pl.ds(q * rows, rows), pl.ds(h * half, half)],
            )


def fetch_gates(copies, left, rows, to):
    for piece, (_, _, chips) in zip(left, PIECES):
        stride = piece.shape[0] // 2
        for a, q in enumerate(chips):
            copies.start(piece.at[pl.ds(a * stride + rows, stride - rows)], to.at[q])


def slots_of(sent, idx_ref, expert, experts, cap, rows):
    extra, half = sent.shape[1:]
    each = half // rows
    tall = experts // each
    line, column = idx_ref[2 * expert], idx_ref[2 * expert + 1]
    r = lax.broadcasted_iota(jnp.int32, (extra, half), 0)
    wanted = (r == line) | (r == line + tall) | (r == line + 2 * tall)
    found = []
    for q in range(4):
        parts = jnp.where(wanted, sent[q].astype(jnp.float32), 0.0)
        parts = jnp.sum(parts, axis=0, keepdims=True)
        g = jnp.zeros((1, rows), jnp.float32)
        for j in range(each):
            g = jnp.where(column == j, parts[:, j * rows : (j + 1) * rows], g)
        found.append(g)
    g = jnp.concatenate(found, axis=0)
    chosen = g > 0.0
    r_io = lax.broadcasted_iota(jnp.int32, (rows, rows), 0)
    c_io = lax.broadcasted_iota(jnp.int32, (rows, rows), 1)
    upto = jnp.where(r_io <= c_io, 1.0, 0.0).astype(jnp.bfloat16)
    count = jnp.dot(
        jnp.where(chosen, 1.0, 0.0).astype(jnp.bfloat16), upto, preferred_element_type=jnp.float32
    ).astype(jnp.int32)
    first = lax.broadcasted_iota(jnp.int32, (4, rows), 0) * cap
    return g, jnp.where(chosen, first + count - 1, -1)


def steps(total, most):
    step = min(most, total)
    return [(n, step) for n in range(0, total, step)]


def attention_kernel(groups, rows, idx_ref, mine_ref, other_ref, *rest):
    pieces, (keep_ref, send_ref, w_v, sems) = rest[: 4 * groups], rest[4 * groups :]
    half = w_v.shape[1] // 2
    count = pieces[0].shape[0] // (2 * rows)
    copies = Copies(sems)
    for g in range(groups):
        l0, r0, l1, r1 = pieces[4 * g : 4 * g + 4]
        for h, (near, far, first, second) in enumerate(((l0, r0, 1, 2), (l1, r1, 2, 1))):
            for piece, base in ((near, 0), (far, second)):
                for a, q in enumerate((base, base + first)):
                    for i in range(count):
                        chip = idx_ref[(g * count + i) * 4 + q]
                        to = pl.ds(pl.multiple_of(chip * rows, rows), rows)
                        copies.start(
                            piece.at[pl.ds((a * count + i) * rows, rows)],
                            w_v.at[to, pl.ds(h * half, half)],
                        )
    copies.wait()
    both = jnp.concatenate([mine_ref[...], other_ref[...]], axis=0)
    here = mine_ref.shape[0]
    for n, step in steps(w_v.shape[0], 512):
        part = lax.dot_general(
            both,
            w_v[pl.ds(n, step), :],
            (((1,), (1,)), ((), ())),
            preferred_element_type=jnp.float32,
        )
        keep_ref[:, pl.ds(n, step)] = part[:here]
        send_ref[:, pl.ds(n, step)] = part[here:]


def pick_kernel(cap, rows, experts, unused, idx_ref, *rest):
    pieces = rest[:4]
    mine_ref, other_ref, xs, sent, pick, out_v, x_sem, g_sem, o_sem = rest[4 + unused :]
    gates, copies = Copies(g_sem), Copies(x_sem)
    fetch_gates(gates, pieces[:2], rows, sent)
    fetch_rows(copies, pieces, rows, xs)
    slots = 4 * cap
    numbers = lax.broadcasted_iota(jnp.int32, (slots, rows), 0)
    gates.wait()
    for e in range(2):
        _, slot = slots_of(sent, idx_ref, e, experts, cap, rows)
        for q in range(4):
            pick[pl.ds(e * slots, slots), pl.ds(q * rows, rows)] = jnp.where(
                numbers == slot[q : q + 1, :], 1.0, 0.0
            ).astype(jnp.bfloat16)
    copies.wait()
    for n, step in steps(xs.shape[1], 512):
        out_v[:, pl.ds(n, step)] = jnp.dot(
            pick[...], xs[:, pl.ds(n, step)], preferred_element_type=jnp.float32
        ).astype(jnp.bfloat16)
    outs = Copies(o_sem)
    outs.start(out_v.at[pl.ds(slots, slots)], other_ref)
    outs.start(out_v.at[pl.ds(0, slots)], mine_ref)
    outs.wait()


def shared_kernel(rows, unused, three_ref, theirs_ref, *rest):
    pieces, (hs_ref, xs, w_v, x_sem) = rest[:4], rest[4 + unused :]
    hp = three_ref.shape[3]
    copies = Copies(x_sem)
    fetch_rows(copies, pieces, rows, xs)
    for e, ref in enumerate((three_ref, theirs_ref)):
        for h in range(2):
            copies.start(ref.at[:, h], w_v.at[:, :, pl.ds((2 * h + e) * hp, hp)])
    copies.wait()
    w = w_v[...].reshape(xs.shape[1], 4 * hp)
    for m, step in steps(4 * rows, 2 * rows):
        both = jnp.dot(xs[pl.ds(m, step), :], w, preferred_element_type=jnp.float32)
        hs_ref[pl.ds(m, step), :] = (silu(both[:, : 2 * hp]) * both[:, 2 * hp :]).astype(
            jnp.bfloat16
        )


def expert_kernel(unused, mine_ref, other_ref, win_ref, wout_ref, *rest):
    mine_out, other_out, x_v, win_v, wout_v, hid_v, y_v, x_sem, w_sem, o_sem = rest[unused:]
    slots, wide = mine_ref.shape
    tiles, tile = win_v.shape[0], win_v.shape[3] // 2
    rows = Copies(x_sem)
    rows.start(mine_ref, x_v.at[pl.ds(0, slots)])
    rows.start(other_ref, x_v.at[pl.ds(slots, slots)])
    copies = Copies(w_sem)
    for t in range(tiles):
        for h in range(2):
            copies.start(
                win_ref.at[:, h, :, pl.ds(t * tile, tile)],
                win_v.at[t, :, :, pl.ds(h * tile, tile)],
            )
    copies.start(wout_ref, wout_v)
    rows.wait()
    here = 0
    for t in range(tiles):
        if t == here:
            here = min(2 * here + 1, tiles)
            for c in copies.all[2 * t : 2 * here]:
                c.wait()
        both = jnp.dot(
            x_v[...], win_v[t].reshape(wide, 2 * tile), preferred_element_type=jnp.float32
        )
        hid_v[:, pl.ds(t * tile, tile)] = (silu(both[:, :tile]) * both[:, tile:]).astype(
            jnp.bfloat16
        )
    copies.all[2 * tiles].wait()
    outs = Copies(o_sem)
    for n, step in steps(wide, 512):
        y_v[:, pl.ds(n, step)] = jnp.dot(
            hid_v[...], wout_v[:, pl.ds(n, step)], preferred_element_type=jnp.float32
        ).astype(jnp.bfloat16)
    outs.start(y_v.at[pl.ds(slots, slots)], other_out)
    outs.start(y_v.at[pl.ds(0, slots)], mine_out)
    outs.wait()


def place_kernel(cap, rows, experts, unused, idx_ref, mine_ref, other_ref, hs_ref, *rest):
    three_ref, theirs_ref, l0, r0 = rest[:4]
    refs, rest = rest[4 + unused : 8 + unused], rest[8 + unused :]
    bufs, (w_v, sent, place, gate_col, g_sem, w_sem, o_sem) = rest[:4], rest[4:]
    near_low, far_low, near_high, far_high = bufs
    wide, half = mine_ref.shape[1], near_low.shape[1]
    hp = three_ref.shape[3]
    slots = 4 * cap
    f32 = jnp.float32
    gates, copies = Copies(g_sem), Copies(w_sem)
    fetch_gates(gates, (l0, r0), rows, sent)
    for e, ref in enumerate((three_ref, theirs_ref)):
        copies.start(ref.at[:, 2], w_v.at[:, :, pl.ds(e * hp, hp)])
    r_io = lax.broadcasted_iota(jnp.int32, (rows, rows), 0)
    c_io = lax.broadcasted_iota(jnp.int32, (rows, rows), 1)
    eye = r_io == c_io
    numbers = lax.broadcasted_iota(jnp.int32, (rows, slots), 1)
    gates.wait()
    for e in range(2):
        g, slot = slots_of(sent, idx_ref, e, experts, cap, rows)
        for q in range(4):
            at = pl.ds(q * rows, rows)
            col = jnp.sum(jnp.where(eye, slot[q : q + 1, :], 0), axis=1, keepdims=True)
            place[e, at, :] = jnp.where(numbers == col, 1.0, 0.0).astype(jnp.bfloat16)
            gcol = jnp.sum(jnp.where(eye, g[q : q + 1, :], 0.0), axis=1, keepdims=True)
            gate_col[e, at, :] = jnp.broadcast_to(gcol, (rows, LANES))
    copies.wait()
    depth = w_v.shape[1]
    outs = Copies(o_sem)
    for n, step in steps(wide, min(256, half)):
        cols = pl.ds(n, step)
        if step % depth == 0:
            down = w_v[pl.ds(n // depth, step // depth)].reshape(step, 2 * hp)
        else:
            down = w_v[...].reshape(wide, 2 * hp)[n : n + step]
        total = lax.dot_general(
            hs_ref[...], down, (((1,), (1,)), ((), ())), preferred_element_type=f32
        )
        for e, ref in enumerate((mine_ref, other_ref)):
            y = jnp.dot(place[e], ref[:, cols], preferred_element_type=f32)
            total = total + gate_col[e][:, 0:1] * y
        if n < half:
            near, far, order, at = near_low, far_low, (0, 1, 2, 3), pl.ds(n, step)
        else:
            near, far, order, at = near_high, far_high, (0, 2, 1, 3), pl.ds(n - half, step)
        for a in range(2):
            to = pl.ds(a * rows, rows)
            q = order[a] * rows
            near[to, at] = total[q : q + rows]
            q = order[2 + a] * rows
            far[to, at] = total[q : q + rows].astype(far.dtype)
        if (n + step) % half == 0:
            k = 2 * (n // half)
            outs.start(bufs[k + 1], refs[k + 1])
            outs.start(bufs[k], refs[k])
    outs.wait()


def call(body, out_shape, in_specs, args, scratch, after=(), outs_in_vmem=True):
    vmem = pl.BlockSpec(memory_space=pltpu.VMEM)
    hbm = pl.BlockSpec(memory_space=pl.ANY)
    kinds = {"s": pl.BlockSpec(memory_space=pltpu.SMEM), "v": vmem, "h": hbm}
    return pl.pallas_call(
        body,
        out_shape=out_shape,
        in_specs=[kinds[k] for k in in_specs] + [hbm] * len(after),
        out_specs=tuple([vmem if outs_in_vmem else hbm] * len(out_shape)),
        scratch_shapes=scratch,
        compiler_params=pltpu.CompilerParams(vmem_limit_bytes=48 * 1024 * 1024),
        cost_estimate=pl.CostEstimate(flops=1, bytes_accessed=1, transcendentals=0),
    )(*args, *after)


def attention(context, out_proj, before, exchange):
    bf, f32 = jnp.bfloat16, jnp.float32
    me = lax.axis_index("expert")
    layers = lax.axis_size("expert") // LAYER
    odd = me % 2 == 1
    wide = context.shape[1]
    half = wide // 2

    def halves(lo, hi):
        return jnp.where(odd, hi, lo), jnp.where(odd, lo, hi)

    turned = out_proj.T
    mine, other = halves(turned[:, :half], turned[:, half:])
    pair = jnp.concatenate(halves(mine, swap(other, 1)), axis=0)
    mine, other = halves(context[:, :half], context[:, half:])
    got = swap(other, 1)
    cut = pair.shape[0]
    blocks = along_z(pair, layers)
    twos = [list(range(i, min(i + 2, layers))) for i in range(0, layers, 2)]
    firsts = [
        spread_first(jnp.concatenate([blocks[k] for k in two], axis=0), cut * len(two))
        for two in twos
    ]
    exchange = lax.all_to_all(
        tie(exchange, *(v for first in firsts for v in first)),
        "expert",
        split_axis=0,
        concat_axis=0,
        tiled=True,
    )
    pieces, chips = [], []
    for two, first in zip(twos, firsts):
        pieces += spread_second(*first)
        for k in two:
            layer = jnp.bitwise_xor(me // LAYER, k)
            chips += [layer * (LAYER // 2) + jnp.bitwise_xor(me % LAYER // 2, q) for q in range(4)]
    mine, before = lax.optimization_barrier((mine, before))
    here = context.shape[0]
    keep, send = call(
        functools.partial(attention_kernel, len(twos), cut),
        [jax.ShapeDtypeStruct((here, wide), f32)] * 2,
        "svv" + "h" * len(pieces),
        (jnp.stack(chips).astype(jnp.int32), mine, got, *pieces),
        [
            pltpu.VMEM((out_proj.shape[1] * lax.axis_size("expert"), half), bf),
            pltpu.SemaphoreType.DMA((8 * layers,)),
        ],
    )
    return keep + swap(send, 1), before, exchange


def whole_rows(
    hidden_state,
    context,
    out_proj,
    norm_gain,
    router_weight,
    expert_in,
    expert_out,
    shared_in,
    shared_out,
    route_ids,
):
    bf, f32 = jnp.bfloat16, jnp.float32
    n = lax.axis_size("expert")
    layers = n // LAYER
    me = lax.axis_index("expert")
    odd = me % 2
    rows, top = route_ids.shape
    experts = router_weight.shape[1]
    wide = out_proj.shape[0]
    half = wide // 2
    cap = capacity_of(rows, top, experts)
    pack = 16
    win = expert_in[0].reshape(wide // pack, pack, 2, -1).transpose(0, 2, 1, 3)
    wout = expert_out[0]
    hidden = wout.shape[0]
    tile = LANES if hidden % LANES == 0 else hidden

    own = shared_in.shape[2] // n
    depth = shared_in.shape[0]
    hp = -(-own // LANES) * LANES
    three = jnp.concatenate([shared_in.transpose(1, 0, 2), shared_out.T[None]], axis=0)
    three = three.reshape(3, depth, n, own)
    three = jnp.pad(three, ((0, 0), (0, 0), (0, 0), (0, hp - own))).transpose(2, 0, 1, 3)

    attn, win, three = attention(context, out_proj, win, three)
    theirs = swap(three, 1)
    mixed = hidden_state.astype(f32) + attn
    inverse = lax.rsqrt(jnp.mean(mixed * mixed, axis=1, keepdims=True) + 1e-06)
    normed32 = mixed * inverse * norm_gain.astype(f32)
    normed = normed32.astype(bf)
    logits = jnp.dot(normed32, router_weight, precision=lax.Precision.HIGHEST)
    named = jnp.any(
        route_ids[:, :, None] == jnp.arange(experts, dtype=jnp.int32)[None, None, :], axis=1
    )
    highest = jnp.max(jnp.where(named, logits, -jnp.inf), axis=1, keepdims=True)
    raised = jnp.where(named, jnp.exp(logits - highest), 0.0)
    gates = raised / jnp.sum(raised, axis=1, keepdims=True)

    rest, parts = gates.T, []
    for _ in range(3):
        parts.append(lax.reduce_precision(rest, 8, 7))
        rest = rest - parts[-1]
    below = jnp.stack(parts).astype(bf).reshape(-1, half)
    extra = -(-below.shape[0] // 16) * 16
    below = jnp.pad(below, ((0, extra - below.shape[0]), (0, half)))
    blocks = along_z(jnp.concatenate([normed, below], axis=0), layers)

    each = half // rows
    chip_experts = (me, jnp.bitwise_xor(me, 1))
    idx = jnp.stack([v for e in chip_experts for v in (e // each, e % each)]).astype(jnp.int32)
    slots, span = 4 * cap, 4 * rows
    sds, dma = jax.ShapeDtypeStruct, pltpu.SemaphoreType.DMA
    xs = pltpu.VMEM((span, wide), bf)
    sent = pltpu.VMEM((4, extra, half), bf)

    def add_first(near_low, far_low, near_high, far_high):
        low = near_low + swap(far_low, 4).astype(f32)
        high = near_high + swap(far_high, 2).astype(f32)
        return low[:rows], low[rows:].astype(bf), high[:rows], high[rows:].astype(bf)

    order = [0] + sorted(range(1, layers), key=lambda k: (k != 1, -k))
    firsts, placed, once = {}, [], []

    def first(k):
        if k not in firsts:
            firsts[k] = spread_first(blocks[k], rows)
        return firsts[k]

    upcoming = spread_second(*first(0))
    for at, k in enumerate(order):
        pieces = upcoming
        after = [placed[-1][1]] if placed else [theirs]
        picked, lent = call(
            functools.partial(pick_kernel, cap, rows, experts, len(after)),
            [sds((slots, wide), bf)] * 2,
            "shhhh",
            (idx, *pieces),
            [
                xs,
                sent,
                pltpu.VMEM((2 * slots, span), bf),
                pltpu.VMEM((2 * slots, wide), bf),
                dma((8,)),
                dma((4,)),
                dma((2,)),
            ],
            after,
            False,
        )
        borrowed = swap(lent, 1)
        (hs,) = call(
            functools.partial(shared_kernel, rows, 1),
            [sds((span, 2 * hp), bf)],
            "hhhhhh",
            (three, theirs, *pieces),
            [xs, pltpu.VMEM((n, depth, 4 * hp), bf), dma((12,))],
            [lent],
        )
        after = [hs]
        if at + 1 < layers:
            after += first(order[at + 1])
        done, back = call(
            functools.partial(expert_kernel, len(after)),
            [sds((slots, wide), bf)] * 2,
            "hhhh",
            (picked, borrowed, win, wout),
            [
                pltpu.VMEM((2 * slots, wide), bf),
                pltpu.VMEM((hidden // tile, wide // pack, pack, 2 * tile), bf),
                pltpu.VMEM((hidden, wide), bf),
                pltpu.VMEM((2 * slots, hidden), bf),
                pltpu.VMEM((2 * slots, wide), bf),
                dma((2,)),
                dma((2 * (hidden // tile) + 1,)),
                dma((2,)),
            ],
            after,
            False,
        )
        after = []
        if at + 1 < layers:
            upcoming = spread_second(*first(order[at + 1]))
            back = tie(back, upcoming[1], upcoming[3])
        if placed:
            once.append(add_first(*placed[-1]))
            after = [once[-1][1], once[-1][3]]
        placed.append(
            call(
                functools.partial(place_kernel, cap, rows, experts, len(after)),
                [sds((2 * rows, half), t) for t in (f32, bf, f32, bf)],
                "svvvhhhh",
                (idx, done, swap(back, 1), hs, three, theirs, pieces[0], pieces[1]),
                [pltpu.VMEM((2 * rows, half), t) for t in (f32, bf, f32, bf)]
                + [
                    pltpu.VMEM((n, depth, 2 * hp), bf),
                    sent,
                    pltpu.VMEM((2, span, slots), bf),
                    pltpu.VMEM((2, span, LANES), f32),
                    dma((4,)),
                    dma((2,)),
                    dma((4,)),
                ],
                after,
                False,
            )
        )
    once.append(add_first(*placed[-1]))
    sums = {}
    for k, (low, far_low, high, far_high) in zip(order, once):
        low = low + swap(far_low, 2).astype(f32)
        high = high + swap(far_high, 4).astype(f32)
        sums[k] = jnp.concatenate([low, high], axis=1)
    for k in reversed(range(1, layers)):
        low = k & -k
        sums[k - low] = sums[k - low] + swap(sums[k].astype(bf), LAYER * low).astype(f32)
    return mixed + sums[0]


def solution(mesh):
    n, mp = mesh.shape["expert"], mesh.shape["mp"]
    fits = mp == 1 and n % LAYER == 0 and (n // LAYER) & (n // LAYER - 1) == 0
    per_device = whole_rows if fits else general
    return jax.shard_map(
        per_device,
        mesh=mesh,
        in_specs=(
            P("expert", "mp"),
            P("expert", "mp"),
            P("mp", "expert"),
            P("mp"),
            P("mp", None),
            P("expert", None, None, "mp"),
            P("expert", "mp", None),
            P("expert", None, "mp"),
            P("mp", "expert"),
            P("expert", None),
        ),
        out_specs=P("expert", "mp"),
        check_vma=False,
    )
```

```python
import functools

import jax
import jax.numpy as jnp
from jax import lax
from jax.experimental import pallas as pl
from jax.experimental.pallas import tpu as pltpu
from jax.sharding import PartitionSpec as P

LANES = 128
LAYER = 8


def capacity_of(rows, top, experts):
    return max(2, min(rows, rows * top // experts * 5 // 3))


def general(
    hidden_state,
    context,
    out_proj,
    norm_gain,
    router_weight,
    expert_in,
    expert_out,
    shared_in,
    shared_out,
    route_ids,
):
    rows_here, top = route_ids.shape
    experts = router_weight.shape[1]
    width = out_proj.shape[0] * lax.axis_size("mp")
    capacity = capacity_of(rows_here, top, experts)
    partial_attn = jnp.dot(
        context,
        lax.all_gather(out_proj, "expert", axis=1, tiled=True),
        preferred_element_type=jnp.float32,
    )
    attn = lax.psum_scatter(partial_attn, "mp", scatter_dimension=1, tiled=True)
    mixed = hidden_state.astype(jnp.float32) + attn
    gain = norm_gain.astype(jnp.float32)
    squares = lax.psum(jnp.sum(mixed * mixed, axis=1), "mp")
    inverse = lax.rsqrt(squares / width + 1e-06)[:, None]
    normed32 = mixed * inverse * gain
    logits = lax.psum(jnp.dot(normed32, router_weight, precision=lax.Precision.HIGHEST), "mp")
    normed = normed32.astype(jnp.bfloat16)
    gates = jax.nn.softmax(jnp.take_along_axis(logits, route_ids, axis=1), axis=1)
    full_rows = lax.all_gather(normed, "mp", axis=1, tiled=True)
    shared_width = shared_in.shape[2]
    piece = lax.all_gather(shared_in, "expert", axis=0, tiled=True)
    shared_both = jnp.dot(
        full_rows,
        piece.reshape(piece.shape[0], 2 * shared_width),
        preferred_element_type=jnp.float32,
    )
    shared_both = shared_both.reshape(rows_here, 2, shared_width)
    shared_hidden = (jax.nn.silu(shared_both[:, 0]) * shared_both[:, 1]).astype(jnp.bfloat16)
    shared_part = jnp.dot(
        shared_hidden,
        lax.all_gather(shared_out, "expert", axis=1, tiled=True),
        preferred_element_type=jnp.float32,
    )
    flat = route_ids.reshape(-1)
    onehot = (flat[:, None] == jnp.arange(experts, dtype=jnp.int32)[None, :]).astype(jnp.int32)
    position = jnp.sum(onehot * jnp.cumsum(onehot, axis=0), axis=1) - 1
    slot_of = flat * capacity + position
    source = (
        jnp.zeros((experts * capacity,), jnp.int32)
        .at[slot_of]
        .set(jnp.arange(flat.shape[0], dtype=jnp.int32) // top)
    )
    filled = jnp.zeros((experts * capacity,), jnp.bool_).at[slot_of].set(True)
    outgoing = jnp.where(filled[:, None], normed[source], jnp.zeros((), jnp.bfloat16)).reshape(
        experts, capacity, normed.shape[1]
    )
    quarter = expert_in.shape[3]
    weights_in = expert_in[0].reshape(width, 2 * quarter)
    incoming = lax.all_to_all(outgoing, "expert", split_axis=0, concat_axis=0, tiled=True)
    sources = incoming.shape[0]
    items = incoming.shape[1]
    gathered = lax.all_gather(incoming, "mp", axis=2, tiled=True).reshape(sources * items, width)
    inner = jnp.dot(gathered, weights_in, preferred_element_type=jnp.float32).reshape(
        -1, 2, quarter
    )
    hidden = (jax.nn.silu(inner[:, 0]) * inner[:, 1]).astype(jnp.bfloat16)
    partial_out = jnp.dot(hidden, expert_out[0], preferred_element_type=jnp.float32).astype(
        jnp.bfloat16
    )
    partial_out = partial_out.reshape(sources, items, width)
    result = lax.all_to_all(partial_out, "expert", split_axis=0, concat_axis=0, tiled=True)
    picked = result.reshape(experts * capacity, result.shape[2])[slot_of]
    slot_total = lax.psum_scatter(
        lax.optimization_barrier(picked).astype(jnp.float32).astype(jnp.bfloat16),
        "mp",
        scatter_dimension=1,
        tiled=True,
    )
    expert_sum = lax.optimization_barrier(slot_total).astype(jnp.float32)
    expert_sum = expert_sum.reshape(rows_here, top, expert_sum.shape[1])
    routed = jnp.sum(gates[:, :, None] * expert_sum, axis=1)
    shared = lax.psum_scatter(shared_part, "mp", scatter_dimension=1, tiled=True)
    return mixed + routed + shared


def swap(x, bit):
    n = lax.axis_size("expert")
    return lax.ppermute(x, "expert", [(i, i ^ bit) for i in range(n)])


def silu(v):
    return v / (1.0 + jnp.exp(-v))


def spread_first(block, rows):
    half = block.shape[1] // 2
    h0, h1 = block[:, :half], block[:rows, half:]
    return jnp.concatenate([h0, swap(h0, 2)], axis=0), jnp.concatenate([h1, swap(h1, 4)], axis=0)


def spread_second(l0, l1):
    return l0, swap(l0, 4), l1, swap(l1, 2)


def along_z(block, layers):
    blocks = [block]
    for k in range(1, layers):
        low = k & -k
        blocks.append(swap(blocks[k - low], LAYER * low))
    return blocks


def tie(x, *others):
    return lax.optimization_barrier((x, *others))[0]


class Copies:
    def __init__(self, sems):
        self.sems, self.all = sems, []

    def start(self, src, dst):
        c = pltpu.make_async_copy(src, dst, self.sems.at[len(self.all)])
        c.start()
        self.all.append(c)

    def wait(self):
        for c in self.all:
            c.wait()


PIECES = ((0, 0, (0, 1)), (1, 0, (2, 3)), (2, 1, (0, 2)), (3, 1, (1, 3)))


def fetch_rows(copies, pieces, rows, xs):
    half = xs.shape[1] // 2
    for n, h, chips in PIECES:
        stride = pieces[n].shape[0] // 2
        for a, q in enumerate(chips):
            copies.start(
                pieces[n].at[pl.ds(a * stride, rows)],
                xs.at[pl.ds(q * rows, rows), pl.ds(h * half, half)],
            )


def fetch_gates(copies, left, rows, to):
    for piece, (_, _, chips) in zip(left, PIECES):
        stride = piece.shape[0] // 2
        for a, q in enumerate(chips):
            copies.start(piece.at[pl.ds(a * stride + rows, stride - rows)], to.at[q])


def slots_of(sent, idx_ref, expert, experts, cap, rows):
    extra, half = sent.shape[1:]
    each = half // rows
    tall = experts // each
    line, column = idx_ref[2 * expert], idx_ref[2 * expert + 1]
    r = lax.broadcasted_iota(jnp.int32, (extra, half), 0)
    wanted = (r == line) | (r == line + tall) | (r == line + 2 * tall)
    found = []
    for q in range(4):
        parts = jnp.where(wanted, sent[q].astype(jnp.float32), 0.0)
        parts = jnp.sum(parts, axis=0, keepdims=True)
        g = jnp.zeros((1, rows), jnp.float32)
        for j in range(each):
            g = jnp.where(column == j, parts[:, j * rows : (j + 1) * rows], g)
        found.append(g)
    g = jnp.concatenate(found, axis=0)
    chosen = g > 0.0
    r_io = lax.broadcasted_iota(jnp.int32, (rows, rows), 0)
    c_io = lax.broadcasted_iota(jnp.int32, (rows, rows), 1)
    upto = jnp.where(r_io <= c_io, 1.0, 0.0).astype(jnp.bfloat16)
    count = jnp.dot(
        jnp.where(chosen, 1.0, 0.0).astype(jnp.bfloat16), upto, preferred_element_type=jnp.float32
    ).astype(jnp.int32)
    first = lax.broadcasted_iota(jnp.int32, (4, rows), 0) * cap
    return g, jnp.where(chosen, first + count - 1, -1)


def steps(total, most):
    step = min(most, total)
    return [(n, step) for n in range(0, total, step)]


def attention_kernel(groups, rows, idx_ref, mine_ref, other_ref, *rest):
    pieces, (keep_ref, send_ref, w_v, sems) = rest[: 4 * groups], rest[4 * groups :]
    half = w_v.shape[1] // 2
    count = pieces[0].shape[0] // (2 * rows)
    copies = Copies(sems)
    for g in range(groups):
        l0, r0, l1, r1 = pieces[4 * g : 4 * g + 4]
        for h, (near, far, first, second) in enumerate(((l0, r0, 1, 2), (l1, r1, 2, 1))):
            for piece, base in ((near, 0), (far, second)):
                for a, q in enumerate((base, base + first)):
                    for i in range(count):
                        chip = idx_ref[(g * count + i) * 4 + q]
                        to = pl.ds(pl.multiple_of(chip * rows, rows), rows)
                        copies.start(
                            piece.at[pl.ds((a * count + i) * rows, rows)],
                            w_v.at[to, pl.ds(h * half, half)],
                        )
    copies.wait()
    both = jnp.concatenate([mine_ref[...], other_ref[...]], axis=0)
    here = mine_ref.shape[0]
    for n, step in steps(w_v.shape[0], 512):
        part = lax.dot_general(
            both,
            w_v[pl.ds(n, step), :],
            (((1,), (1,)), ((), ())),
            preferred_element_type=jnp.float32,
        )
        keep_ref[:, pl.ds(n, step)] = part[:here]
        send_ref[:, pl.ds(n, step)] = part[here:]


def pick_kernel(cap, rows, experts, unused, idx_ref, *rest):
    pieces = rest[:4]
    mine_ref, other_ref, xs, sent, pick, out_v, x_sem, g_sem, o_sem = rest[4 + unused :]
    gates, copies = Copies(g_sem), Copies(x_sem)
    fetch_gates(gates, pieces[:2], rows, sent)
    fetch_rows(copies, pieces, rows, xs)
    slots = 4 * cap
    numbers = lax.broadcasted_iota(jnp.int32, (slots, rows), 0)
    gates.wait()
    for e in range(2):
        _, slot = slots_of(sent, idx_ref, e, experts, cap, rows)
        for q in range(4):
            pick[pl.ds(e * slots, slots), pl.ds(q * rows, rows)] = jnp.where(
                numbers == slot[q : q + 1, :], 1.0, 0.0
            ).astype(jnp.bfloat16)
    copies.wait()
    for n, step in steps(xs.shape[1], 512):
        out_v[:, pl.ds(n, step)] = jnp.dot(
            pick[...], xs[:, pl.ds(n, step)], preferred_element_type=jnp.float32
        ).astype(jnp.bfloat16)
    outs = Copies(o_sem)
    outs.start(out_v.at[pl.ds(slots, slots)], other_ref)
    outs.start(out_v.at[pl.ds(0, slots)], mine_ref)
    outs.wait()


def shared_kernel(rows, unused, three_ref, theirs_ref, *rest):
    pieces, (hs_ref, xs, w_v, x_sem) = rest[:4], rest[4 + unused :]
    hp = three_ref.shape[3]
    copies = Copies(x_sem)
    fetch_rows(copies, pieces, rows, xs)
    for e, ref in enumerate((three_ref, theirs_ref)):
        for h in range(2):
            copies.start(ref.at[:, h], w_v.at[:, :, pl.ds((2 * h + e) * hp, hp)])
    copies.wait()
    w = w_v[...].reshape(xs.shape[1], 4 * hp)
    for m, step in steps(4 * rows, 2 * rows):
        both = jnp.dot(xs[pl.ds(m, step), :], w, preferred_element_type=jnp.float32)
        hs_ref[pl.ds(m, step), :] = (silu(both[:, : 2 * hp]) * both[:, 2 * hp :]).astype(
            jnp.bfloat16
        )


def expert_kernel(unused, mine_ref, other_ref, win_ref, wout_ref, *rest):
    mine_out, other_out, x_v, win_v, wout_v, hid_v, y_v, x_sem, w_sem, o_sem = rest[unused:]
    slots, wide = mine_ref.shape
    tiles, tile = win_v.shape[0], win_v.shape[3] // 2
    rows = Copies(x_sem)
    rows.start(mine_ref, x_v.at[pl.ds(0, slots)])
    rows.start(other_ref, x_v.at[pl.ds(slots, slots)])
    copies = Copies(w_sem)
    for t in range(tiles):
        for h in range(2):
            copies.start(
                win_ref.at[:, h, :, pl.ds(t * tile, tile)],
                win_v.at[t, :, :, pl.ds(h * tile, tile)],
            )
    copies.start(wout_ref, wout_v)
    rows.wait()
    here = 0
    for t in range(tiles):
        if t == here:
            here = min(2 * here + 1, tiles)
            for c in copies.all[2 * t : 2 * here]:
                c.wait()
        both = jnp.dot(
            x_v[...], win_v[t].reshape(wide, 2 * tile), preferred_element_type=jnp.float32
        )
        hid_v[:, pl.ds(t * tile, tile)] = (silu(both[:, :tile]) * both[:, tile:]).astype(
            jnp.bfloat16
        )
    copies.all[2 * tiles].wait()
    outs = Copies(o_sem)
    for n, step in steps(wide, 512):
        y_v[:, pl.ds(n, step)] = jnp.dot(
            hid_v[...], wout_v[:, pl.ds(n, step)], preferred_element_type=jnp.float32
        ).astype(jnp.bfloat16)
    outs.start(y_v.at[pl.ds(slots, slots)], other_out)
    outs.start(y_v.at[pl.ds(0, slots)], mine_out)
    outs.wait()


def place_kernel(cap, rows, experts, unused, idx_ref, mine_ref, other_ref, hs_ref, *rest):
    three_ref, theirs_ref, l0, r0 = rest[:4]
    refs, rest = rest[4 + unused : 8 + unused], rest[8 + unused :]
    bufs, (w_v, sent, place, gate_col, g_sem, w_sem, o_sem) = rest[:4], rest[4:]
    near_low, far_low, near_high, far_high = bufs
    wide, half = mine_ref.shape[1], near_low.shape[1]
    hp = three_ref.shape[3]
    slots = 4 * cap
    f32 = jnp.float32
    gates, copies = Copies(g_sem), Copies(w_sem)
    fetch_gates(gates, (l0, r0), rows, sent)
    for e, ref in enumerate((three_ref, theirs_ref)):
        copies.start(ref.at[:, 2], w_v.at[:, :, pl.ds(e * hp, hp)])
    r_io = lax.broadcasted_iota(jnp.int32, (rows, rows), 0)
    c_io = lax.broadcasted_iota(jnp.int32, (rows, rows), 1)
    eye = r_io == c_io
    numbers = lax.broadcasted_iota(jnp.int32, (rows, slots), 1)
    gates.wait()
    for e in range(2):
        g, slot = slots_of(sent, idx_ref, e, experts, cap, rows)
        for q in range(4):
            at = pl.ds(q * rows, rows)
            col = jnp.sum(jnp.where(eye, slot[q : q + 1, :], 0), axis=1, keepdims=True)
            place[e, at, :] = jnp.where(numbers == col, 1.0, 0.0).astype(jnp.bfloat16)
            gcol = jnp.sum(jnp.where(eye, g[q : q + 1, :], 0.0), axis=1, keepdims=True)
            gate_col[e, at, :] = jnp.broadcast_to(gcol, (rows, LANES))
    copies.wait()
    depth = w_v.shape[1]
    outs = Copies(o_sem)
    for n, step in steps(wide, min(256, half)):
        cols = pl.ds(n, step)
        if step % depth == 0:
            down = w_v[pl.ds(n // depth, step // depth)].reshape(step, 2 * hp)
        else:
            down = w_v[...].reshape(wide, 2 * hp)[n : n + step]
        total = lax.dot_general(
            hs_ref[...], down, (((1,), (1,)), ((), ())), preferred_element_type=f32
        )
        for e, ref in enumerate((mine_ref, other_ref)):
            y = jnp.dot(place[e], ref[:, cols], preferred_element_type=f32)
            total = total + gate_col[e][:, 0:1] * y
        if n < half:
            near, far, order, at = near_low, far_low, (0, 1, 2, 3), pl.ds(n, step)
        else:
            near, far, order, at = near_high, far_high, (0, 2, 1, 3), pl.ds(n - half, step)
        for a in range(2):
            to = pl.ds(a * rows, rows)
            q = order[a] * rows
            near[to, at] = total[q : q + rows]
            q = order[2 + a] * rows
            far[to, at] = total[q : q + rows].astype(far.dtype)
        if (n + step) % half == 0:
            k = 2 * (n // half)
            outs.start(bufs[k + 1], refs[k + 1])
            outs.start(bufs[k], refs[k])
    outs.wait()


def call(body, out_shape, in_specs, args, scratch, after=(), outs_in_vmem=True):
    vmem = pl.BlockSpec(memory_space=pltpu.VMEM)
    hbm = pl.BlockSpec(memory_space=pl.ANY)
    kinds = {"s": pl.BlockSpec(memory_space=pltpu.SMEM), "v": vmem, "h": hbm}
    return pl.pallas_call(
        body,
        out_shape=out_shape,
        in_specs=[kinds[k] for k in in_specs] + [hbm] * len(after),
        out_specs=tuple([vmem if outs_in_vmem else hbm] * len(out_shape)),
        scratch_shapes=scratch,
        compiler_params=pltpu.CompilerParams(vmem_limit_bytes=48 * 1024 * 1024),
        cost_estimate=pl.CostEstimate(flops=1, bytes_accessed=1, transcendentals=0),
    )(*args, *after)


def attention(context, out_proj, before, exchange):
    bf, f32 = jnp.bfloat16, jnp.float32
    me = lax.axis_index("expert")
    layers = lax.axis_size("expert") // LAYER
    odd = me % 2 == 1
    wide = context.shape[1]
    half = wide // 2

    def halves(lo, hi):
        return jnp.where(odd, hi, lo), jnp.where(odd, lo, hi)

    turned = out_proj.T
    mine, other = halves(turned[:, :half], turned[:, half:])
    pair = jnp.concatenate(halves(mine, swap(other, 1)), axis=0)
    mine, other = halves(context[:, :half], context[:, half:])
    got = swap(other, 1)
    cut = pair.shape[0]
    blocks = along_z(pair, layers)
    if layers > 1:
        blocks[1], before = lax.optimization_barrier((blocks[1], before))
    twos = [list(range(i, min(i + 2, layers))) for i in range(0, layers, 2)]
    firsts = [
        spread_first(jnp.concatenate([blocks[k] for k in two], axis=0), cut * len(two))
        for two in twos
    ]
    pieces, chips = [], []
    for two, first in zip(twos, firsts):
        pieces += spread_second(*first)
        for k in two:
            layer = jnp.bitwise_xor(me // LAYER, k)
            chips += [layer * (LAYER // 2) + jnp.bitwise_xor(me % LAYER // 2, q) for q in range(4)]
    exchange = lax.all_to_all(
        tie(exchange, *pieces), "expert", split_axis=0, concat_axis=0, tiled=True
    )
    here = context.shape[0]
    keep, send = call(
        functools.partial(attention_kernel, len(twos), cut),
        [jax.ShapeDtypeStruct((here, wide), f32)] * 2,
        "svv" + "h" * len(pieces),
        (jnp.stack(chips).astype(jnp.int32), mine, got, *pieces),
        [
            pltpu.VMEM((out_proj.shape[1] * lax.axis_size("expert"), half), bf),
            pltpu.SemaphoreType.DMA((8 * layers,)),
        ],
    )
    return keep + swap(send, 1), before, exchange


def whole_rows(
    hidden_state,
    context,
    out_proj,
    norm_gain,
    router_weight,
    expert_in,
    expert_out,
    shared_in,
    shared_out,
    route_ids,
):
    bf, f32 = jnp.bfloat16, jnp.float32
    n = lax.axis_size("expert")
    layers = n // LAYER
    me = lax.axis_index("expert")
    odd = me % 2
    rows, top = route_ids.shape
    experts = router_weight.shape[1]
    wide = out_proj.shape[0]
    half = wide // 2
    cap = capacity_of(rows, top, experts)
    pack = 16
    win = expert_in[0].reshape(wide // pack, pack, 2, -1).transpose(0, 2, 1, 3)
    wout = expert_out[0]
    hidden = wout.shape[0]
    tile = LANES if hidden % LANES == 0 else hidden

    own = shared_in.shape[2] // n
    depth = shared_in.shape[0]
    hp = -(-own // LANES) * LANES
    three = jnp.concatenate([shared_in.transpose(1, 0, 2), shared_out.T[None]], axis=0)
    three = three.reshape(3, depth, n, own)
    three = jnp.pad(three, ((0, 0), (0, 0), (0, 0), (0, hp - own))).transpose(2, 0, 1, 3)

    attn, win, three = attention(context, out_proj, win, three)
    theirs = swap(three, 1)
    mixed = hidden_state.astype(f32) + attn
    inverse = lax.rsqrt(jnp.mean(mixed * mixed, axis=1, keepdims=True) + 1e-06)
    normed32 = mixed * inverse * norm_gain.astype(f32)
    normed = normed32.astype(bf)
    logits = jnp.dot(normed32, router_weight, precision=lax.Precision.HIGHEST)
    named = jnp.any(
        route_ids[:, :, None] == jnp.arange(experts, dtype=jnp.int32)[None, None, :], axis=1
    )
    highest = jnp.max(jnp.where(named, logits, -jnp.inf), axis=1, keepdims=True)
    raised = jnp.where(named, jnp.exp(logits - highest), 0.0)
    gates = raised / jnp.sum(raised, axis=1, keepdims=True)

    rest, parts = gates.T, []
    for _ in range(3):
        parts.append(lax.reduce_precision(rest, 8, 7))
        rest = rest - parts[-1]
    below = jnp.stack(parts).astype(bf).reshape(-1, half)
    extra = -(-below.shape[0] // 16) * 16
    below = jnp.pad(below, ((0, extra - below.shape[0]), (0, half)))
    blocks = along_z(jnp.concatenate([normed, below], axis=0), layers)

    each = half // rows
    chip_experts = (me, jnp.bitwise_xor(me, 1))
    idx = jnp.stack([v for e in chip_experts for v in (e // each, e % each)]).astype(jnp.int32)
    slots, span = 4 * cap, 4 * rows
    sds, dma = jax.ShapeDtypeStruct, pltpu.SemaphoreType.DMA
    xs = pltpu.VMEM((span, wide), bf)
    sent = pltpu.VMEM((4, extra, half), bf)

    def add_first(near_low, far_low, near_high, far_high):
        low = near_low + swap(far_low, 4).astype(f32)
        high = near_high + swap(far_high, 2).astype(f32)
        return low[:rows], low[rows:].astype(bf), high[:rows], high[rows:].astype(bf)

    def pick(pieces, after):
        return call(
            functools.partial(pick_kernel, cap, rows, experts, len(after)),
            [sds((slots, wide), bf)] * 2,
            "shhhh",
            (idx, *pieces),
            [
                xs,
                sent,
                pltpu.VMEM((2 * slots, span), bf),
                pltpu.VMEM((2 * slots, wide), bf),
                dma((8,)),
                dma((4,)),
                dma((2,)),
            ],
            after,
            False,
        )

    def shared(pieces, after):
        return call(
            functools.partial(shared_kernel, rows, len(after)),
            [sds((span, 2 * hp), bf)],
            "hhhhhh",
            (three, theirs, *pieces),
            [xs, pltpu.VMEM((n, depth, 4 * hp), bf), dma((12,))],
            after,
        )[0]

    def expert(picked, borrowed, after):
        return call(
            functools.partial(expert_kernel, len(after)),
            [sds((slots, wide), bf)] * 2,
            "hhhh",
            (picked, borrowed, win, wout),
            [
                pltpu.VMEM((2 * slots, wide), bf),
                pltpu.VMEM((hidden // tile, wide // pack, pack, 2 * tile), bf),
                pltpu.VMEM((hidden, wide), bf),
                pltpu.VMEM((2 * slots, hidden), bf),
                pltpu.VMEM((2 * slots, wide), bf),
                dma((2,)),
                dma((2 * (hidden // tile) + 1,)),
                dma((2,)),
            ],
            after,
            False,
        )

    def place(done, returned, hs, pieces, after):
        return call(
            functools.partial(place_kernel, cap, rows, experts, len(after)),
            [sds((2 * rows, half), t) for t in (f32, bf, f32, bf)],
            "svvvhhhh",
            (idx, done, returned, hs, three, theirs, pieces[0], pieces[1]),
            [pltpu.VMEM((2 * rows, half), t) for t in (f32, bf, f32, bf)]
            + [
                pltpu.VMEM((n, depth, 2 * hp), bf),
                sent,
                pltpu.VMEM((2, span, slots), bf),
                pltpu.VMEM((2, span, LANES), f32),
                dma((4,)),
                dma((2,)),
                dma((4,)),
            ],
            after,
            False,
        )

    order = [0] + list(range(2, layers)) + [1] * (layers > 1)
    firsts, placed, once = {}, [], []

    def first(k, *others):
        if k not in firsts:
            firsts[k] = spread_first(tie(blocks[k], *others), rows)
        return firsts[k]

    pieces = spread_second(*first(0))
    picked, lent = pick(pieces, [])
    hs = None
    for at, k in enumerate(order):
        more = at + 1 < layers
        after = [hs] if at else []
        if more:
            after += first(order[at + 1], *([done] if at else []))
        done, back = expert(picked, swap(lent, 1), after)
        if not at:
            hs = shared(pieces, [done])
        now, after = (hs, pieces), []
        if more:
            pieces = spread_second(*first(order[at + 1]))
            back = tie(back, pieces[1], pieces[3])
            picked, lent = pick(pieces, [done])
            after = [lent]
        if at:
            once.append(add_first(*placed[-1]))
            after += [once[-1][1], once[-1][3]]
        placed.append(place(done, swap(back, 1), *now, after))
        if more:
            hs = shared(pieces, [placed[-1][1]])
    once.append(add_first(*placed[-1]))
    sums = {}
    for k, (low, far_low, high, far_high) in zip(order, once):
        low = low + swap(far_low, 2).astype(f32)
        high = high + swap(far_high, 4).astype(f32)
        sums[k] = jnp.concatenate([low, high], axis=1)
    for k in reversed(range(1, layers)):
        low = k & -k
        sums[k - low] = sums[k - low] + swap(sums[k].astype(bf), LAYER * low).astype(f32)
    return mixed + sums[0]


def solution(mesh):
    n, mp = mesh.shape["expert"], mesh.shape["mp"]
    fits = mp == 1 and n % LAYER == 0 and (n // LAYER) & (n // LAYER - 1) == 0
    per_device = whole_rows if fits else general
    return jax.shard_map(
        per_device,
        mesh=mesh,
        in_specs=(
            P("expert", "mp"),
            P("expert", "mp"),
            P("mp", "expert"),
            P("mp"),
            P("mp", None),
            P("expert", None, None, "mp"),
            P("expert", "mp", None),
            P("expert", None, "mp"),
            P("mp", "expert"),
            P("expert", None),
        ),
        out_specs=P("expert", "mp"),
        check_vma=False,
    )
```

```python
import functools

import jax
import jax.numpy as jnp
from jax import lax
from jax.experimental import pallas as pl
from jax.experimental.pallas import tpu as pltpu
from jax.sharding import PartitionSpec as P

LANES = 128
LAYER = 8


def capacity_of(rows, top, experts):
    return max(2, min(rows, rows * top // experts * 5 // 3))


def general(
    hidden_state,
    context,
    out_proj,
    norm_gain,
    router_weight,
    expert_in,
    expert_out,
    shared_in,
    shared_out,
    route_ids,
):
    rows_here, top = route_ids.shape
    experts = router_weight.shape[1]
    width = out_proj.shape[0] * lax.axis_size("mp")
    capacity = capacity_of(rows_here, top, experts)
    partial_attn = jnp.dot(
        context,
        lax.all_gather(out_proj, "expert", axis=1, tiled=True),
        preferred_element_type=jnp.float32,
    )
    attn = lax.psum_scatter(partial_attn, "mp", scatter_dimension=1, tiled=True)
    mixed = hidden_state.astype(jnp.float32) + attn
    gain = norm_gain.astype(jnp.float32)
    squares = lax.psum(jnp.sum(mixed * mixed, axis=1), "mp")
    inverse = lax.rsqrt(squares / width + 1e-06)[:, None]
    normed32 = mixed * inverse * gain
    logits = lax.psum(jnp.dot(normed32, router_weight, precision=lax.Precision.HIGHEST), "mp")
    normed = normed32.astype(jnp.bfloat16)
    gates = jax.nn.softmax(jnp.take_along_axis(logits, route_ids, axis=1), axis=1)
    full_rows = lax.all_gather(normed, "mp", axis=1, tiled=True)
    shared_width = shared_in.shape[2]
    piece = lax.all_gather(shared_in, "expert", axis=0, tiled=True)
    shared_both = jnp.dot(
        full_rows,
        piece.reshape(piece.shape[0], 2 * shared_width),
        preferred_element_type=jnp.float32,
    )
    shared_both = shared_both.reshape(rows_here, 2, shared_width)
    shared_hidden = (jax.nn.silu(shared_both[:, 0]) * shared_both[:, 1]).astype(jnp.bfloat16)
    shared_part = jnp.dot(
        shared_hidden,
        lax.all_gather(shared_out, "expert", axis=1, tiled=True),
        preferred_element_type=jnp.float32,
    )
    flat = route_ids.reshape(-1)
    onehot = (flat[:, None] == jnp.arange(experts, dtype=jnp.int32)[None, :]).astype(jnp.int32)
    position = jnp.sum(onehot * jnp.cumsum(onehot, axis=0), axis=1) - 1
    slot_of = flat * capacity + position
    source = (
        jnp.zeros((experts * capacity,), jnp.int32)
        .at[slot_of]
        .set(jnp.arange(flat.shape[0], dtype=jnp.int32) // top)
    )
    filled = jnp.zeros((experts * capacity,), jnp.bool_).at[slot_of].set(True)
    outgoing = jnp.where(filled[:, None], normed[source], jnp.zeros((), jnp.bfloat16)).reshape(
        experts, capacity, normed.shape[1]
    )
    quarter = expert_in.shape[3]
    weights_in = expert_in[0].reshape(width, 2 * quarter)
    incoming = lax.all_to_all(outgoing, "expert", split_axis=0, concat_axis=0, tiled=True)
    sources = incoming.shape[0]
    items = incoming.shape[1]
    gathered = lax.all_gather(incoming, "mp", axis=2, tiled=True).reshape(sources * items, width)
    inner = jnp.dot(gathered, weights_in, preferred_element_type=jnp.float32).reshape(
        -1, 2, quarter
    )
    hidden = (jax.nn.silu(inner[:, 0]) * inner[:, 1]).astype(jnp.bfloat16)
    partial_out = jnp.dot(hidden, expert_out[0], preferred_element_type=jnp.float32).astype(
        jnp.bfloat16
    )
    partial_out = partial_out.reshape(sources, items, width)
    result = lax.all_to_all(partial_out, "expert", split_axis=0, concat_axis=0, tiled=True)
    picked = result.reshape(experts * capacity, result.shape[2])[slot_of]
    slot_total = lax.psum_scatter(
        lax.optimization_barrier(picked).astype(jnp.float32).astype(jnp.bfloat16),
        "mp",
        scatter_dimension=1,
        tiled=True,
    )
    expert_sum = lax.optimization_barrier(slot_total).astype(jnp.float32)
    expert_sum = expert_sum.reshape(rows_here, top, expert_sum.shape[1])
    routed = jnp.sum(gates[:, :, None] * expert_sum, axis=1)
    shared = lax.psum_scatter(shared_part, "mp", scatter_dimension=1, tiled=True)
    return mixed + routed + shared


def swap(x, bit):
    n = lax.axis_size("expert")
    return lax.ppermute(x, "expert", [(i, i ^ bit) for i in range(n)])


def silu(v):
    return v / (1.0 + jnp.exp(-v))


def spread_first(h0, h1):
    return jnp.concatenate([h0, swap(h0, 2)], axis=0), jnp.concatenate([h1, swap(h1, 4)], axis=0)


def spread_second(l0, l1):
    return l0, swap(l0, 4), l1, swap(l1, 2)


def along_z(block, layers):
    blocks = [block]
    for k in range(1, layers):
        low = k & -k
        blocks.append(swap(blocks[k - low], LAYER * low))
    return blocks


def tie(x, *others):
    return lax.optimization_barrier((x, *others))[0]


class Copies:
    def __init__(self, sems):
        self.sems, self.all = sems, []

    def start(self, src, dst):
        c = pltpu.make_async_copy(src, dst, self.sems.at[len(self.all)])
        c.start()
        self.all.append(c)

    def wait(self):
        for c in self.all:
            c.wait()


PIECES = ((0, 0, (0, 1)), (1, 0, (2, 3)), (2, 1, (0, 2)), (3, 1, (1, 3)))


def fetch_rows(copies, pieces, rows, xs):
    half = xs.shape[1] // 2
    for n, h, chips in PIECES:
        stride = pieces[n].shape[0] // 2
        for a, q in enumerate(chips):
            copies.start(
                pieces[n].at[pl.ds(a * stride, rows)],
                xs.at[pl.ds(q * rows, rows), pl.ds(h * half, half)],
            )


def fetch_gates(copies, left, rows, to):
    for piece, (_, _, chips) in zip(left, PIECES):
        stride = piece.shape[0] // 2
        for a, q in enumerate(chips):
            copies.start(piece.at[pl.ds(a * stride + rows, stride - rows)], to.at[q])


def slots_of(sent, idx_ref, expert, experts, cap, rows):
    extra, half = sent.shape[1:]
    each = half // rows
    tall = experts // each
    line, column = idx_ref[2 * expert], idx_ref[2 * expert + 1]
    r = lax.broadcasted_iota(jnp.int32, (extra, half), 0)
    wanted = (r == line) | (r == line + tall) | (r == line + 2 * tall)
    found = []
    for q in range(4):
        parts = jnp.where(wanted, sent[q].astype(jnp.float32), 0.0)
        parts = jnp.sum(parts, axis=0, keepdims=True)
        g = jnp.zeros((1, rows), jnp.float32)
        for j in range(each):
            g = jnp.where(column == j, parts[:, j * rows : (j + 1) * rows], g)
        found.append(g)
    g = jnp.concatenate(found, axis=0)
    chosen = g > 0.0
    r_io = lax.broadcasted_iota(jnp.int32, (rows, rows), 0)
    c_io = lax.broadcasted_iota(jnp.int32, (rows, rows), 1)
    upto = jnp.where(r_io <= c_io, 1.0, 0.0).astype(jnp.bfloat16)
    count = jnp.dot(
        jnp.where(chosen, 1.0, 0.0).astype(jnp.bfloat16), upto, preferred_element_type=jnp.float32
    ).astype(jnp.int32)
    first = lax.broadcasted_iota(jnp.int32, (4, rows), 0) * cap
    return g, jnp.where(chosen, first + count - 1, -1)


def steps(total, most):
    step = min(most, total)
    return [(n, step) for n in range(0, total, step)]


def attention_kernel(groups, rows, idx_ref, mine_ref, other_ref, *rest):
    pieces, (keep_ref, send_ref, w_v, sems) = rest[: 4 * groups], rest[4 * groups :]
    half = w_v.shape[1] // 2
    count = pieces[0].shape[0] // (2 * rows)
    copies = Copies(sems)
    for g in range(groups):
        l0, r0, l1, r1 = pieces[4 * g : 4 * g + 4]
        for h, (near, far, first, second) in enumerate(((l0, r0, 1, 2), (l1, r1, 2, 1))):
            for piece, base in ((near, 0), (far, second)):
                for a, q in enumerate((base, base + first)):
                    for i in range(count):
                        chip = idx_ref[(g * count + i) * 4 + q]
                        to = pl.ds(pl.multiple_of(chip * rows, rows), rows)
                        copies.start(
                            piece.at[pl.ds((a * count + i) * rows, rows)],
                            w_v.at[to, pl.ds(h * half, half)],
                        )
    copies.wait()
    both = jnp.concatenate([mine_ref[...], other_ref[...]], axis=0)
    here = mine_ref.shape[0]
    for n, step in steps(w_v.shape[0], 512):
        part = lax.dot_general(
            both,
            w_v[pl.ds(n, step), :],
            (((1,), (1,)), ((), ())),
            preferred_element_type=jnp.float32,
        )
        keep_ref[:, pl.ds(n, step)] = part[:here]
        send_ref[:, pl.ds(n, step)] = part[here:]


def pick_kernel(cap, rows, experts, unused, idx_ref, *rest):
    pieces = rest[:4]
    mine_ref, other_ref, xs, sent, pick, out_v, x_sem, g_sem, o_sem = rest[4 + unused :]
    gates, copies = Copies(g_sem), Copies(x_sem)
    fetch_gates(gates, pieces[:2], rows, sent)
    fetch_rows(copies, pieces, rows, xs)
    slots = 4 * cap
    numbers = lax.broadcasted_iota(jnp.int32, (slots, rows), 0)
    gates.wait()
    for e in range(2):
        _, slot = slots_of(sent, idx_ref, e, experts, cap, rows)
        for q in range(4):
            pick[pl.ds(e * slots, slots), pl.ds(q * rows, rows)] = jnp.where(
                numbers == slot[q : q + 1, :], 1.0, 0.0
            ).astype(jnp.bfloat16)
    copies.wait()
    for n, step in steps(xs.shape[1], 512):
        out_v[:, pl.ds(n, step)] = jnp.dot(
            pick[...], xs[:, pl.ds(n, step)], preferred_element_type=jnp.float32
        ).astype(jnp.bfloat16)
    outs = Copies(o_sem)
    outs.start(out_v.at[pl.ds(slots, slots)], other_ref)
    outs.start(out_v.at[pl.ds(0, slots)], mine_ref)
    outs.wait()


def shared_kernel(rows, unused, three_ref, theirs_ref, *rest):
    pieces, (hs_ref, xs, w_v, x_sem) = rest[:4], rest[4 + unused :]
    hp = three_ref.shape[3]
    copies = Copies(x_sem)
    fetch_rows(copies, pieces, rows, xs)
    for e, ref in enumerate((three_ref, theirs_ref)):
        for h in range(2):
            copies.start(ref.at[:, h], w_v.at[:, :, pl.ds((2 * h + e) * hp, hp)])
    copies.wait()
    w = w_v[...].reshape(xs.shape[1], 4 * hp)
    for m, step in steps(4 * rows, 2 * rows):
        both = jnp.dot(xs[pl.ds(m, step), :], w, preferred_element_type=jnp.float32)
        hs_ref[pl.ds(m, step), :] = (silu(both[:, : 2 * hp]) * both[:, 2 * hp :]).astype(
            jnp.bfloat16
        )


def expert_kernel(unused, mine_ref, other_ref, win_ref, wout_ref, *rest):
    mine_out, other_out, x_v, win_v, wout_v, hid_v, y_v, x_sem, w_sem, o_sem = rest[unused:]
    slots, wide = mine_ref.shape
    tiles, tile = win_v.shape[0], win_v.shape[3] // 2
    rows = Copies(x_sem)
    rows.start(mine_ref, x_v.at[pl.ds(0, slots)])
    rows.start(other_ref, x_v.at[pl.ds(slots, slots)])
    copies = Copies(w_sem)
    for t in range(tiles):
        for h in range(2):
            copies.start(
                win_ref.at[:, h, :, pl.ds(t * tile, tile)],
                win_v.at[t, :, :, pl.ds(h * tile, tile)],
            )
    copies.start(wout_ref, wout_v)
    rows.wait()
    here = 0
    for t in range(tiles):
        if t == here:
            here = min(2 * here + 1, tiles)
            for c in copies.all[2 * t : 2 * here]:
                c.wait()
        both = jnp.dot(
            x_v[...], win_v[t].reshape(wide, 2 * tile), preferred_element_type=jnp.float32
        )
        hid_v[:, pl.ds(t * tile, tile)] = (silu(both[:, :tile]) * both[:, tile:]).astype(
            jnp.bfloat16
        )
    copies.all[2 * tiles].wait()
    outs = Copies(o_sem)
    for n, step in steps(wide, 512):
        y_v[:, pl.ds(n, step)] = jnp.dot(
            hid_v[...], wout_v[:, pl.ds(n, step)], preferred_element_type=jnp.float32
        ).astype(jnp.bfloat16)
    outs.start(y_v.at[pl.ds(slots, slots)], other_out)
    outs.start(y_v.at[pl.ds(0, slots)], mine_out)
    outs.wait()


def place_kernel(cap, rows, experts, unused, idx_ref, mine_ref, other_ref, hs_ref, *rest):
    three_ref, theirs_ref, l0, r0 = rest[:4]
    refs, rest = rest[4 + unused : 8 + unused], rest[8 + unused :]
    bufs, (w_v, sent, place, gate_col, g_sem, w_sem, o_sem) = rest[:4], rest[4:]
    near_low, far_low, near_high, far_high = bufs
    wide, half = mine_ref.shape[1], near_low.shape[1]
    hp = three_ref.shape[3]
    slots = 4 * cap
    f32 = jnp.float32
    gates, copies = Copies(g_sem), Copies(w_sem)
    fetch_gates(gates, (l0, r0), rows, sent)
    for e, ref in enumerate((three_ref, theirs_ref)):
        copies.start(ref.at[:, 2], w_v.at[:, :, pl.ds(e * hp, hp)])
    r_io = lax.broadcasted_iota(jnp.int32, (rows, rows), 0)
    c_io = lax.broadcasted_iota(jnp.int32, (rows, rows), 1)
    eye = r_io == c_io
    numbers = lax.broadcasted_iota(jnp.int32, (rows, slots), 1)
    gates.wait()
    for e in range(2):
        g, slot = slots_of(sent, idx_ref, e, experts, cap, rows)
        for q in range(4):
            at = pl.ds(q * rows, rows)
            col = jnp.sum(jnp.where(eye, slot[q : q + 1, :], 0), axis=1, keepdims=True)
            place[e, at, :] = jnp.where(numbers == col, 1.0, 0.0).astype(jnp.bfloat16)
            gcol = jnp.sum(jnp.where(eye, g[q : q + 1, :], 0.0), axis=1, keepdims=True)
            gate_col[e, at, :] = jnp.broadcast_to(gcol, (rows, LANES))
    copies.wait()
    depth = w_v.shape[1]
    outs = Copies(o_sem)
    for n, step in steps(wide, min(256, half)):
        cols = pl.ds(n, step)
        if step % depth == 0:
            down = w_v[pl.ds(n // depth, step // depth)].reshape(step, 2 * hp)
        else:
            down = w_v[...].reshape(wide, 2 * hp)[n : n + step]
        total = lax.dot_general(
            hs_ref[...], down, (((1,), (1,)), ((), ())), preferred_element_type=f32
        )
        for e, ref in enumerate((mine_ref, other_ref)):
            y = jnp.dot(place[e], ref[:, cols], preferred_element_type=f32)
            total = total + gate_col[e][:, 0:1] * y
        if n < half:
            near, far, order, at = near_low, far_low, (0, 1, 2, 3), pl.ds(n, step)
        else:
            near, far, order, at = near_high, far_high, (0, 2, 1, 3), pl.ds(n - half, step)
        for a in range(2):
            to = pl.ds(a * rows, rows)
            q = order[a] * rows
            near[to, at] = total[q : q + rows]
            q = order[2 + a] * rows
            far[to, at] = total[q : q + rows].astype(far.dtype)
        if (n + step) % half == 0:
            k = 2 * (n // half)
            outs.start(bufs[k + 1], refs[k + 1])
            outs.start(bufs[k], refs[k])
    outs.wait()


def call(body, out_shape, in_specs, args, scratch, after=(), outs_in_vmem=True):
    vmem = pl.BlockSpec(memory_space=pltpu.VMEM)
    hbm = pl.BlockSpec(memory_space=pl.ANY)
    kinds = {"s": pl.BlockSpec(memory_space=pltpu.SMEM), "v": vmem, "h": hbm}
    return pl.pallas_call(
        body,
        out_shape=out_shape,
        in_specs=[kinds[k] for k in in_specs] + [hbm] * len(after),
        out_specs=tuple([vmem if outs_in_vmem else hbm] * len(out_shape)),
        scratch_shapes=scratch,
        compiler_params=pltpu.CompilerParams(vmem_limit_bytes=48 * 1024 * 1024),
        cost_estimate=pl.CostEstimate(flops=1, bytes_accessed=1, transcendentals=0),
    )(*args, *after)


def attention(context, out_proj, before, exchange):
    bf, f32 = jnp.bfloat16, jnp.float32
    me = lax.axis_index("expert")
    layers = lax.axis_size("expert") // LAYER
    odd = me % 2 == 1
    wide = context.shape[1]
    half = wide // 2

    def halves(lo, hi):
        return jnp.where(odd, hi, lo), jnp.where(odd, lo, hi)

    turned = out_proj.T
    mine, other = halves(turned[:, :half], turned[:, half:])
    pair = jnp.concatenate(halves(mine, swap(other, 1)), axis=0)
    mine, other = halves(context[:, :half], context[:, half:])
    got = swap(other, 1)
    cut = pair.shape[0]
    blocks = along_z(pair, layers)
    if layers > 1:
        blocks[1], exchange = lax.optimization_barrier((blocks[1], exchange))
    twos = [list(range(i, min(i + 2, layers))) for i in range(0, layers, 2)]
    stacks = [jnp.concatenate([blocks[k] for k in two], axis=0) for two in twos]
    quarter = half // 2
    firsts = [spread_first(stack[:, :quarter], stack[:, quarter:]) for stack in stacks]
    pieces, chips = [], []
    for two, first in zip(twos, firsts):
        pieces += spread_second(*first)
        for k in two:
            layer = jnp.bitwise_xor(me // LAYER, k)
            chips += [layer * (LAYER // 2) + jnp.bitwise_xor(me % LAYER // 2, q) for q in range(4)]
    mine, before = lax.optimization_barrier((mine, before))
    exchange = lax.all_to_all(
        tie(exchange, *pieces), "expert", split_axis=0, concat_axis=0, tiled=True
    )
    here = context.shape[0]
    keep, send = call(
        functools.partial(attention_kernel, len(twos), cut),
        [jax.ShapeDtypeStruct((here, wide), f32)] * 2,
        "svv" + "h" * len(pieces),
        (jnp.stack(chips).astype(jnp.int32), mine, got, *pieces),
        [
            pltpu.VMEM((out_proj.shape[1] * lax.axis_size("expert"), half), bf),
            pltpu.SemaphoreType.DMA((8 * layers,)),
        ],
    )
    return keep + swap(send, 1), before, exchange


def whole_rows(
    hidden_state,
    context,
    out_proj,
    norm_gain,
    router_weight,
    expert_in,
    expert_out,
    shared_in,
    shared_out,
    route_ids,
):
    bf, f32 = jnp.bfloat16, jnp.float32
    n = lax.axis_size("expert")
    layers = n // LAYER
    me = lax.axis_index("expert")
    odd = me % 2
    rows, top = route_ids.shape
    experts = router_weight.shape[1]
    wide = out_proj.shape[0]
    half = wide // 2
    cap = capacity_of(rows, top, experts)
    pack = 16
    win = expert_in[0].reshape(wide // pack, pack, 2, -1).transpose(0, 2, 1, 3)
    wout = expert_out[0]
    hidden = wout.shape[0]
    tile = LANES if hidden % LANES == 0 else hidden

    own = shared_in.shape[2] // n
    depth = shared_in.shape[0]
    hp = -(-own // LANES) * LANES
    three = jnp.concatenate([shared_in.transpose(1, 0, 2), shared_out.T[None]], axis=0)
    three = three.reshape(3, depth, n, own)
    three = jnp.pad(three, ((0, 0), (0, 0), (0, 0), (0, hp - own))).transpose(2, 0, 1, 3)

    attn, win, three = attention(context, out_proj, win, three)
    mixed = hidden_state.astype(f32) + attn
    inverse = lax.rsqrt(jnp.mean(mixed * mixed, axis=1, keepdims=True) + 1e-06)
    normed32 = mixed * inverse * norm_gain.astype(f32)
    normed = normed32.astype(bf)
    logits = jnp.dot(normed32, router_weight, precision=lax.Precision.HIGHEST)
    named = jnp.any(
        route_ids[:, :, None] == jnp.arange(experts, dtype=jnp.int32)[None, None, :], axis=1
    )
    highest = jnp.max(jnp.where(named, logits, -jnp.inf), axis=1, keepdims=True)
    raised = jnp.where(named, jnp.exp(logits - highest), 0.0)
    gates = raised / jnp.sum(raised, axis=1, keepdims=True)

    rest, parts = gates.T, []
    for _ in range(3):
        parts.append(lax.reduce_precision(rest, 8, 7))
        rest = rest - parts[-1]
    below = jnp.stack(parts).astype(bf).reshape(-1, half)
    extra = -(-below.shape[0] // 16) * 16
    below = jnp.pad(below, ((0, extra - below.shape[0]), (0, 0)))
    left = along_z(jnp.concatenate([normed[:, :half], below], axis=0), layers)
    right = along_z(normed[:, half:], layers)

    each = half // rows
    chip_experts = (me, jnp.bitwise_xor(me, 1))
    idx = jnp.stack([v for e in chip_experts for v in (e // each, e % each)]).astype(jnp.int32)
    slots, span = 4 * cap, 4 * rows
    sds, dma = jax.ShapeDtypeStruct, pltpu.SemaphoreType.DMA
    xs = pltpu.VMEM((span, wide), bf)
    sent = pltpu.VMEM((4, extra, half), bf)

    def add_first(near_low, far_low, near_high, far_high):
        low = near_low + swap(far_low, 4).astype(f32)
        high = near_high + swap(far_high, 2).astype(f32)
        return low[:rows], low[rows:].astype(bf), high[:rows], high[rows:].astype(bf)

    def pick(pieces, after):
        return call(
            functools.partial(pick_kernel, cap, rows, experts, len(after)),
            [sds((slots, wide), bf)] * 2,
            "shhhh",
            (idx, *pieces),
            [
                xs,
                sent,
                pltpu.VMEM((2 * slots, span), bf),
                pltpu.VMEM((2 * slots, wide), bf),
                dma((8,)),
                dma((4,)),
                dma((2,)),
            ],
            after,
            False,
        )

    def shared(pieces, after):
        return call(
            functools.partial(shared_kernel, rows, len(after)),
            [sds((span, 2 * hp), bf)],
            "hhhhhh",
            (three, theirs, *pieces),
            [xs, pltpu.VMEM((n, depth, 4 * hp), bf), dma((12,))],
            after,
        )[0]

    def expert(picked, borrowed, after):
        return call(
            functools.partial(expert_kernel, len(after)),
            [sds((slots, wide), bf)] * 2,
            "hhhh",
            (picked, borrowed, win, wout),
            [
                pltpu.VMEM((2 * slots, wide), bf),
                pltpu.VMEM((hidden // tile, wide // pack, pack, 2 * tile), bf),
                pltpu.VMEM((hidden, wide), bf),
                pltpu.VMEM((2 * slots, hidden), bf),
                pltpu.VMEM((2 * slots, wide), bf),
                dma((2,)),
                dma((2 * (hidden // tile) + 1,)),
                dma((2,)),
            ],
            after,
            False,
        )

    def place(done, returned, hs, pieces, after):
        return call(
            functools.partial(place_kernel, cap, rows, experts, len(after)),
            [sds((2 * rows, half), t) for t in (f32, bf, f32, bf)],
            "svvvhhhh",
            (idx, done, returned, hs, three, theirs, pieces[0], pieces[1]),
            [pltpu.VMEM((2 * rows, half), t) for t in (f32, bf, f32, bf)]
            + [
                pltpu.VMEM((n, depth, 2 * hp), bf),
                sent,
                pltpu.VMEM((2, span, slots), bf),
                pltpu.VMEM((2, span, LANES), f32),
                dma((4,)),
                dma((2,)),
                dma((4,)),
            ],
            after,
            False,
        )

    order = [0] + list(reversed(range(1, layers)))
    placed, once = [], []

    def first(k, *others):
        if not others:
            return spread_first(left[k], right[k])
        return spread_first(tie(left[k], *others), tie(right[k], *others))

    pieces = spread_second(*first(0))
    picked, lent = pick(pieces, [])
    far = [*left[2:3], *right[2:3]]
    done, back = expert(picked, swap(lent, 1), far)
    back = tie(back, *left[3:], *right[3:])
    theirs = swap(tie(three, done, *left[3:], *right[3:]), 1)
    hs = shared(pieces, [done])
    ahead = first(order[1], done) if layers > 1 else []
    placed.append(place(done, swap(back, 1), hs, pieces, [*ahead]))
    for at in range(1, layers):
        if at == 1:
            pieces = spread_second(*ahead)
            picked, lent = pick(pieces, [placed[-1][1]])
            hs = shared(pieces, [lent])
        more = at + 1 < layers
        after = [hs]
        if more:
            ahead = first(order[at + 1], *ahead)
            after += ahead
        done, back = expert(picked, swap(lent, 1), after)
        now, after = (hs, pieces), []
        if more:
            pieces = spread_second(*ahead)
            back = tie(back, pieces[1], pieces[3])
            picked, lent = pick(pieces, [done])
            after = [lent]
        once.append(add_first(*placed[-1]))
        after += [once[-1][1], once[-1][3]]
        placed.append(place(done, swap(back, 1), *now, after))
        if more:
            hs = shared(pieces, [placed[-1][1]])
    once.append(add_first(*placed[-1]))
    sums = {}
    for k, (low, far_low, high, far_high) in zip(order, once):
        low = low + swap(far_low, 2).astype(f32)
        high = high + swap(far_high, 4).astype(f32)
        sums[k] = jnp.concatenate([low, high], axis=1)
    for k in reversed(range(1, layers)):
        low = k & -k
        sums[k - low] = sums[k - low] + swap(sums[k].astype(bf), LAYER * low).astype(f32)
    return mixed + sums[0]


def solution(mesh):
    n, mp = mesh.shape["expert"], mesh.shape["mp"]
    fits = mp == 1 and n % LAYER == 0 and (n // LAYER) & (n // LAYER - 1) == 0
    per_device = whole_rows if fits else general
    return jax.shard_map(
        per_device,
        mesh=mesh,
        in_specs=(
            P("expert", "mp"),
            P("expert", "mp"),
            P("mp", "expert"),
            P("mp"),
            P("mp", None),
            P("expert", None, None, "mp"),
            P("expert", "mp", None),
            P("expert", None, "mp"),
            P("mp", "expert"),
            P("expert", None),
        ),
        out_specs=P("expert", "mp"),
        check_vma=False,
    )
```

```python
import functools

import jax
import jax.numpy as jnp
from jax import lax
from jax.experimental import pallas as pl
from jax.experimental.pallas import tpu as pltpu
from jax.sharding import PartitionSpec as P

LANES = 128
LAYER = 8


def capacity_of(rows, top, experts):
    return max(2, min(rows, rows * top // experts * 5 // 3))


def general(
    hidden_state,
    context,
    out_proj,
    norm_gain,
    router_weight,
    expert_in,
    expert_out,
    shared_in,
    shared_out,
    route_ids,
):
    rows_here, top = route_ids.shape
    experts = router_weight.shape[1]
    width = out_proj.shape[0] * lax.axis_size("mp")
    capacity = capacity_of(rows_here, top, experts)
    partial_attn = jnp.dot(
        context,
        lax.all_gather(out_proj, "expert", axis=1, tiled=True),
        preferred_element_type=jnp.float32,
    )
    attn = lax.psum_scatter(partial_attn, "mp", scatter_dimension=1, tiled=True)
    mixed = hidden_state.astype(jnp.float32) + attn
    gain = norm_gain.astype(jnp.float32)
    squares = lax.psum(jnp.sum(mixed * mixed, axis=1), "mp")
    inverse = lax.rsqrt(squares / width + 1e-06)[:, None]
    normed32 = mixed * inverse * gain
    logits = lax.psum(jnp.dot(normed32, router_weight, precision=lax.Precision.HIGHEST), "mp")
    normed = normed32.astype(jnp.bfloat16)
    gates = jax.nn.softmax(jnp.take_along_axis(logits, route_ids, axis=1), axis=1)
    full_rows = lax.all_gather(normed, "mp", axis=1, tiled=True)
    shared_width = shared_in.shape[2]
    piece = lax.all_gather(shared_in, "expert", axis=0, tiled=True)
    shared_both = jnp.dot(
        full_rows,
        piece.reshape(piece.shape[0], 2 * shared_width),
        preferred_element_type=jnp.float32,
    )
    shared_both = shared_both.reshape(rows_here, 2, shared_width)
    shared_hidden = (jax.nn.silu(shared_both[:, 0]) * shared_both[:, 1]).astype(jnp.bfloat16)
    shared_part = jnp.dot(
        shared_hidden,
        lax.all_gather(shared_out, "expert", axis=1, tiled=True),
        preferred_element_type=jnp.float32,
    )
    flat = route_ids.reshape(-1)
    onehot = (flat[:, None] == jnp.arange(experts, dtype=jnp.int32)[None, :]).astype(jnp.int32)
    position = jnp.sum(onehot * jnp.cumsum(onehot, axis=0), axis=1) - 1
    slot_of = flat * capacity + position
    source = (
        jnp.zeros((experts * capacity,), jnp.int32)
        .at[slot_of]
        .set(jnp.arange(flat.shape[0], dtype=jnp.int32) // top)
    )
    filled = jnp.zeros((experts * capacity,), jnp.bool_).at[slot_of].set(True)
    outgoing = jnp.where(filled[:, None], normed[source], jnp.zeros((), jnp.bfloat16)).reshape(
        experts, capacity, normed.shape[1]
    )
    quarter = expert_in.shape[3]
    weights_in = expert_in[0].reshape(width, 2 * quarter)
    incoming = lax.all_to_all(outgoing, "expert", split_axis=0, concat_axis=0, tiled=True)
    sources = incoming.shape[0]
    items = incoming.shape[1]
    gathered = lax.all_gather(incoming, "mp", axis=2, tiled=True).reshape(sources * items, width)
    inner = jnp.dot(gathered, weights_in, preferred_element_type=jnp.float32).reshape(
        -1, 2, quarter
    )
    hidden = (jax.nn.silu(inner[:, 0]) * inner[:, 1]).astype(jnp.bfloat16)
    partial_out = jnp.dot(hidden, expert_out[0], preferred_element_type=jnp.float32).astype(
        jnp.bfloat16
    )
    partial_out = partial_out.reshape(sources, items, width)
    result = lax.all_to_all(partial_out, "expert", split_axis=0, concat_axis=0, tiled=True)
    picked = result.reshape(experts * capacity, result.shape[2])[slot_of]
    slot_total = lax.psum_scatter(
        lax.optimization_barrier(picked).astype(jnp.float32).astype(jnp.bfloat16),
        "mp",
        scatter_dimension=1,
        tiled=True,
    )
    expert_sum = lax.optimization_barrier(slot_total).astype(jnp.float32)
    expert_sum = expert_sum.reshape(rows_here, top, expert_sum.shape[1])
    routed = jnp.sum(gates[:, :, None] * expert_sum, axis=1)
    shared = lax.psum_scatter(shared_part, "mp", scatter_dimension=1, tiled=True)
    return mixed + routed + shared


def swap(x, bit):
    n = lax.axis_size("expert")
    return lax.ppermute(x, "expert", [(i, i ^ bit) for i in range(n)])


def silu(v):
    return v / (1.0 + jnp.exp(-v))


def spread_first(h0, h1):
    return jnp.concatenate([h0, swap(h0, 2)], axis=0), jnp.concatenate([h1, swap(h1, 4)], axis=0)


def spread_second(l0, l1):
    return l0, swap(l0, 4), l1, swap(l1, 2)


def along_z(block, layers):
    blocks = [block]
    for k in range(1, layers):
        low = k & -k
        blocks.append(swap(blocks[k - low], LAYER * low))
    return blocks


def tie(x, *others):
    return lax.optimization_barrier((x, *others))[0]


class Copies:
    def __init__(self, sems):
        self.sems, self.all = sems, []

    def start(self, src, dst):
        c = pltpu.make_async_copy(src, dst, self.sems.at[len(self.all)])
        c.start()
        self.all.append(c)

    def wait(self):
        for c in self.all:
            c.wait()


PIECES = ((0, 0, (0, 1)), (1, 0, (2, 3)), (2, 1, (0, 2)), (3, 1, (1, 3)))


def fetch_rows(copies, pieces, rows, xs):
    half = xs.shape[1] // 2
    for n, h, chips in PIECES:
        stride = pieces[n].shape[0] // 2
        for a, q in enumerate(chips):
            copies.start(
                pieces[n].at[pl.ds(a * stride, rows)],
                xs.at[pl.ds(q * rows, rows), pl.ds(h * half, half)],
            )


def fetch_gates(copies, left, rows, to):
    for piece, (_, _, chips) in zip(left, PIECES):
        stride = piece.shape[0] // 2
        for a, q in enumerate(chips):
            copies.start(piece.at[pl.ds(a * stride + rows, stride - rows)], to.at[q])


def slots_of(sent, idx_ref, expert, experts, cap, rows):
    extra, half = sent.shape[1:]
    each = half // rows
    tall = experts // each
    line, column = idx_ref[2 * expert], idx_ref[2 * expert + 1]
    r = lax.broadcasted_iota(jnp.int32, (extra, half), 0)
    wanted = (r == line) | (r == line + tall) | (r == line + 2 * tall)
    found = []
    for q in range(4):
        parts = jnp.where(wanted, sent[q].astype(jnp.float32), 0.0)
        parts = jnp.sum(parts, axis=0, keepdims=True)
        g = jnp.zeros((1, rows), jnp.float32)
        for j in range(each):
            g = jnp.where(column == j, parts[:, j * rows : (j + 1) * rows], g)
        found.append(g)
    g = jnp.concatenate(found, axis=0)
    chosen = g > 0.0
    r_io = lax.broadcasted_iota(jnp.int32, (rows, rows), 0)
    c_io = lax.broadcasted_iota(jnp.int32, (rows, rows), 1)
    upto = jnp.where(r_io <= c_io, 1.0, 0.0).astype(jnp.bfloat16)
    count = jnp.dot(
        jnp.where(chosen, 1.0, 0.0).astype(jnp.bfloat16), upto, preferred_element_type=jnp.float32
    ).astype(jnp.int32)
    first = lax.broadcasted_iota(jnp.int32, (4, rows), 0) * cap
    return g, jnp.where(chosen, first + count - 1, -1)


def steps(total, most):
    step = min(most, total)
    return [(n, step) for n in range(0, total, step)]


def attention_kernel(groups, rows, idx_ref, mine_ref, other_ref, *rest):
    pieces, (keep_ref, send_ref, w_v, sems) = rest[: 4 * groups], rest[4 * groups :]
    half = w_v.shape[1] // 2
    count = pieces[0].shape[0] // (2 * rows)
    copies = Copies(sems)
    for g in range(groups):
        l0, r0, l1, r1 = pieces[4 * g : 4 * g + 4]
        for h, (near, far, first, second) in enumerate(((l0, r0, 1, 2), (l1, r1, 2, 1))):
            for piece, base in ((near, 0), (far, second)):
                for a, q in enumerate((base, base + first)):
                    for i in range(count):
                        chip = idx_ref[(g * count + i) * 4 + q]
                        to = pl.ds(pl.multiple_of(chip * rows, rows), rows)
                        copies.start(
                            piece.at[pl.ds((a * count + i) * rows, rows)],
                            w_v.at[to, pl.ds(h * half, half)],
                        )
    copies.wait()
    both = jnp.concatenate([mine_ref[...], other_ref[...]], axis=0)
    here = mine_ref.shape[0]
    for n, step in steps(w_v.shape[0], 512):
        part = lax.dot_general(
            both,
            w_v[pl.ds(n, step), :],
            (((1,), (1,)), ((), ())),
            preferred_element_type=jnp.float32,
        )
        keep_ref[:, pl.ds(n, step)] = part[:here]
        send_ref[:, pl.ds(n, step)] = part[here:]


def pick_kernel(cap, rows, experts, unused, idx_ref, *rest):
    pieces = rest[:4]
    mine_ref, other_ref, xs, sent, pick, out_v, x_sem, g_sem, o_sem = rest[4 + unused :]
    gates, copies = Copies(g_sem), Copies(x_sem)
    fetch_gates(gates, pieces[:2], rows, sent)
    fetch_rows(copies, pieces, rows, xs)
    slots = 4 * cap
    numbers = lax.broadcasted_iota(jnp.int32, (slots, rows), 0)
    gates.wait()
    for e in range(2):
        _, slot = slots_of(sent, idx_ref, e, experts, cap, rows)
        for q in range(4):
            pick[pl.ds(e * slots, slots), pl.ds(q * rows, rows)] = jnp.where(
                numbers == slot[q : q + 1, :], 1.0, 0.0
            ).astype(jnp.bfloat16)
    copies.wait()
    for n, step in steps(xs.shape[1], 512):
        out_v[:, pl.ds(n, step)] = jnp.dot(
            pick[...], xs[:, pl.ds(n, step)], preferred_element_type=jnp.float32
        ).astype(jnp.bfloat16)
    outs = Copies(o_sem)
    outs.start(out_v.at[pl.ds(slots, slots)], other_ref)
    outs.start(out_v.at[pl.ds(0, slots)], mine_ref)
    outs.wait()


def shared_kernel(rows, unused, three_ref, theirs_ref, *rest):
    pieces, (hs_ref, xs, w_v, x_sem) = rest[:4], rest[4 + unused :]
    hp = three_ref.shape[3]
    copies = Copies(x_sem)
    fetch_rows(copies, pieces, rows, xs)
    for e, ref in enumerate((three_ref, theirs_ref)):
        for h in range(2):
            copies.start(ref.at[:, h], w_v.at[:, :, pl.ds((2 * h + e) * hp, hp)])
    copies.wait()
    w = w_v[...].reshape(xs.shape[1], 4 * hp)
    for m, step in steps(4 * rows, 2 * rows):
        both = jnp.dot(xs[pl.ds(m, step), :], w, preferred_element_type=jnp.float32)
        hs_ref[pl.ds(m, step), :] = (silu(both[:, : 2 * hp]) * both[:, 2 * hp :]).astype(
            jnp.bfloat16
        )


def expert_kernel(unused, mine_ref, other_ref, win_ref, wout_ref, *rest):
    mine_out, other_out, x_v, win_v, wout_v, hid_v, y_v, x_sem, w_sem, o_sem = rest[unused:]
    slots, wide = mine_ref.shape
    tiles, tile = win_v.shape[0], win_v.shape[3] // 2
    rows = Copies(x_sem)
    rows.start(mine_ref, x_v.at[pl.ds(0, slots)])
    rows.start(other_ref, x_v.at[pl.ds(slots, slots)])
    copies = Copies(w_sem)
    for t in range(tiles):
        for h in range(2):
            copies.start(
                win_ref.at[:, h, :, pl.ds(t * tile, tile)],
                win_v.at[t, :, :, pl.ds(h * tile, tile)],
            )
    copies.start(wout_ref, wout_v)
    rows.wait()
    here = 0
    for t in range(tiles):
        if t == here:
            here = min(2 * here + 1, tiles)
            for c in copies.all[2 * t : 2 * here]:
                c.wait()
        both = jnp.dot(
            x_v[...], win_v[t].reshape(wide, 2 * tile), preferred_element_type=jnp.float32
        )
        hid_v[:, pl.ds(t * tile, tile)] = (silu(both[:, :tile]) * both[:, tile:]).astype(
            jnp.bfloat16
        )
    copies.all[2 * tiles].wait()
    outs = Copies(o_sem)
    for n, step in steps(wide, 512):
        y_v[:, pl.ds(n, step)] = jnp.dot(
            hid_v[...], wout_v[:, pl.ds(n, step)], preferred_element_type=jnp.float32
        ).astype(jnp.bfloat16)
    outs.start(y_v.at[pl.ds(slots, slots)], other_out)
    outs.start(y_v.at[pl.ds(0, slots)], mine_out)
    outs.wait()


def place_kernel(cap, rows, experts, unused, idx_ref, mine_ref, other_ref, hs_ref, *rest):
    three_ref, theirs_ref, l0, r0 = rest[:4]
    refs, rest = rest[4 + unused : 8 + unused], rest[8 + unused :]
    bufs, (w_v, sent, place, gate_col, g_sem, w_sem, o_sem) = rest[:4], rest[4:]
    near_low, far_low, near_high, far_high = bufs
    wide, half = mine_ref.shape[1], near_low.shape[1]
    hp = three_ref.shape[3]
    slots = 4 * cap
    f32 = jnp.float32
    gates, copies = Copies(g_sem), Copies(w_sem)
    fetch_gates(gates, (l0, r0), rows, sent)
    for e, ref in enumerate((three_ref, theirs_ref)):
        copies.start(ref.at[:, 2], w_v.at[:, :, pl.ds(e * hp, hp)])
    r_io = lax.broadcasted_iota(jnp.int32, (rows, rows), 0)
    c_io = lax.broadcasted_iota(jnp.int32, (rows, rows), 1)
    eye = r_io == c_io
    numbers = lax.broadcasted_iota(jnp.int32, (rows, slots), 1)
    gates.wait()
    for e in range(2):
        g, slot = slots_of(sent, idx_ref, e, experts, cap, rows)
        for q in range(4):
            at = pl.ds(q * rows, rows)
            col = jnp.sum(jnp.where(eye, slot[q : q + 1, :], 0), axis=1, keepdims=True)
            place[e, at, :] = jnp.where(numbers == col, 1.0, 0.0).astype(jnp.bfloat16)
            gcol = jnp.sum(jnp.where(eye, g[q : q + 1, :], 0.0), axis=1, keepdims=True)
            gate_col[e, at, :] = jnp.broadcast_to(gcol, (rows, LANES))
    copies.wait()
    depth = w_v.shape[1]
    outs = Copies(o_sem)
    for n, step in steps(wide, min(256, half)):
        cols = pl.ds(n, step)
        if step % depth == 0:
            down = w_v[pl.ds(n // depth, step // depth)].reshape(step, 2 * hp)
        else:
            down = w_v[...].reshape(wide, 2 * hp)[n : n + step]
        total = lax.dot_general(
            hs_ref[...], down, (((1,), (1,)), ((), ())), preferred_element_type=f32
        )
        for e, ref in enumerate((mine_ref, other_ref)):
            y = jnp.dot(place[e], ref[:, cols], preferred_element_type=f32)
            total = total + gate_col[e][:, 0:1] * y
        if n < half:
            near, far, order, at = near_low, far_low, (0, 1, 2, 3), pl.ds(n, step)
        else:
            near, far, order, at = near_high, far_high, (0, 2, 1, 3), pl.ds(n - half, step)
        for a in range(2):
            to = pl.ds(a * rows, rows)
            q = order[a] * rows
            near[to, at] = total[q : q + rows]
            q = order[2 + a] * rows
            far[to, at] = total[q : q + rows].astype(far.dtype)
        if (n + step) % half == 0:
            k = 2 * (n // half)
            outs.start(bufs[k + 1], refs[k + 1])
            outs.start(bufs[k], refs[k])
    outs.wait()


def call(body, out_shape, in_specs, args, scratch, after=(), outs_in_vmem=True):
    vmem = pl.BlockSpec(memory_space=pltpu.VMEM)
    hbm = pl.BlockSpec(memory_space=pl.ANY)
    kinds = {"s": pl.BlockSpec(memory_space=pltpu.SMEM), "v": vmem, "h": hbm}
    return pl.pallas_call(
        body,
        out_shape=out_shape,
        in_specs=[kinds[k] for k in in_specs] + [hbm] * len(after),
        out_specs=tuple([vmem if outs_in_vmem else hbm] * len(out_shape)),
        scratch_shapes=scratch,
        compiler_params=pltpu.CompilerParams(vmem_limit_bytes=48 * 1024 * 1024),
        cost_estimate=pl.CostEstimate(flops=1, bytes_accessed=1, transcendentals=0),
    )(*args, *after)


def attention(context, out_proj, before, exchange):
    bf, f32 = jnp.bfloat16, jnp.float32
    me = lax.axis_index("expert")
    layers = lax.axis_size("expert") // LAYER
    odd = me % 2 == 1
    wide = context.shape[1]
    half = wide // 2

    def halves(lo, hi):
        return jnp.where(odd, hi, lo), jnp.where(odd, lo, hi)

    turned = out_proj.T
    mine, other = halves(turned[:, :half], turned[:, half:])
    pair = jnp.concatenate(halves(mine, swap(other, 1)), axis=0)
    mine, other = halves(context[:, :half], context[:, half:])
    got = swap(other, 1)
    cut = pair.shape[0]
    blocks = [pair]
    twos = [list(range(i, min(i + 2, layers))) for i in range(0, layers, 2)]
    quarter, firsts = half // 2, []
    for two in twos:
        for k in two:
            low = k & -k
            if k and k == two[-1] and firsts:
                blocks.append(swap(tie(blocks[k - low], *firsts[-1]), LAYER * low))
            elif k:
                blocks.append(swap(blocks[k - low], LAYER * low))
        stack = jnp.concatenate([blocks[k] for k in two], axis=0)
        firsts.append(spread_first(stack[:, :quarter], stack[:, quarter:]))
    pieces, chips = [], []
    for two, first in zip(twos, firsts):
        pieces += spread_second(*first)
        for k in two:
            layer = jnp.bitwise_xor(me // LAYER, k)
            chips += [layer * (LAYER // 2) + jnp.bitwise_xor(me % LAYER // 2, q) for q in range(4)]
    mine, before, exchange = lax.optimization_barrier((mine, before, exchange))
    exchange = lax.all_to_all(
        tie(exchange, *pieces), "expert", split_axis=0, concat_axis=0, tiled=True
    )
    here = context.shape[0]
    keep, send = call(
        functools.partial(attention_kernel, len(twos), cut),
        [jax.ShapeDtypeStruct((here, wide), f32)] * 2,
        "svv" + "h" * len(pieces),
        (jnp.stack(chips).astype(jnp.int32), mine, got, *pieces),
        [
            pltpu.VMEM((out_proj.shape[1] * lax.axis_size("expert"), half), bf),
            pltpu.SemaphoreType.DMA((8 * layers,)),
        ],
    )
    return keep + swap(send, 1), before, exchange


def whole_rows(
    hidden_state,
    context,
    out_proj,
    norm_gain,
    router_weight,
    expert_in,
    expert_out,
    shared_in,
    shared_out,
    route_ids,
):
    bf, f32 = jnp.bfloat16, jnp.float32
    n = lax.axis_size("expert")
    layers = n // LAYER
    me = lax.axis_index("expert")
    odd = me % 2
    rows, top = route_ids.shape
    experts = router_weight.shape[1]
    wide = out_proj.shape[0]
    half = wide // 2
    cap = capacity_of(rows, top, experts)
    pack = 16
    win = expert_in[0].reshape(wide // pack, pack, 2, -1).transpose(0, 2, 1, 3)
    wout = expert_out[0]
    hidden = wout.shape[0]
    tile = LANES if hidden % LANES == 0 else hidden

    own = shared_in.shape[2] // n
    depth = shared_in.shape[0]
    hp = -(-own // LANES) * LANES
    three = jnp.concatenate([shared_in.transpose(1, 0, 2), shared_out.T[None]], axis=0)
    three = three.reshape(3, depth, n, own)
    three = jnp.pad(three, ((0, 0), (0, 0), (0, 0), (0, hp - own))).transpose(2, 0, 1, 3)

    attn, win, three = attention(context, out_proj, win, three)
    mixed = hidden_state.astype(f32) + attn
    inverse = lax.rsqrt(jnp.mean(mixed * mixed, axis=1, keepdims=True) + 1e-06)
    normed32 = mixed * inverse * norm_gain.astype(f32)
    normed = normed32.astype(bf)
    logits = jnp.dot(normed32, router_weight, precision=lax.Precision.HIGHEST)
    named = jnp.any(
        route_ids[:, :, None] == jnp.arange(experts, dtype=jnp.int32)[None, None, :], axis=1
    )
    highest = jnp.max(jnp.where(named, logits, -jnp.inf), axis=1, keepdims=True)
    raised = jnp.where(named, jnp.exp(logits - highest), 0.0)
    gates = raised / jnp.sum(raised, axis=1, keepdims=True)

    rest, parts = gates.T, []
    for _ in range(3):
        parts.append(lax.reduce_precision(rest, 8, 7))
        rest = rest - parts[-1]
    below = jnp.stack(parts).astype(bf).reshape(-1, half)
    extra = -(-below.shape[0] // 16) * 16
    below = jnp.pad(below, ((0, extra - below.shape[0]), (0, 0)))
    below = jnp.pad(below, ((0, 0), (0, half)))
    blocks = along_z(jnp.concatenate([normed, below], axis=0), layers)

    each = half // rows
    chip_experts = (me, jnp.bitwise_xor(me, 1))
    idx = jnp.stack([v for e in chip_experts for v in (e // each, e % each)]).astype(jnp.int32)
    slots, span = 4 * cap, 4 * rows
    sds, dma = jax.ShapeDtypeStruct, pltpu.SemaphoreType.DMA
    xs = pltpu.VMEM((span, wide), bf)
    sent = pltpu.VMEM((4, extra, half), bf)

    def add_first(near_low, far_low, near_high, far_high):
        low = near_low + swap(far_low, 4).astype(f32)
        high = near_high + swap(far_high, 2).astype(f32)
        return low[:rows], low[rows:].astype(bf), high[:rows], high[rows:].astype(bf)

    def pick(pieces, after):
        return call(
            functools.partial(pick_kernel, cap, rows, experts, len(after)),
            [sds((slots, wide), bf)] * 2,
            "shhhh",
            (idx, *pieces),
            [
                xs,
                sent,
                pltpu.VMEM((2 * slots, span), bf),
                pltpu.VMEM((2 * slots, wide), bf),
                dma((8,)),
                dma((4,)),
                dma((2,)),
            ],
            after,
            False,
        )

    def shared(pieces, after):
        return call(
            functools.partial(shared_kernel, rows, len(after)),
            [sds((span, 2 * hp), bf)],
            "hhhhhh",
            (three, theirs, *pieces),
            [xs, pltpu.VMEM((n, depth, 4 * hp), bf), dma((12,))],
            after,
        )[0]

    def expert(picked, borrowed, after):
        return call(
            functools.partial(expert_kernel, len(after)),
            [sds((slots, wide), bf)] * 2,
            "hhhh",
            (picked, borrowed, win, wout),
            [
                pltpu.VMEM((2 * slots, wide), bf),
                pltpu.VMEM((hidden // tile, wide // pack, pack, 2 * tile), bf),
                pltpu.VMEM((hidden, wide), bf),
                pltpu.VMEM((2 * slots, hidden), bf),
                pltpu.VMEM((2 * slots, wide), bf),
                dma((2,)),
                dma((2 * (hidden // tile) + 1,)),
                dma((2,)),
            ],
            after,
            False,
        )

    def place(done, returned, hs, pieces, after):
        return call(
            functools.partial(place_kernel, cap, rows, experts, len(after)),
            [sds((2 * rows, half), t) for t in (f32, bf, f32, bf)],
            "svvvhhhh",
            (idx, done, returned, hs, three, theirs, pieces[0], pieces[1]),
            [pltpu.VMEM((2 * rows, half), t) for t in (f32, bf, f32, bf)]
            + [
                pltpu.VMEM((n, depth, 2 * hp), bf),
                sent,
                pltpu.VMEM((2, span, slots), bf),
                pltpu.VMEM((2, span, LANES), f32),
                dma((4,)),
                dma((2,)),
                dma((4,)),
            ],
            after,
            False,
        )

    order = [0] + list(reversed(range(1, layers)))
    placed, once = [], []
    arrived = {k: [] for k in order}

    def home(k, parts):
        low, far_low, high, far_high = parts
        low = low + swap(far_low, 2).astype(f32)
        high = high + swap(far_high, 4).astype(f32)
        arrived[k].append(jnp.concatenate([low, high], axis=1))
        if not k:
            return []
        bit = k & -k
        got = swap(sum(arrived[k]).astype(bf), LAYER * bit)
        arrived[k - bit].append(got.astype(f32))
        return [got]

    def first(k, *others):
        block = tie(blocks[k], *others) if others else blocks[k]
        return spread_first(block[:, :half], block[:rows, half:])

    pieces = spread_second(*first(0))
    picked, lent = pick(pieces, [])
    far = blocks[order[1] :][:1] if layers > 1 else []
    done, back = expert(picked, swap(lent, 1), far)
    ahead = first(order[1]) if layers > 1 else []
    back = tie(back, *ahead) if ahead else back
    theirs = swap(tie(three, done, *ahead), 1)
    hs = shared(pieces, [done])
    placed.append(place(done, swap(back, 1), hs, pieces, []))
    for at in range(1, layers):
        if at == 1:
            pieces = spread_second(*ahead)
            picked, lent = pick(pieces, [placed[-1][1]])
            hs = shared(pieces, [lent])
        more = at + 1 < layers
        after = [hs]
        if more:
            ahead = first(order[at + 1], *ahead)
            after += ahead
        done, back = expert(picked, swap(lent, 1), after)
        now, after = (hs, pieces), []
        if more:
            pieces = spread_second(*ahead)
            back = tie(back, pieces[1], pieces[3])
            picked, lent = pick(pieces, [done])
            after = [lent]
        once.append(add_first(*placed[-1]))
        after += [once[-1][1], once[-1][3]]
        if at >= 2:
            after += home(order[at - 2], once[at - 2])
        placed.append(place(done, swap(back, 1), *now, after))
        if more:
            hs = shared(pieces, [placed[-1][1]])
    once.append(add_first(*placed[-1]))
    for at in range(max(layers - 2, 0), layers):
        home(order[at], once[at])
    return mixed + sum(arrived[0])


def solution(mesh):
    n, mp = mesh.shape["expert"], mesh.shape["mp"]
    fits = mp == 1 and n % LAYER == 0 and (n // LAYER) & (n // LAYER - 1) == 0
    per_device = whole_rows if fits else general
    return jax.shard_map(
        per_device,
        mesh=mesh,
        in_specs=(
            P("expert", "mp"),
            P("expert", "mp"),
            P("mp", "expert"),
            P("mp"),
            P("mp", None),
            P("expert", None, None, "mp"),
            P("expert", "mp", None),
            P("expert", None, "mp"),
            P("mp", "expert"),
            P("expert", None),
        ),
        out_specs=P("expert", "mp"),
        check_vma=False,
    )
```

```python
import functools

import jax
import jax.numpy as jnp
from jax import lax
from jax.experimental import pallas as pl
from jax.experimental.pallas import tpu as pltpu
from jax.sharding import PartitionSpec as P

LANES = 128
LAYER = 8


def capacity_of(rows, top, experts):
    return max(2, min(rows, rows * top // experts * 5 // 3))


def general(
    hidden_state,
    context,
    out_proj,
    norm_gain,
    router_weight,
    expert_in,
    expert_out,
    shared_in,
    shared_out,
    route_ids,
):
    rows_here, top = route_ids.shape
    experts = router_weight.shape[1]
    width = out_proj.shape[0] * lax.axis_size("mp")
    capacity = capacity_of(rows_here, top, experts)
    partial_attn = jnp.dot(
        context,
        lax.all_gather(out_proj, "expert", axis=1, tiled=True),
        preferred_element_type=jnp.float32,
    )
    attn = lax.psum_scatter(partial_attn, "mp", scatter_dimension=1, tiled=True)
    mixed = hidden_state.astype(jnp.float32) + attn
    gain = norm_gain.astype(jnp.float32)
    squares = lax.psum(jnp.sum(mixed * mixed, axis=1), "mp")
    inverse = lax.rsqrt(squares / width + 1e-06)[:, None]
    normed32 = mixed * inverse * gain
    logits = lax.psum(jnp.dot(normed32, router_weight, precision=lax.Precision.HIGHEST), "mp")
    normed = normed32.astype(jnp.bfloat16)
    gates = jax.nn.softmax(jnp.take_along_axis(logits, route_ids, axis=1), axis=1)
    full_rows = lax.all_gather(normed, "mp", axis=1, tiled=True)
    shared_width = shared_in.shape[2]
    piece = lax.all_gather(shared_in, "expert", axis=0, tiled=True)
    shared_both = jnp.dot(
        full_rows,
        piece.reshape(piece.shape[0], 2 * shared_width),
        preferred_element_type=jnp.float32,
    )
    shared_both = shared_both.reshape(rows_here, 2, shared_width)
    shared_hidden = (jax.nn.silu(shared_both[:, 0]) * shared_both[:, 1]).astype(jnp.bfloat16)
    shared_part = jnp.dot(
        shared_hidden,
        lax.all_gather(shared_out, "expert", axis=1, tiled=True),
        preferred_element_type=jnp.float32,
    )
    flat = route_ids.reshape(-1)
    onehot = (flat[:, None] == jnp.arange(experts, dtype=jnp.int32)[None, :]).astype(jnp.int32)
    position = jnp.sum(onehot * jnp.cumsum(onehot, axis=0), axis=1) - 1
    slot_of = flat * capacity + position
    source = (
        jnp.zeros((experts * capacity,), jnp.int32)
        .at[slot_of]
        .set(jnp.arange(flat.shape[0], dtype=jnp.int32) // top)
    )
    filled = jnp.zeros((experts * capacity,), jnp.bool_).at[slot_of].set(True)
    outgoing = jnp.where(filled[:, None], normed[source], jnp.zeros((), jnp.bfloat16)).reshape(
        experts, capacity, normed.shape[1]
    )
    quarter = expert_in.shape[3]
    weights_in = expert_in[0].reshape(width, 2 * quarter)
    incoming = lax.all_to_all(outgoing, "expert", split_axis=0, concat_axis=0, tiled=True)
    sources = incoming.shape[0]
    items = incoming.shape[1]
    gathered = lax.all_gather(incoming, "mp", axis=2, tiled=True).reshape(sources * items, width)
    inner = jnp.dot(gathered, weights_in, preferred_element_type=jnp.float32).reshape(
        -1, 2, quarter
    )
    hidden = (jax.nn.silu(inner[:, 0]) * inner[:, 1]).astype(jnp.bfloat16)
    partial_out = jnp.dot(hidden, expert_out[0], preferred_element_type=jnp.float32).astype(
        jnp.bfloat16
    )
    partial_out = partial_out.reshape(sources, items, width)
    result = lax.all_to_all(partial_out, "expert", split_axis=0, concat_axis=0, tiled=True)
    picked = result.reshape(experts * capacity, result.shape[2])[slot_of]
    slot_total = lax.psum_scatter(
        lax.optimization_barrier(picked).astype(jnp.float32).astype(jnp.bfloat16),
        "mp",
        scatter_dimension=1,
        tiled=True,
    )
    expert_sum = lax.optimization_barrier(slot_total).astype(jnp.float32)
    expert_sum = expert_sum.reshape(rows_here, top, expert_sum.shape[1])
    routed = jnp.sum(gates[:, :, None] * expert_sum, axis=1)
    shared = lax.psum_scatter(shared_part, "mp", scatter_dimension=1, tiled=True)
    return mixed + routed + shared


def swap(x, bit):
    n = lax.axis_size("expert")
    return lax.ppermute(x, "expert", [(i, i ^ bit) for i in range(n)])


def silu(v):
    return v / (1.0 + jnp.exp(-v))


def spread_first(h0, h1):
    return jnp.concatenate([h0, swap(h0, 2)], axis=0), jnp.concatenate([h1, swap(h1, 4)], axis=0)


def spread_second(l0, l1):
    return l0, swap(l0, 4), l1, swap(l1, 2)


def along_z(block, layers):
    blocks = [block]
    for k in range(1, layers):
        low = k & -k
        blocks.append(swap(blocks[k - low], LAYER * low))
    return blocks


def tie(x, *others):
    return lax.optimization_barrier((x, *others))[0]


class Copies:
    def __init__(self, sems):
        self.sems, self.all = sems, []

    def start(self, src, dst):
        c = pltpu.make_async_copy(src, dst, self.sems.at[len(self.all)])
        c.start()
        self.all.append(c)

    def wait(self):
        for c in self.all:
            c.wait()


PIECES = ((0, 0, (0, 1)), (1, 0, (2, 3)), (2, 1, (0, 2)), (3, 1, (1, 3)))


def fetch_rows(copies, pieces, rows, xs):
    half = xs.shape[1] // 2
    for n, h, chips in PIECES:
        stride = pieces[n].shape[0] // 2
        for a, q in enumerate(chips):
            copies.start(
                pieces[n].at[pl.ds(a * stride, rows)],
                xs.at[pl.ds(q * rows, rows), pl.ds(h * half, half)],
            )


def fetch_gates(copies, left, rows, to):
    for piece, (_, _, chips) in zip(left, PIECES):
        stride = piece.shape[0] // 2
        for a, q in enumerate(chips):
            copies.start(piece.at[pl.ds(a * stride + rows, stride - rows)], to.at[q])


def slots_of(sent, idx_ref, expert, experts, cap, rows):
    extra, half = sent.shape[1:]
    each = half // rows
    tall = experts // each
    line, column = idx_ref[2 * expert], idx_ref[2 * expert + 1]
    r = lax.broadcasted_iota(jnp.int32, (extra, half), 0)
    wanted = (r == line) | (r == line + tall) | (r == line + 2 * tall)
    found = []
    for q in range(4):
        parts = jnp.where(wanted, sent[q].astype(jnp.float32), 0.0)
        parts = jnp.sum(parts, axis=0, keepdims=True)
        g = jnp.zeros((1, rows), jnp.float32)
        for j in range(each):
            g = jnp.where(column == j, parts[:, j * rows : (j + 1) * rows], g)
        found.append(g)
    g = jnp.concatenate(found, axis=0)
    chosen = g > 0.0
    r_io = lax.broadcasted_iota(jnp.int32, (rows, rows), 0)
    c_io = lax.broadcasted_iota(jnp.int32, (rows, rows), 1)
    upto = jnp.where(r_io <= c_io, 1.0, 0.0).astype(jnp.bfloat16)
    count = jnp.dot(
        jnp.where(chosen, 1.0, 0.0).astype(jnp.bfloat16), upto, preferred_element_type=jnp.float32
    ).astype(jnp.int32)
    first = lax.broadcasted_iota(jnp.int32, (4, rows), 0) * cap
    return g, jnp.where(chosen, first + count - 1, -1)


def steps(total, most):
    step = min(most, total)
    return [(n, step) for n in range(0, total, step)]


def attention_kernel(groups, rows, idx_ref, mine_ref, other_ref, *rest):
    pieces, (keep_ref, send_ref, w_v, sems) = rest[: 4 * groups], rest[4 * groups :]
    half = w_v.shape[1] // 2
    count = pieces[0].shape[0] // (2 * rows)
    copies = Copies(sems)
    for g in range(groups):
        l0, r0, l1, r1 = pieces[4 * g : 4 * g + 4]
        for h, (near, far, first, second) in enumerate(((l0, r0, 1, 2), (l1, r1, 2, 1))):
            for piece, base in ((near, 0), (far, second)):
                for a, q in enumerate((base, base + first)):
                    for i in range(count):
                        chip = idx_ref[(g * count + i) * 4 + q]
                        to = pl.ds(pl.multiple_of(chip * rows, rows), rows)
                        copies.start(
                            piece.at[pl.ds((a * count + i) * rows, rows)],
                            w_v.at[to, pl.ds(h * half, half)],
                        )
    copies.wait()
    both = jnp.concatenate([mine_ref[...], other_ref[...]], axis=0)
    here = mine_ref.shape[0]
    for n, step in steps(w_v.shape[0], 512):
        part = lax.dot_general(
            both,
            w_v[pl.ds(n, step), :],
            (((1,), (1,)), ((), ())),
            preferred_element_type=jnp.float32,
        )
        keep_ref[:, pl.ds(n, step)] = part[:here]
        send_ref[:, pl.ds(n, step)] = part[here:]


def pick_kernel(cap, rows, experts, unused, idx_ref, *rest):
    pieces = rest[:4]
    mine_ref, other_ref, xs, sent, pick, out_v, x_sem, g_sem, o_sem = rest[4 + unused :]
    gates, copies = Copies(g_sem), Copies(x_sem)
    fetch_gates(gates, pieces[:2], rows, sent)
    fetch_rows(copies, pieces, rows, xs)
    slots = 4 * cap
    numbers = lax.broadcasted_iota(jnp.int32, (slots, rows), 0)
    gates.wait()
    for e in range(2):
        _, slot = slots_of(sent, idx_ref, e, experts, cap, rows)
        for q in range(4):
            pick[pl.ds(e * slots, slots), pl.ds(q * rows, rows)] = jnp.where(
                numbers == slot[q : q + 1, :], 1.0, 0.0
            ).astype(jnp.bfloat16)
    copies.wait()
    for n, step in steps(xs.shape[1], 512):
        out_v[:, pl.ds(n, step)] = jnp.dot(
            pick[...], xs[:, pl.ds(n, step)], preferred_element_type=jnp.float32
        ).astype(jnp.bfloat16)
    outs = Copies(o_sem)
    outs.start(out_v.at[pl.ds(slots, slots)], other_ref)
    outs.start(out_v.at[pl.ds(0, slots)], mine_ref)
    outs.wait()


def shared_kernel(rows, unused, three_ref, theirs_ref, *rest):
    pieces, (hs_ref, xs, w_v, x_sem) = rest[:4], rest[4 + unused :]
    hp = three_ref.shape[3]
    copies = Copies(x_sem)
    fetch_rows(copies, pieces, rows, xs)
    for e, ref in enumerate((three_ref, theirs_ref)):
        for h in range(2):
            copies.start(ref.at[:, h], w_v.at[:, :, pl.ds((2 * h + e) * hp, hp)])
    copies.wait()
    w = w_v[...].reshape(xs.shape[1], 4 * hp)
    for m, step in steps(4 * rows, 2 * rows):
        both = jnp.dot(xs[pl.ds(m, step), :], w, preferred_element_type=jnp.float32)
        hs_ref[pl.ds(m, step), :] = (silu(both[:, : 2 * hp]) * both[:, 2 * hp :]).astype(
            jnp.bfloat16
        )


def expert_kernel(unused, mine_ref, other_ref, win_ref, wout_ref, *rest):
    mine_out, other_out, x_v, win_v, wout_v, hid_v, y_v, x_sem, w_sem, o_sem = rest[unused:]
    slots, wide = mine_ref.shape
    tiles, tile = win_v.shape[0], win_v.shape[3] // 2
    rows = Copies(x_sem)
    rows.start(mine_ref, x_v.at[pl.ds(0, slots)])
    rows.start(other_ref, x_v.at[pl.ds(slots, slots)])
    copies = Copies(w_sem)
    for t in range(tiles):
        for h in range(2):
            copies.start(
                win_ref.at[:, h, :, pl.ds(t * tile, tile)],
                win_v.at[t, :, :, pl.ds(h * tile, tile)],
            )
    copies.start(wout_ref, wout_v)
    rows.wait()
    here = 0
    for t in range(tiles):
        if t == here:
            here = min(2 * here + 1, tiles)
            for c in copies.all[2 * t : 2 * here]:
                c.wait()
        both = jnp.dot(
            x_v[...], win_v[t].reshape(wide, 2 * tile), preferred_element_type=jnp.float32
        )
        hid_v[:, pl.ds(t * tile, tile)] = (silu(both[:, :tile]) * both[:, tile:]).astype(
            jnp.bfloat16
        )
    copies.all[2 * tiles].wait()
    outs = Copies(o_sem)
    for n, step in steps(wide, 512):
        y_v[:, pl.ds(n, step)] = jnp.dot(
            hid_v[...], wout_v[:, pl.ds(n, step)], preferred_element_type=jnp.float32
        ).astype(jnp.bfloat16)
    outs.start(y_v.at[pl.ds(slots, slots)], other_out)
    outs.start(y_v.at[pl.ds(0, slots)], mine_out)
    outs.wait()


def place_kernel(cap, rows, experts, unused, idx_ref, mine_ref, other_ref, hs_ref, *rest):
    three_ref, theirs_ref, l0, r0 = rest[:4]
    refs, rest = rest[4 + unused : 8 + unused], rest[8 + unused :]
    bufs, (w_v, sent, place, gate_col, g_sem, w_sem, o_sem) = rest[:4], rest[4:]
    near_low, far_low, near_high, far_high = bufs
    wide, half = mine_ref.shape[1], near_low.shape[1]
    hp = three_ref.shape[3]
    slots = 4 * cap
    f32 = jnp.float32
    gates, copies = Copies(g_sem), Copies(w_sem)
    fetch_gates(gates, (l0, r0), rows, sent)
    for e, ref in enumerate((three_ref, theirs_ref)):
        copies.start(ref.at[:, 2], w_v.at[:, :, pl.ds(e * hp, hp)])
    r_io = lax.broadcasted_iota(jnp.int32, (rows, rows), 0)
    c_io = lax.broadcasted_iota(jnp.int32, (rows, rows), 1)
    eye = r_io == c_io
    numbers = lax.broadcasted_iota(jnp.int32, (rows, slots), 1)
    gates.wait()
    for e in range(2):
        g, slot = slots_of(sent, idx_ref, e, experts, cap, rows)
        for q in range(4):
            at = pl.ds(q * rows, rows)
            col = jnp.sum(jnp.where(eye, slot[q : q + 1, :], 0), axis=1, keepdims=True)
            place[e, at, :] = jnp.where(numbers == col, 1.0, 0.0).astype(jnp.bfloat16)
            gcol = jnp.sum(jnp.where(eye, g[q : q + 1, :], 0.0), axis=1, keepdims=True)
            gate_col[e, at, :] = jnp.broadcast_to(gcol, (rows, LANES))
    copies.wait()
    depth = w_v.shape[1]
    outs = Copies(o_sem)
    for n, step in steps(wide, min(256, half)):
        cols = pl.ds(n, step)
        if step % depth == 0:
            down = w_v[pl.ds(n // depth, step // depth)].reshape(step, 2 * hp)
        else:
            down = w_v[...].reshape(wide, 2 * hp)[n : n + step]
        total = lax.dot_general(
            hs_ref[...], down, (((1,), (1,)), ((), ())), preferred_element_type=f32
        )
        for e, ref in enumerate((mine_ref, other_ref)):
            y = jnp.dot(place[e], ref[:, cols], preferred_element_type=f32)
            total = total + gate_col[e][:, 0:1] * y
        if n < half:
            near, far, order, at = near_low, far_low, (0, 1, 2, 3), pl.ds(n, step)
        else:
            near, far, order, at = near_high, far_high, (0, 2, 1, 3), pl.ds(n - half, step)
        for a in range(2):
            to = pl.ds(a * rows, rows)
            q = order[a] * rows
            near[to, at] = total[q : q + rows]
            q = order[2 + a] * rows
            far[to, at] = total[q : q + rows].astype(far.dtype)
        if (n + step) % half == 0:
            k = 2 * (n // half)
            outs.start(bufs[k + 1], refs[k + 1])
            outs.start(bufs[k], refs[k])
    outs.wait()


def call(body, out_shape, in_specs, args, scratch, after=(), outs_in_vmem=True):
    vmem = pl.BlockSpec(memory_space=pltpu.VMEM)
    hbm = pl.BlockSpec(memory_space=pl.ANY)
    kinds = {"s": pl.BlockSpec(memory_space=pltpu.SMEM), "v": vmem, "h": hbm}
    return pl.pallas_call(
        body,
        out_shape=out_shape,
        in_specs=[kinds[k] for k in in_specs] + [hbm] * len(after),
        out_specs=tuple([vmem if outs_in_vmem else hbm] * len(out_shape)),
        scratch_shapes=scratch,
        compiler_params=pltpu.CompilerParams(vmem_limit_bytes=48 * 1024 * 1024),
        cost_estimate=pl.CostEstimate(flops=1, bytes_accessed=1, transcendentals=0),
    )(*args, *after)


def attention(context, out_proj, before, exchange):
    bf, f32 = jnp.bfloat16, jnp.float32
    me = lax.axis_index("expert")
    layers = lax.axis_size("expert") // LAYER
    odd = me % 2 == 1
    wide = context.shape[1]
    half = wide // 2

    def halves(lo, hi):
        return jnp.where(odd, hi, lo), jnp.where(odd, lo, hi)

    turned = out_proj.T
    mine, other = halves(turned[:, :half], turned[:, half:])
    pair = jnp.concatenate(halves(mine, swap(other, 1)), axis=0)
    mine, other = halves(context[:, :half], context[:, half:])
    got = swap(other, 1)
    cut = pair.shape[0]
    blocks = along_z(pair, layers)
    if layers > 1:
        blocks[1], exchange = lax.optimization_barrier((blocks[1], exchange))
    twos = [list(range(i, min(i + 2, layers))) for i in range(0, layers, 2)]
    stacks = [jnp.concatenate([blocks[k] for k in two], axis=0) for two in twos]
    quarter = half // 2
    firsts = [spread_first(stack[:, :quarter], stack[:, quarter:]) for stack in stacks]
    pieces, chips = [], []
    for two, first in zip(twos, firsts):
        pieces += spread_second(*first)
        for k in two:
            layer = jnp.bitwise_xor(me // LAYER, k)
            chips += [layer * (LAYER // 2) + jnp.bitwise_xor(me % LAYER // 2, q) for q in range(4)]
    mine, before = lax.optimization_barrier((mine, before))
    exchange = lax.all_to_all(
        tie(exchange, *pieces), "expert", split_axis=0, concat_axis=0, tiled=True
    )
    here = context.shape[0]
    keep, send = call(
        functools.partial(attention_kernel, len(twos), cut),
        [jax.ShapeDtypeStruct((here, wide), f32)] * 2,
        "svv" + "h" * len(pieces),
        (jnp.stack(chips).astype(jnp.int32), mine, got, *pieces),
        [
            pltpu.VMEM((out_proj.shape[1] * lax.axis_size("expert"), half), bf),
            pltpu.SemaphoreType.DMA((8 * layers,)),
        ],
    )
    return keep + swap(send, 1), before, exchange


def whole_rows(
    hidden_state,
    context,
    out_proj,
    norm_gain,
    router_weight,
    expert_in,
    expert_out,
    shared_in,
    shared_out,
    route_ids,
):
    bf, f32 = jnp.bfloat16, jnp.float32
    n = lax.axis_size("expert")
    layers = n // LAYER
    me = lax.axis_index("expert")
    odd = me % 2
    rows, top = route_ids.shape
    experts = router_weight.shape[1]
    wide = out_proj.shape[0]
    half = wide // 2
    cap = capacity_of(rows, top, experts)
    pack = 16
    win = expert_in[0].reshape(wide // pack, pack, 2, -1).transpose(0, 2, 1, 3)
    wout = expert_out[0]
    hidden = wout.shape[0]
    tile = LANES if hidden % LANES == 0 else hidden

    own = shared_in.shape[2] // n
    depth = shared_in.shape[0]
    hp = -(-own // LANES) * LANES
    three = jnp.concatenate([shared_in.transpose(1, 0, 2), shared_out.T[None]], axis=0)
    three = three.reshape(3, depth, n, own)
    three = jnp.pad(three, ((0, 0), (0, 0), (0, 0), (0, hp - own))).transpose(2, 0, 1, 3)

    attn, win, three = attention(context, out_proj, win, three)
    mixed = hidden_state.astype(f32) + attn
    inverse = lax.rsqrt(jnp.mean(mixed * mixed, axis=1, keepdims=True) + 1e-06)
    normed32 = mixed * inverse * norm_gain.astype(f32)
    normed = normed32.astype(bf)
    logits = jnp.dot(normed32, router_weight, precision=lax.Precision.HIGHEST)
    named = jnp.any(
        route_ids[:, :, None] == jnp.arange(experts, dtype=jnp.int32)[None, None, :], axis=1
    )
    highest = jnp.max(jnp.where(named, logits, -jnp.inf), axis=1, keepdims=True)
    raised = jnp.where(named, jnp.exp(logits - highest), 0.0)
    gates = raised / jnp.sum(raised, axis=1, keepdims=True)

    rest, parts = gates.T, []
    for _ in range(3):
        parts.append(lax.reduce_precision(rest, 8, 7))
        rest = rest - parts[-1]
    below = jnp.stack(parts).astype(bf).reshape(-1, half)
    extra = -(-below.shape[0] // 16) * 16
    below = jnp.pad(below, ((0, extra - below.shape[0]), (0, 0)))
    below = jnp.pad(below, ((0, 0), (0, half)))
    blocks = along_z(jnp.concatenate([normed, below], axis=0), layers)

    each = half // rows
    chip_experts = (me, jnp.bitwise_xor(me, 1))
    idx = jnp.stack([v for e in chip_experts for v in (e // each, e % each)]).astype(jnp.int32)
    slots, span = 4 * cap, 4 * rows
    sds, dma = jax.ShapeDtypeStruct, pltpu.SemaphoreType.DMA
    xs = pltpu.VMEM((span, wide), bf)
    sent = pltpu.VMEM((4, extra, half), bf)

    def add_first(near_low, far_low, near_high, far_high):
        low = near_low + swap(far_low, 4).astype(f32)
        high = near_high + swap(far_high, 2).astype(f32)
        return low[:rows], low[rows:].astype(bf), high[:rows], high[rows:].astype(bf)

    def pick(pieces, after):
        return call(
            functools.partial(pick_kernel, cap, rows, experts, len(after)),
            [sds((slots, wide), bf)] * 2,
            "shhhh",
            (idx, *pieces),
            [
                xs,
                sent,
                pltpu.VMEM((2 * slots, span), bf),
                pltpu.VMEM((2 * slots, wide), bf),
                dma((8,)),
                dma((4,)),
                dma((2,)),
            ],
            after,
            False,
        )

    def shared(pieces, after):
        return call(
            functools.partial(shared_kernel, rows, len(after)),
            [sds((span, 2 * hp), bf)],
            "hhhhhh",
            (three, theirs, *pieces),
            [xs, pltpu.VMEM((n, depth, 4 * hp), bf), dma((12,))],
            after,
        )[0]

    def expert(picked, borrowed, after):
        return call(
            functools.partial(expert_kernel, len(after)),
            [sds((slots, wide), bf)] * 2,
            "hhhh",
            (picked, borrowed, win, wout),
            [
                pltpu.VMEM((2 * slots, wide), bf),
                pltpu.VMEM((hidden // tile, wide // pack, pack, 2 * tile), bf),
                pltpu.VMEM((hidden, wide), bf),
                pltpu.VMEM((2 * slots, hidden), bf),
                pltpu.VMEM((2 * slots, wide), bf),
                dma((2,)),
                dma((2 * (hidden // tile) + 1,)),
                dma((2,)),
            ],
            after,
            False,
        )

    def place(done, returned, hs, pieces, after):
        return call(
            functools.partial(place_kernel, cap, rows, experts, len(after)),
            [sds((2 * rows, half), t) for t in (f32, bf, f32, bf)],
            "svvvhhhh",
            (idx, done, returned, hs, three, theirs, pieces[0], pieces[1]),
            [pltpu.VMEM((2 * rows, half), t) for t in (f32, bf, f32, bf)]
            + [
                pltpu.VMEM((n, depth, 2 * hp), bf),
                sent,
                pltpu.VMEM((2, span, slots), bf),
                pltpu.VMEM((2, span, LANES), f32),
                dma((4,)),
                dma((2,)),
                dma((4,)),
            ],
            after,
            False,
        )

    def first(k, *others):
        block = tie(blocks[k], *others) if others else blocks[k]
        return spread_first(block[:, :half], block[:rows, half:])

    def home(k, parts):
        low, far_low, high, far_high = parts
        low = low + swap(far_low, 2).astype(f32)
        high = high + swap(far_high, 4).astype(f32)
        both = jnp.concatenate([low, high], axis=1)
        return swap(both.astype(bf), LAYER * k).astype(f32) if k else both

    placed, once = [], []
    pieces = spread_second(*first(0))
    picked, lent = pick(pieces, [])
    hs = theirs = done = None
    for k in range(layers):
        more = k + 1 < layers
        after = [hs] if k else []
        if more:
            ahead = first(k + 1, *([done] if k > 1 else []))
            after += ahead
        done, back = expert(picked, swap(lent, 1), after)
        now, after = pieces, []
        if more:
            pieces = spread_second(*ahead)
            back = tie(back, pieces[1], pieces[3])
            picked, lent = pick(pieces, [done])
            after = [lent]
        if k == 0:
            theirs = swap(tie(three, done, *after, *blocks[2:3]), 1)
            hs = shared(now, after or [done])
        else:
            once.append(add_first(*placed[-1]))
            after += [once[-1][1], once[-1][3]]
        placed.append(place(done, swap(back, 1), hs, now, after))
        if more:
            hs = shared(pieces, [placed[-1][1]])
    once.append(add_first(*placed[-1]))
    total = mixed
    for k in range(layers):
        total = total + home(k, once[k])
    return total


def solution(mesh):
    n, mp = mesh.shape["expert"], mesh.shape["mp"]
    fits = mp == 1 and n % LAYER == 0 and (n // LAYER) & (n // LAYER - 1) == 0
    per_device = whole_rows if fits else general
    return jax.shard_map(
        per_device,
        mesh=mesh,
        in_specs=(
            P("expert", "mp"),
            P("expert", "mp"),
            P("mp", "expert"),
            P("mp"),
            P("mp", None),
            P("expert", None, None, "mp"),
            P("expert", "mp", None),
            P("expert", None, "mp"),
            P("mp", "expert"),
            P("expert", None),
        ),
        out_specs=P("expert", "mp"),
        check_vma=False,
    )
```

```python
import functools

import jax
import jax.numpy as jnp
from jax import lax
from jax.experimental import pallas as pl
from jax.experimental.pallas import tpu as pltpu
from jax.sharding import PartitionSpec as P

LANES = 128
LAYER = 8


def capacity_of(rows, top, experts):
    return max(2, min(rows, rows * top // experts * 5 // 3))


def general(
    hidden_state,
    context,
    out_proj,
    norm_gain,
    router_weight,
    expert_in,
    expert_out,
    shared_in,
    shared_out,
    route_ids,
):
    rows_here, top = route_ids.shape
    experts = router_weight.shape[1]
    width = out_proj.shape[0] * lax.axis_size("mp")
    capacity = capacity_of(rows_here, top, experts)
    partial_attn = jnp.dot(
        context,
        lax.all_gather(out_proj, "expert", axis=1, tiled=True),
        preferred_element_type=jnp.float32,
    )
    attn = lax.psum_scatter(partial_attn, "mp", scatter_dimension=1, tiled=True)
    mixed = hidden_state.astype(jnp.float32) + attn
    gain = norm_gain.astype(jnp.float32)
    squares = lax.psum(jnp.sum(mixed * mixed, axis=1), "mp")
    inverse = lax.rsqrt(squares / width + 1e-06)[:, None]
    normed32 = mixed * inverse * gain
    logits = lax.psum(jnp.dot(normed32, router_weight, precision=lax.Precision.HIGHEST), "mp")
    normed = normed32.astype(jnp.bfloat16)
    gates = jax.nn.softmax(jnp.take_along_axis(logits, route_ids, axis=1), axis=1)
    full_rows = lax.all_gather(normed, "mp", axis=1, tiled=True)
    shared_width = shared_in.shape[2]
    piece = lax.all_gather(shared_in, "expert", axis=0, tiled=True)
    shared_both = jnp.dot(
        full_rows,
        piece.reshape(piece.shape[0], 2 * shared_width),
        preferred_element_type=jnp.float32,
    )
    shared_both = shared_both.reshape(rows_here, 2, shared_width)
    shared_hidden = (jax.nn.silu(shared_both[:, 0]) * shared_both[:, 1]).astype(jnp.bfloat16)
    shared_part = jnp.dot(
        shared_hidden,
        lax.all_gather(shared_out, "expert", axis=1, tiled=True),
        preferred_element_type=jnp.float32,
    )
    flat = route_ids.reshape(-1)
    onehot = (flat[:, None] == jnp.arange(experts, dtype=jnp.int32)[None, :]).astype(jnp.int32)
    position = jnp.sum(onehot * jnp.cumsum(onehot, axis=0), axis=1) - 1
    slot_of = flat * capacity + position
    source = (
        jnp.zeros((experts * capacity,), jnp.int32)
        .at[slot_of]
        .set(jnp.arange(flat.shape[0], dtype=jnp.int32) // top)
    )
    filled = jnp.zeros((experts * capacity,), jnp.bool_).at[slot_of].set(True)
    outgoing = jnp.where(filled[:, None], normed[source], jnp.zeros((), jnp.bfloat16)).reshape(
        experts, capacity, normed.shape[1]
    )
    quarter = expert_in.shape[3]
    weights_in = expert_in[0].reshape(width, 2 * quarter)
    incoming = lax.all_to_all(outgoing, "expert", split_axis=0, concat_axis=0, tiled=True)
    sources = incoming.shape[0]
    items = incoming.shape[1]
    gathered = lax.all_gather(incoming, "mp", axis=2, tiled=True).reshape(sources * items, width)
    inner = jnp.dot(gathered, weights_in, preferred_element_type=jnp.float32).reshape(
        -1, 2, quarter
    )
    hidden = (jax.nn.silu(inner[:, 0]) * inner[:, 1]).astype(jnp.bfloat16)
    partial_out = jnp.dot(hidden, expert_out[0], preferred_element_type=jnp.float32).astype(
        jnp.bfloat16
    )
    partial_out = partial_out.reshape(sources, items, width)
    result = lax.all_to_all(partial_out, "expert", split_axis=0, concat_axis=0, tiled=True)
    picked = result.reshape(experts * capacity, result.shape[2])[slot_of]
    slot_total = lax.psum_scatter(
        lax.optimization_barrier(picked).astype(jnp.float32).astype(jnp.bfloat16),
        "mp",
        scatter_dimension=1,
        tiled=True,
    )
    expert_sum = lax.optimization_barrier(slot_total).astype(jnp.float32)
    expert_sum = expert_sum.reshape(rows_here, top, expert_sum.shape[1])
    routed = jnp.sum(gates[:, :, None] * expert_sum, axis=1)
    shared = lax.psum_scatter(shared_part, "mp", scatter_dimension=1, tiled=True)
    return mixed + routed + shared


def swap(x, bit):
    n = lax.axis_size("expert")
    return lax.ppermute(x, "expert", [(i, i ^ bit) for i in range(n)])


def silu(v):
    return v / (1.0 + jnp.exp(-v))


def spread_first(h0, h1):
    return jnp.concatenate([h0, swap(h0, 2)], axis=0), jnp.concatenate([h1, swap(h1, 4)], axis=0)


def spread_second(l0, l1):
    return l0, swap(l0, 4), l1, swap(l1, 2)


def along_z(block, layers):
    blocks = [block]
    for k in range(1, layers):
        low = k & -k
        blocks.append(swap(blocks[k - low], LAYER * low))
    return blocks


def tie(x, *others):
    return lax.optimization_barrier((x, *others))[0]


class Copies:
    def __init__(self, sems):
        self.sems, self.all = sems, []

    def start(self, src, dst):
        c = pltpu.make_async_copy(src, dst, self.sems.at[len(self.all)])
        c.start()
        self.all.append(c)

    def wait(self):
        for c in self.all:
            c.wait()


PIECES = ((0, 0, (0, 1)), (1, 0, (2, 3)), (2, 1, (0, 2)), (3, 1, (1, 3)))


def fetch_rows(copies, pieces, rows, xs):
    half = xs.shape[1] // 2
    for n, h, chips in PIECES:
        stride = pieces[n].shape[0] // 2
        for a, q in enumerate(chips):
            copies.start(
                pieces[n].at[pl.ds(a * stride, rows)],
                xs.at[pl.ds(q * rows, rows), pl.ds(h * half, half)],
            )


def fetch_gates(copies, left, rows, to):
    for piece, (_, _, chips) in zip(left, PIECES):
        stride = piece.shape[0] // 2
        for a, q in enumerate(chips):
            copies.start(piece.at[pl.ds(a * stride + rows, stride - rows)], to.at[q])


def slots_of(sent, idx_ref, expert, experts, cap, rows):
    extra, half = sent.shape[1:]
    each = half // rows
    tall = experts // each
    line, column = idx_ref[2 * expert], idx_ref[2 * expert + 1]
    r = lax.broadcasted_iota(jnp.int32, (extra, half), 0)
    wanted = (r == line) | (r == line + tall) | (r == line + 2 * tall)
    found = []
    for q in range(4):
        parts = jnp.where(wanted, sent[q].astype(jnp.float32), 0.0)
        parts = jnp.sum(parts, axis=0, keepdims=True)
        g = jnp.zeros((1, rows), jnp.float32)
        for j in range(each):
            g = jnp.where(column == j, parts[:, j * rows : (j + 1) * rows], g)
        found.append(g)
    g = jnp.concatenate(found, axis=0)
    chosen = g > 0.0
    r_io = lax.broadcasted_iota(jnp.int32, (rows, rows), 0)
    c_io = lax.broadcasted_iota(jnp.int32, (rows, rows), 1)
    upto = jnp.where(r_io <= c_io, 1.0, 0.0).astype(jnp.bfloat16)
    count = jnp.dot(
        jnp.where(chosen, 1.0, 0.0).astype(jnp.bfloat16), upto, preferred_element_type=jnp.float32
    ).astype(jnp.int32)
    first = lax.broadcasted_iota(jnp.int32, (4, rows), 0) * cap
    return g, jnp.where(chosen, first + count - 1, -1)


def steps(total, most):
    step = min(most, total)
    return [(n, step) for n in range(0, total, step)]


def attention_kernel(groups, rows, idx_ref, mine_ref, other_ref, *rest):
    pieces, (keep_ref, send_ref, w_v, sems) = rest[: 4 * groups], rest[4 * groups :]
    half = w_v.shape[1] // 2
    count = pieces[0].shape[0] // (2 * rows)
    copies = Copies(sems)
    for g in range(groups):
        l0, r0, l1, r1 = pieces[4 * g : 4 * g + 4]
        for h, (near, far, first, second) in enumerate(((l0, r0, 1, 2), (l1, r1, 2, 1))):
            for piece, base in ((near, 0), (far, second)):
                for a, q in enumerate((base, base + first)):
                    for i in range(count):
                        chip = idx_ref[(g * count + i) * 4 + q]
                        to = pl.ds(pl.multiple_of(chip * rows, rows), rows)
                        copies.start(
                            piece.at[pl.ds((a * count + i) * rows, rows)],
                            w_v.at[to, pl.ds(h * half, half)],
                        )
    copies.wait()
    both = jnp.concatenate([mine_ref[...], other_ref[...]], axis=0)
    here = mine_ref.shape[0]
    for n, step in steps(w_v.shape[0], 512):
        part = lax.dot_general(
            both,
            w_v[pl.ds(n, step), :],
            (((1,), (1,)), ((), ())),
            preferred_element_type=jnp.float32,
        )
        keep_ref[:, pl.ds(n, step)] = part[:here]
        send_ref[:, pl.ds(n, step)] = part[here:]


def pick_kernel(cap, rows, experts, unused, idx_ref, *rest):
    pieces = rest[:4]
    mine_ref, other_ref, xs, sent, pick, out_v, x_sem, g_sem, o_sem = rest[4 + unused :]
    gates, copies = Copies(g_sem), Copies(x_sem)
    fetch_gates(gates, pieces[:2], rows, sent)
    fetch_rows(copies, pieces, rows, xs)
    slots = 4 * cap
    numbers = lax.broadcasted_iota(jnp.int32, (slots, rows), 0)
    gates.wait()
    for e in range(2):
        _, slot = slots_of(sent, idx_ref, e, experts, cap, rows)
        for q in range(4):
            pick[pl.ds(e * slots, slots), pl.ds(q * rows, rows)] = jnp.where(
                numbers == slot[q : q + 1, :], 1.0, 0.0
            ).astype(jnp.bfloat16)
    copies.wait()
    for n, step in steps(xs.shape[1], 512):
        out_v[:, pl.ds(n, step)] = jnp.dot(
            pick[...], xs[:, pl.ds(n, step)], preferred_element_type=jnp.float32
        ).astype(jnp.bfloat16)
    outs = Copies(o_sem)
    outs.start(out_v.at[pl.ds(slots, slots)], other_ref)
    outs.start(out_v.at[pl.ds(0, slots)], mine_ref)
    outs.wait()


def shared_kernel(rows, unused, three_ref, theirs_ref, *rest):
    pieces, (hs_ref, xs, w_v, x_sem) = rest[:4], rest[4 + unused :]
    hp = three_ref.shape[3]
    copies = Copies(x_sem)
    fetch_rows(copies, pieces, rows, xs)
    for e, ref in enumerate((three_ref, theirs_ref)):
        for h in range(2):
            copies.start(ref.at[:, h], w_v.at[:, :, pl.ds((2 * h + e) * hp, hp)])
    copies.wait()
    w = w_v[...].reshape(xs.shape[1], 4 * hp)
    for m, step in steps(4 * rows, 2 * rows):
        both = jnp.dot(xs[pl.ds(m, step), :], w, preferred_element_type=jnp.float32)
        hs_ref[pl.ds(m, step), :] = (silu(both[:, : 2 * hp]) * both[:, 2 * hp :]).astype(
            jnp.bfloat16
        )


def expert_kernel(unused, mine_ref, other_ref, win_ref, wout_ref, *rest):
    mine_out, other_out, x_v, win_v, wout_v, hid_v, y_v, x_sem, w_sem, o_sem = rest[unused:]
    slots, wide = mine_ref.shape
    tiles, tile = win_v.shape[0], win_v.shape[3] // 2
    rows = Copies(x_sem)
    rows.start(mine_ref, x_v.at[pl.ds(0, slots)])
    rows.start(other_ref, x_v.at[pl.ds(slots, slots)])
    copies = Copies(w_sem)
    for t in range(tiles):
        for h in range(2):
            copies.start(
                win_ref.at[:, h, :, pl.ds(t * tile, tile)],
                win_v.at[t, :, :, pl.ds(h * tile, tile)],
            )
    copies.start(wout_ref, wout_v)
    rows.wait()
    here = 0
    for t in range(tiles):
        if t == here:
            here = min(2 * here + 1, tiles)
            for c in copies.all[2 * t : 2 * here]:
                c.wait()
        both = jnp.dot(
            x_v[...], win_v[t].reshape(wide, 2 * tile), preferred_element_type=jnp.float32
        )
        hid_v[:, pl.ds(t * tile, tile)] = (silu(both[:, :tile]) * both[:, tile:]).astype(
            jnp.bfloat16
        )
    copies.all[2 * tiles].wait()
    outs = Copies(o_sem)
    for n, step in steps(wide, 512):
        y_v[:, pl.ds(n, step)] = jnp.dot(
            hid_v[...], wout_v[:, pl.ds(n, step)], preferred_element_type=jnp.float32
        ).astype(jnp.bfloat16)
    outs.start(y_v.at[pl.ds(slots, slots)], other_out)
    outs.start(y_v.at[pl.ds(0, slots)], mine_out)
    outs.wait()


def place_kernel(cap, rows, experts, unused, idx_ref, mine_ref, other_ref, hs_ref, *rest):
    three_ref, theirs_ref, l0, r0 = rest[:4]
    refs, rest = rest[4 + unused : 8 + unused], rest[8 + unused :]
    bufs, (w_v, sent, place, gate_col, g_sem, w_sem, o_sem) = rest[:4], rest[4:]
    near_low, far_low, near_high, far_high = bufs
    wide, half = mine_ref.shape[1], near_low.shape[1]
    hp = three_ref.shape[3]
    slots = 4 * cap
    f32 = jnp.float32
    gates, copies = Copies(g_sem), Copies(w_sem)
    fetch_gates(gates, (l0, r0), rows, sent)
    for e, ref in enumerate((three_ref, theirs_ref)):
        copies.start(ref.at[:, 2], w_v.at[:, :, pl.ds(e * hp, hp)])
    r_io = lax.broadcasted_iota(jnp.int32, (rows, rows), 0)
    c_io = lax.broadcasted_iota(jnp.int32, (rows, rows), 1)
    eye = r_io == c_io
    numbers = lax.broadcasted_iota(jnp.int32, (rows, slots), 1)
    gates.wait()
    for e in range(2):
        g, slot = slots_of(sent, idx_ref, e, experts, cap, rows)
        for q in range(4):
            at = pl.ds(q * rows, rows)
            col = jnp.sum(jnp.where(eye, slot[q : q + 1, :], 0), axis=1, keepdims=True)
            place[e, at, :] = jnp.where(numbers == col, 1.0, 0.0).astype(jnp.bfloat16)
            gcol = jnp.sum(jnp.where(eye, g[q : q + 1, :], 0.0), axis=1, keepdims=True)
            gate_col[e, at, :] = jnp.broadcast_to(gcol, (rows, LANES))
    copies.wait()
    depth = w_v.shape[1]
    outs = Copies(o_sem)
    for n, step in steps(wide, min(256, half)):
        cols = pl.ds(n, step)
        if step % depth == 0:
            down = w_v[pl.ds(n // depth, step // depth)].reshape(step, 2 * hp)
        else:
            down = w_v[...].reshape(wide, 2 * hp)[n : n + step]
        total = lax.dot_general(
            hs_ref[...], down, (((1,), (1,)), ((), ())), preferred_element_type=f32
        )
        for e, ref in enumerate((mine_ref, other_ref)):
            y = jnp.dot(place[e], ref[:, cols], preferred_element_type=f32)
            total = total + gate_col[e][:, 0:1] * y
        if n < half:
            near, far, order, at = near_low, far_low, (0, 1, 2, 3), pl.ds(n, step)
        else:
            near, far, order, at = near_high, far_high, (0, 2, 1, 3), pl.ds(n - half, step)
        for a in range(2):
            to = pl.ds(a * rows, rows)
            q = order[a] * rows
            near[to, at] = total[q : q + rows]
            q = order[2 + a] * rows
            far[to, at] = total[q : q + rows].astype(far.dtype)
        if (n + step) % half == 0:
            k = 2 * (n // half)
            outs.start(bufs[k + 1], refs[k + 1])
            outs.start(bufs[k], refs[k])
    outs.wait()


def call(body, out_shape, in_specs, args, scratch, after=(), outs_in_vmem=True):
    vmem = pl.BlockSpec(memory_space=pltpu.VMEM)
    hbm = pl.BlockSpec(memory_space=pl.ANY)
    kinds = {"s": pl.BlockSpec(memory_space=pltpu.SMEM), "v": vmem, "h": hbm}
    return pl.pallas_call(
        body,
        out_shape=out_shape,
        in_specs=[kinds[k] for k in in_specs] + [hbm] * len(after),
        out_specs=tuple([vmem if outs_in_vmem else hbm] * len(out_shape)),
        scratch_shapes=scratch,
        compiler_params=pltpu.CompilerParams(vmem_limit_bytes=48 * 1024 * 1024),
        cost_estimate=pl.CostEstimate(flops=1, bytes_accessed=1, transcendentals=0),
    )(*args, *after)


def attention(context, out_proj, before, exchange):
    bf, f32 = jnp.bfloat16, jnp.float32
    me = lax.axis_index("expert")
    layers = lax.axis_size("expert") // LAYER
    odd = me % 2 == 1
    wide = context.shape[1]
    half = wide // 2

    def halves(lo, hi):
        return jnp.where(odd, hi, lo), jnp.where(odd, lo, hi)

    turned = out_proj.T
    mine, other = halves(turned[:, :half], turned[:, half:])
    pair = jnp.concatenate(halves(mine, swap(other, 1)), axis=0)
    mine, other = halves(context[:, :half], context[:, half:])
    got = swap(other, 1)
    cut = pair.shape[0]
    blocks = along_z(pair, layers)
    if layers > 1:
        blocks[1], exchange = lax.optimization_barrier((blocks[1], exchange))
    twos = [list(range(i, min(i + 2, layers))) for i in range(0, layers, 2)]
    stacks = [jnp.concatenate([blocks[k] for k in two], axis=0) for two in twos]
    quarter = half // 2
    firsts = [spread_first(stack[:, :quarter], stack[:, quarter:]) for stack in stacks]
    pieces, chips = [], []
    for two, first in zip(twos, firsts):
        pieces += spread_second(*first)
        for k in two:
            layer = jnp.bitwise_xor(me // LAYER, k)
            chips += [layer * (LAYER // 2) + jnp.bitwise_xor(me % LAYER // 2, q) for q in range(4)]
    mine, before = lax.optimization_barrier((mine, before))
    exchange = lax.all_to_all(
        tie(exchange, *pieces), "expert", split_axis=0, concat_axis=0, tiled=True
    )
    here = context.shape[0]
    keep, send = call(
        functools.partial(attention_kernel, len(twos), cut),
        [jax.ShapeDtypeStruct((here, wide), f32)] * 2,
        "svv" + "h" * len(pieces),
        (jnp.stack(chips).astype(jnp.int32), mine, got, *pieces),
        [
            pltpu.VMEM((out_proj.shape[1] * lax.axis_size("expert"), half), bf),
            pltpu.SemaphoreType.DMA((8 * layers,)),
        ],
    )
    return keep + swap(send, 1), before, exchange


def whole_rows(
    hidden_state,
    context,
    out_proj,
    norm_gain,
    router_weight,
    expert_in,
    expert_out,
    shared_in,
    shared_out,
    route_ids,
):
    bf, f32 = jnp.bfloat16, jnp.float32
    n = lax.axis_size("expert")
    layers = n // LAYER
    me = lax.axis_index("expert")
    odd = me % 2
    rows, top = route_ids.shape
    experts = router_weight.shape[1]
    wide = out_proj.shape[0]
    half = wide // 2
    cap = capacity_of(rows, top, experts)
    pack = 16
    win = expert_in[0].reshape(wide // pack, pack, 2, -1).transpose(0, 2, 1, 3)
    wout = expert_out[0]
    hidden = wout.shape[0]
    tile = LANES if hidden % LANES == 0 else hidden

    own = shared_in.shape[2] // n
    depth = shared_in.shape[0]
    hp = -(-own // LANES) * LANES
    three = jnp.concatenate([shared_in.transpose(1, 0, 2), shared_out.T[None]], axis=0)
    three = three.reshape(3, depth, n, own)
    three = jnp.pad(three, ((0, 0), (0, 0), (0, 0), (0, hp - own))).transpose(2, 0, 1, 3)

    attn, win, three = attention(context, out_proj, win, three)
    mixed = hidden_state.astype(f32) + attn
    inverse = lax.rsqrt(jnp.mean(mixed * mixed, axis=1, keepdims=True) + 1e-06)
    normed32 = mixed * inverse * norm_gain.astype(f32)
    normed = normed32.astype(bf)
    logits = jnp.dot(normed32, router_weight, precision=lax.Precision.HIGHEST)
    named = jnp.any(
        route_ids[:, :, None] == jnp.arange(experts, dtype=jnp.int32)[None, None, :], axis=1
    )
    highest = jnp.max(jnp.where(named, logits, -jnp.inf), axis=1, keepdims=True)
    raised = jnp.where(named, jnp.exp(logits - highest), 0.0)
    gates = raised / jnp.sum(raised, axis=1, keepdims=True)

    rest, parts = gates.T, []
    for _ in range(3):
        parts.append(lax.reduce_precision(rest, 8, 7))
        rest = rest - parts[-1]
    below = jnp.stack(parts).astype(bf).reshape(-1, half)
    extra = -(-below.shape[0] // 16) * 16
    below = jnp.pad(below, ((0, extra - below.shape[0]), (0, 0)))
    below = jnp.pad(below, ((0, 0), (0, half)))
    blocks = along_z(jnp.concatenate([normed, below], axis=0), layers)

    each = half // rows
    chip_experts = (me, jnp.bitwise_xor(me, 1))
    idx = jnp.stack([v for e in chip_experts for v in (e // each, e % each)]).astype(jnp.int32)
    slots, span = 4 * cap, 4 * rows
    sds, dma = jax.ShapeDtypeStruct, pltpu.SemaphoreType.DMA
    xs = pltpu.VMEM((span, wide), bf)
    sent = pltpu.VMEM((4, extra, half), bf)

    def add_first(near_low, far_low, near_high, far_high):
        low = near_low + swap(far_low, 4).astype(f32)
        high = near_high + swap(far_high, 2).astype(f32)
        return low[:rows], low[rows:].astype(bf), high[:rows], high[rows:].astype(bf)

    def pick(pieces, after):
        return call(
            functools.partial(pick_kernel, cap, rows, experts, len(after)),
            [sds((slots, wide), bf)] * 2,
            "shhhh",
            (idx, *pieces),
            [
                xs,
                sent,
                pltpu.VMEM((2 * slots, span), bf),
                pltpu.VMEM((2 * slots, wide), bf),
                dma((8,)),
                dma((4,)),
                dma((2,)),
            ],
            after,
            False,
        )

    def shared(pieces, after):
        return call(
            functools.partial(shared_kernel, rows, len(after)),
            [sds((span, 2 * hp), bf)],
            "hhhhhh",
            (three, theirs, *pieces),
            [xs, pltpu.VMEM((n, depth, 4 * hp), bf), dma((12,))],
            after,
        )[0]

    def expert(picked, borrowed, after):
        return call(
            functools.partial(expert_kernel, len(after)),
            [sds((slots, wide), bf)] * 2,
            "hhhh",
            (picked, borrowed, win, wout),
            [
                pltpu.VMEM((2 * slots, wide), bf),
                pltpu.VMEM((hidden // tile, wide // pack, pack, 2 * tile), bf),
                pltpu.VMEM((hidden, wide), bf),
                pltpu.VMEM((2 * slots, hidden), bf),
                pltpu.VMEM((2 * slots, wide), bf),
                dma((2,)),
                dma((2 * (hidden // tile) + 1,)),
                dma((2,)),
            ],
            after,
            False,
        )

    def place(done, returned, hs, pieces, after):
        return call(
            functools.partial(place_kernel, cap, rows, experts, len(after)),
            [sds((2 * rows, half), t) for t in (f32, bf, f32, bf)],
            "svvvhhhh",
            (idx, done, returned, hs, three, theirs, pieces[0], pieces[1]),
            [pltpu.VMEM((2 * rows, half), t) for t in (f32, bf, f32, bf)]
            + [
                pltpu.VMEM((n, depth, 2 * hp), bf),
                sent,
                pltpu.VMEM((2, span, slots), bf),
                pltpu.VMEM((2, span, LANES), f32),
                dma((4,)),
                dma((2,)),
                dma((4,)),
            ],
            after,
            False,
        )

    def first(k, *others):
        block = tie(blocks[k], *others) if others else blocks[k]
        return spread_first(block[:, :half], block[:rows, half:])

    def home(k, parts):
        low, far_low, high, far_high = parts
        low = low + swap(far_low, 2).astype(f32)
        high = high + swap(far_high, 4).astype(f32)
        both = jnp.concatenate([low, high], axis=1)
        return swap(both.astype(bf), LAYER * k).astype(f32) if k else both

    order = list(range(1, layers)) + [0]
    placed, once = [], []
    pieces = spread_second(*first(order[0]))
    picked, lent = pick(pieces, blocks[2:3])
    hs = theirs = done = None
    for k in range(layers):
        more = k + 1 < layers
        after = [hs] if k else []
        if more:
            ahead = first(order[k + 1], *([done] if k > 1 else []))
            after += ahead
        done, back = expert(picked, swap(lent, 1), after)
        now, after = pieces, []
        if more:
            pieces = spread_second(*ahead)
            back = tie(back, pieces[1], pieces[3])
            picked, lent = pick(pieces, [done])
            after = [lent]
        if k == 0:
            theirs = swap(tie(three, done, *after, *blocks[2:4]), 1)
            hs = shared(now, after or [done])
        else:
            once.append(add_first(*placed[-1]))
            after += [once[-1][1], once[-1][3]]
        placed.append(place(done, swap(back, 1), hs, now, after))
        if more:
            hs = shared(pieces, [placed[-1][1]])
    once.append(add_first(*placed[-1]))
    total = mixed
    for k, parts in zip(order, once):
        total = total + home(k, parts)
    return total


def solution(mesh):
    n, mp = mesh.shape["expert"], mesh.shape["mp"]
    fits = mp == 1 and n % LAYER == 0 and (n // LAYER) & (n // LAYER - 1) == 0
    per_device = whole_rows if fits else general
    return jax.shard_map(
        per_device,
        mesh=mesh,
        in_specs=(
            P("expert", "mp"),
            P("expert", "mp"),
            P("mp", "expert"),
            P("mp"),
            P("mp", None),
            P("expert", None, None, "mp"),
            P("expert", "mp", None),
            P("expert", None, "mp"),
            P("mp", "expert"),
            P("expert", None),
        ),
        out_specs=P("expert", "mp"),
        check_vma=False,
    )
```

```python
import functools

import jax
import jax.numpy as jnp
from jax import lax
from jax.experimental import pallas as pl
from jax.experimental.pallas import tpu as pltpu
from jax.sharding import PartitionSpec as P

LANES = 128
LAYER = 8


def capacity_of(rows, top, experts):
    return max(2, min(rows, rows * top // experts * 5 // 3))


def general(
    hidden_state,
    context,
    out_proj,
    norm_gain,
    router_weight,
    expert_in,
    expert_out,
    shared_in,
    shared_out,
    route_ids,
):
    rows_here, top = route_ids.shape
    experts = router_weight.shape[1]
    width = out_proj.shape[0] * lax.axis_size("mp")
    capacity = capacity_of(rows_here, top, experts)
    partial_attn = jnp.dot(
        context,
        lax.all_gather(out_proj, "expert", axis=1, tiled=True),
        preferred_element_type=jnp.float32,
    )
    attn = lax.psum_scatter(partial_attn, "mp", scatter_dimension=1, tiled=True)
    mixed = hidden_state.astype(jnp.float32) + attn
    gain = norm_gain.astype(jnp.float32)
    squares = lax.psum(jnp.sum(mixed * mixed, axis=1), "mp")
    inverse = lax.rsqrt(squares / width + 1e-06)[:, None]
    normed32 = mixed * inverse * gain
    logits = lax.psum(jnp.dot(normed32, router_weight, precision=lax.Precision.HIGHEST), "mp")
    normed = normed32.astype(jnp.bfloat16)
    gates = jax.nn.softmax(jnp.take_along_axis(logits, route_ids, axis=1), axis=1)
    full_rows = lax.all_gather(normed, "mp", axis=1, tiled=True)
    shared_width = shared_in.shape[2]
    piece = lax.all_gather(shared_in, "expert", axis=0, tiled=True)
    shared_both = jnp.dot(
        full_rows,
        piece.reshape(piece.shape[0], 2 * shared_width),
        preferred_element_type=jnp.float32,
    )
    shared_both = shared_both.reshape(rows_here, 2, shared_width)
    shared_hidden = (jax.nn.silu(shared_both[:, 0]) * shared_both[:, 1]).astype(jnp.bfloat16)
    shared_part = jnp.dot(
        shared_hidden,
        lax.all_gather(shared_out, "expert", axis=1, tiled=True),
        preferred_element_type=jnp.float32,
    )
    flat = route_ids.reshape(-1)
    onehot = (flat[:, None] == jnp.arange(experts, dtype=jnp.int32)[None, :]).astype(jnp.int32)
    position = jnp.sum(onehot * jnp.cumsum(onehot, axis=0), axis=1) - 1
    slot_of = flat * capacity + position
    source = (
        jnp.zeros((experts * capacity,), jnp.int32)
        .at[slot_of]
        .set(jnp.arange(flat.shape[0], dtype=jnp.int32) // top)
    )
    filled = jnp.zeros((experts * capacity,), jnp.bool_).at[slot_of].set(True)
    outgoing = jnp.where(filled[:, None], normed[source], jnp.zeros((), jnp.bfloat16)).reshape(
        experts, capacity, normed.shape[1]
    )
    quarter = expert_in.shape[3]
    weights_in = expert_in[0].reshape(width, 2 * quarter)
    incoming = lax.all_to_all(outgoing, "expert", split_axis=0, concat_axis=0, tiled=True)
    sources = incoming.shape[0]
    items = incoming.shape[1]
    gathered = lax.all_gather(incoming, "mp", axis=2, tiled=True).reshape(sources * items, width)
    inner = jnp.dot(gathered, weights_in, preferred_element_type=jnp.float32).reshape(
        -1, 2, quarter
    )
    hidden = (jax.nn.silu(inner[:, 0]) * inner[:, 1]).astype(jnp.bfloat16)
    partial_out = jnp.dot(hidden, expert_out[0], preferred_element_type=jnp.float32).astype(
        jnp.bfloat16
    )
    partial_out = partial_out.reshape(sources, items, width)
    result = lax.all_to_all(partial_out, "expert", split_axis=0, concat_axis=0, tiled=True)
    picked = result.reshape(experts * capacity, result.shape[2])[slot_of]
    slot_total = lax.psum_scatter(
        lax.optimization_barrier(picked).astype(jnp.float32).astype(jnp.bfloat16),
        "mp",
        scatter_dimension=1,
        tiled=True,
    )
    expert_sum = lax.optimization_barrier(slot_total).astype(jnp.float32)
    expert_sum = expert_sum.reshape(rows_here, top, expert_sum.shape[1])
    routed = jnp.sum(gates[:, :, None] * expert_sum, axis=1)
    shared = lax.psum_scatter(shared_part, "mp", scatter_dimension=1, tiled=True)
    return mixed + routed + shared


def swap(x, bit):
    n = lax.axis_size("expert")
    return lax.ppermute(x, "expert", [(i, i ^ bit) for i in range(n)])


def silu(v):
    return v / (1.0 + jnp.exp(-v))


def spread_first(block, rows):
    half = block.shape[1] // 2
    h0, h1 = block[:, :half], block[:rows, half:]
    return jnp.concatenate([h0, swap(h0, 2)], axis=0), jnp.concatenate([h1, swap(h1, 4)], axis=0)


def spread_second(l0, l1):
    return l0, swap(l0, 4), l1, swap(l1, 2)


def along_z(block, layers):
    blocks = [block]
    for k in range(1, layers):
        low = k & -k
        blocks.append(swap(blocks[k - low], LAYER * low))
    return blocks


def tie(x, *others):
    return lax.optimization_barrier((x, *others))[0]


class Copies:
    def __init__(self, sems):
        self.sems, self.all = sems, []

    def start(self, src, dst):
        c = pltpu.make_async_copy(src, dst, self.sems.at[len(self.all)])
        c.start()
        self.all.append(c)

    def wait(self):
        for c in self.all:
            c.wait()


PIECES = ((0, 0, (0, 1)), (1, 0, (2, 3)), (2, 1, (0, 2)), (3, 1, (1, 3)))


def fetch_rows(copies, pieces, rows, xs):
    half = xs.shape[1] // 2
    for n, h, chips in PIECES:
        stride = pieces[n].shape[0] // 2
        for a, q in enumerate(chips):
            copies.start(
                pieces[n].at[pl.ds(a * stride, rows)],
                xs.at[pl.ds(q * rows, rows), pl.ds(h * half, half)],
            )


def fetch_gates(copies, left, rows, to):
    for piece, (_, _, chips) in zip(left, PIECES):
        stride = piece.shape[0] // 2
        for a, q in enumerate(chips):
            copies.start(piece.at[pl.ds(a * stride + rows, stride - rows)], to.at[q])


def slots_of(sent, idx_ref, expert, experts, cap, rows):
    extra, half = sent.shape[1:]
    each = half // rows
    tall = experts // each
    line, column = idx_ref[2 * expert], idx_ref[2 * expert + 1]
    r = lax.broadcasted_iota(jnp.int32, (extra, half), 0)
    wanted = (r == line) | (r == line + tall) | (r == line + 2 * tall)
    found = []
    for q in range(4):
        parts = jnp.where(wanted, sent[q].astype(jnp.float32), 0.0)
        parts = jnp.sum(parts, axis=0, keepdims=True)
        g = jnp.zeros((1, rows), jnp.float32)
        for j in range(each):
            g = jnp.where(column == j, parts[:, j * rows : (j + 1) * rows], g)
        found.append(g)
    g = jnp.concatenate(found, axis=0)
    chosen = g > 0.0
    r_io = lax.broadcasted_iota(jnp.int32, (rows, rows), 0)
    c_io = lax.broadcasted_iota(jnp.int32, (rows, rows), 1)
    upto = jnp.where(r_io <= c_io, 1.0, 0.0).astype(jnp.bfloat16)
    count = jnp.dot(
        jnp.where(chosen, 1.0, 0.0).astype(jnp.bfloat16), upto, preferred_element_type=jnp.float32
    ).astype(jnp.int32)
    first = lax.broadcasted_iota(jnp.int32, (4, rows), 0) * cap
    return g, jnp.where(chosen, first + count - 1, -1)


def steps(total, most):
    step = min(most, total)
    return [(n, step) for n in range(0, total, step)]


def attention_kernel(groups, rows, idx_ref, mine_ref, other_ref, *rest):
    pieces, (keep_ref, send_ref, w_v, sems) = rest[: 4 * groups], rest[4 * groups :]
    half = w_v.shape[1] // 2
    count = pieces[0].shape[0] // (2 * rows)
    copies = Copies(sems)
    for g in range(groups):
        l0, r0, l1, r1 = pieces[4 * g : 4 * g + 4]
        for h, (near, far, first, second) in enumerate(((l0, r0, 1, 2), (l1, r1, 2, 1))):
            for piece, base in ((near, 0), (far, second)):
                for a, q in enumerate((base, base + first)):
                    for i in range(count):
                        chip = idx_ref[(g * count + i) * 4 + q]
                        to = pl.ds(pl.multiple_of(chip * rows, rows), rows)
                        copies.start(
                            piece.at[pl.ds((a * count + i) * rows, rows)],
                            w_v.at[to, pl.ds(h * half, half)],
                        )
    copies.wait()
    both = jnp.concatenate([mine_ref[...], other_ref[...]], axis=0)
    here = mine_ref.shape[0]
    for n, step in steps(w_v.shape[0], 512):
        part = lax.dot_general(
            both,
            w_v[pl.ds(n, step), :],
            (((1,), (1,)), ((), ())),
            preferred_element_type=jnp.float32,
        )
        keep_ref[:, pl.ds(n, step)] = part[:here]
        send_ref[:, pl.ds(n, step)] = part[here:]


def pick_kernel(cap, rows, experts, unused, idx_ref, *rest):
    pieces = rest[:4]
    mine_ref, other_ref, xs, sent, pick, out_v, x_sem, g_sem, o_sem = rest[4 + unused :]
    gates, copies = Copies(g_sem), Copies(x_sem)
    fetch_gates(gates, pieces[:2], rows, sent)
    fetch_rows(copies, pieces, rows, xs)
    slots = 4 * cap
    numbers = lax.broadcasted_iota(jnp.int32, (slots, rows), 0)
    gates.wait()
    for e in range(2):
        _, slot = slots_of(sent, idx_ref, e, experts, cap, rows)
        for q in range(4):
            pick[pl.ds(e * slots, slots), pl.ds(q * rows, rows)] = jnp.where(
                numbers == slot[q : q + 1, :], 1.0, 0.0
            ).astype(jnp.bfloat16)
    copies.wait()
    for n, step in steps(xs.shape[1], 512):
        out_v[:, pl.ds(n, step)] = jnp.dot(
            pick[...], xs[:, pl.ds(n, step)], preferred_element_type=jnp.float32
        ).astype(jnp.bfloat16)
    outs = Copies(o_sem)
    outs.start(out_v.at[pl.ds(slots, slots)], other_ref)
    outs.start(out_v.at[pl.ds(0, slots)], mine_ref)
    outs.wait()


def shared_kernel(rows, unused, three_ref, theirs_ref, *rest):
    pieces, (hs_ref, xs, w_v, x_sem) = rest[:4], rest[4 + unused :]
    hp = three_ref.shape[3]
    copies = Copies(x_sem)
    fetch_rows(copies, pieces, rows, xs)
    for e, ref in enumerate((three_ref, theirs_ref)):
        for h in range(2):
            copies.start(ref.at[:, h], w_v.at[:, :, pl.ds((2 * h + e) * hp, hp)])
    copies.wait()
    w = w_v[...].reshape(xs.shape[1], 4 * hp)
    for m, step in steps(4 * rows, 2 * rows):
        both = jnp.dot(xs[pl.ds(m, step), :], w, preferred_element_type=jnp.float32)
        hs_ref[pl.ds(m, step), :] = (silu(both[:, : 2 * hp]) * both[:, 2 * hp :]).astype(
            jnp.bfloat16
        )


def expert_kernel(unused, mine_ref, other_ref, win_ref, wout_ref, *rest):
    mine_out, other_out, x_v, win_v, wout_v, hid_v, y_v, x_sem, w_sem, o_sem = rest[unused:]
    slots, wide = mine_ref.shape
    tiles, tile = win_v.shape[0], win_v.shape[3] // 2
    rows = Copies(x_sem)
    rows.start(mine_ref, x_v.at[pl.ds(0, slots)])
    rows.start(other_ref, x_v.at[pl.ds(slots, slots)])
    copies = Copies(w_sem)
    for t in range(tiles):
        for h in range(2):
            copies.start(
                win_ref.at[:, h, :, pl.ds(t * tile, tile)],
                win_v.at[t, :, :, pl.ds(h * tile, tile)],
            )
    copies.start(wout_ref, wout_v)
    rows.wait()
    here = 0
    for t in range(tiles):
        if t == here:
            here = min(2 * here + 1, tiles)
            for c in copies.all[2 * t : 2 * here]:
                c.wait()
        both = jnp.dot(
            x_v[...], win_v[t].reshape(wide, 2 * tile), preferred_element_type=jnp.float32
        )
        hid_v[:, pl.ds(t * tile, tile)] = (silu(both[:, :tile]) * both[:, tile:]).astype(
            jnp.bfloat16
        )
    copies.all[2 * tiles].wait()
    outs = Copies(o_sem)
    for n, step in steps(wide, 512):
        y_v[:, pl.ds(n, step)] = jnp.dot(
            hid_v[...], wout_v[:, pl.ds(n, step)], preferred_element_type=jnp.float32
        ).astype(jnp.bfloat16)
    outs.start(y_v.at[pl.ds(slots, slots)], other_out)
    outs.start(y_v.at[pl.ds(0, slots)], mine_out)
    outs.wait()


def place_kernel(cap, rows, experts, unused, idx_ref, mine_ref, other_ref, hs_ref, *rest):
    three_ref, theirs_ref, l0, r0 = rest[:4]
    refs, rest = rest[4 + unused : 8 + unused], rest[8 + unused :]
    bufs, (w_v, sent, place, gate_col, g_sem, w_sem, o_sem) = rest[:4], rest[4:]
    near_low, far_low, near_high, far_high = bufs
    wide, half = mine_ref.shape[1], near_low.shape[1]
    hp = three_ref.shape[3]
    slots = 4 * cap
    f32 = jnp.float32
    gates, copies = Copies(g_sem), Copies(w_sem)
    fetch_gates(gates, (l0, r0), rows, sent)
    for e, ref in enumerate((three_ref, theirs_ref)):
        copies.start(ref.at[:, 2], w_v.at[:, :, pl.ds(e * hp, hp)])
    r_io = lax.broadcasted_iota(jnp.int32, (rows, rows), 0)
    c_io = lax.broadcasted_iota(jnp.int32, (rows, rows), 1)
    eye = r_io == c_io
    numbers = lax.broadcasted_iota(jnp.int32, (rows, slots), 1)
    gates.wait()
    for e in range(2):
        g, slot = slots_of(sent, idx_ref, e, experts, cap, rows)
        for q in range(4):
            at = pl.ds(q * rows, rows)
            col = jnp.sum(jnp.where(eye, slot[q : q + 1, :], 0), axis=1, keepdims=True)
            place[e, at, :] = jnp.where(numbers == col, 1.0, 0.0).astype(jnp.bfloat16)
            gcol = jnp.sum(jnp.where(eye, g[q : q + 1, :], 0.0), axis=1, keepdims=True)
            gate_col[e, at, :] = jnp.broadcast_to(gcol, (rows, LANES))
    copies.wait()
    depth = w_v.shape[1]
    outs = Copies(o_sem)
    for n, step in steps(wide, min(256, half)):
        cols = pl.ds(n, step)
        if step % depth == 0:
            down = w_v[pl.ds(n // depth, step // depth)].reshape(step, 2 * hp)
        else:
            down = w_v[...].reshape(wide, 2 * hp)[n : n + step]
        total = lax.dot_general(
            hs_ref[...], down, (((1,), (1,)), ((), ())), preferred_element_type=f32
        )
        for e, ref in enumerate((mine_ref, other_ref)):
            y = jnp.dot(place[e], ref[:, cols], preferred_element_type=f32)
            total = total + gate_col[e][:, 0:1] * y
        if n < half:
            near, far, order, at = near_low, far_low, (0, 1, 2, 3), pl.ds(n, step)
        else:
            near, far, order, at = near_high, far_high, (0, 2, 1, 3), pl.ds(n - half, step)
        for a in range(2):
            to = pl.ds(a * rows, rows)
            q = order[a] * rows
            near[to, at] = total[q : q + rows]
            q = order[2 + a] * rows
            far[to, at] = total[q : q + rows].astype(far.dtype)
        if (n + step) % half == 0:
            k = 2 * (n // half)
            outs.start(bufs[k + 1], refs[k + 1])
            outs.start(bufs[k], refs[k])
    outs.wait()


def call(body, out_shape, in_specs, args, scratch, after=(), outs_in_vmem=True):
    vmem = pl.BlockSpec(memory_space=pltpu.VMEM)
    hbm = pl.BlockSpec(memory_space=pl.ANY)
    kinds = {"s": pl.BlockSpec(memory_space=pltpu.SMEM), "v": vmem, "h": hbm}
    return pl.pallas_call(
        body,
        out_shape=out_shape,
        in_specs=[kinds[k] for k in in_specs] + [hbm] * len(after),
        out_specs=tuple([vmem if outs_in_vmem else hbm] * len(out_shape)),
        scratch_shapes=scratch,
        compiler_params=pltpu.CompilerParams(vmem_limit_bytes=48 * 1024 * 1024),
        cost_estimate=pl.CostEstimate(flops=1, bytes_accessed=1, transcendentals=0),
    )(*args, *after)


def attention(context, out_proj, before, exchange):
    bf, f32 = jnp.bfloat16, jnp.float32
    me = lax.axis_index("expert")
    layers = lax.axis_size("expert") // LAYER
    odd = me % 2 == 1
    wide = context.shape[1]
    half = wide // 2

    def halves(lo, hi):
        return jnp.where(odd, hi, lo), jnp.where(odd, lo, hi)

    turned = out_proj.T
    mine, other = halves(turned[:, :half], turned[:, half:])
    pair = jnp.concatenate(halves(mine, swap(other, 1)), axis=0)
    mine, other = halves(context[:, :half], context[:, half:])
    got = swap(other, 1)
    cut = pair.shape[0]
    blocks = along_z(pair, layers)
    twos = [list(range(i, min(i + 2, layers))) for i in range(0, layers, 2)]
    firsts = [
        spread_first(jnp.concatenate([blocks[k] for k in two], axis=0), cut * len(two))
        for two in twos
    ]
    exchange = lax.all_to_all(
        tie(exchange, *(v for first in firsts for v in first)),
        "expert",
        split_axis=0,
        concat_axis=0,
        tiled=True,
    )
    pieces, chips = [], []
    for two, first in zip(twos, firsts):
        pieces += spread_second(*first)
        for k in two:
            layer = jnp.bitwise_xor(me // LAYER, k)
            chips += [layer * (LAYER // 2) + jnp.bitwise_xor(me % LAYER // 2, q) for q in range(4)]
    mine, before = lax.optimization_barrier((mine, before))
    here = context.shape[0]
    keep, send = call(
        functools.partial(attention_kernel, len(twos), cut),
        [jax.ShapeDtypeStruct((here, wide), f32)] * 2,
        "svv" + "h" * len(pieces),
        (jnp.stack(chips).astype(jnp.int32), mine, got, *pieces),
        [
            pltpu.VMEM((out_proj.shape[1] * lax.axis_size("expert"), half), bf),
            pltpu.SemaphoreType.DMA((8 * layers,)),
        ],
    )
    return keep + swap(send, 1), before, exchange


def whole_rows(
    hidden_state,
    context,
    out_proj,
    norm_gain,
    router_weight,
    expert_in,
    expert_out,
    shared_in,
    shared_out,
    route_ids,
):
    bf, f32 = jnp.bfloat16, jnp.float32
    n = lax.axis_size("expert")
    layers = n // LAYER
    me = lax.axis_index("expert")
    odd = me % 2
    rows, top = route_ids.shape
    experts = router_weight.shape[1]
    wide = out_proj.shape[0]
    half = wide // 2
    cap = capacity_of(rows, top, experts)
    pack = 16
    win = expert_in[0].reshape(wide // pack, pack, 2, -1).transpose(0, 2, 1, 3)
    wout = expert_out[0]
    hidden = wout.shape[0]
    tile = LANES if hidden % LANES == 0 else hidden

    own = shared_in.shape[2] // n
    depth = shared_in.shape[0]
    hp = -(-own // LANES) * LANES
    three = jnp.concatenate([shared_in.transpose(1, 0, 2), shared_out.T[None]], axis=0)
    three = three.reshape(3, depth, n, own)
    three = jnp.pad(three, ((0, 0), (0, 0), (0, 0), (0, hp - own))).transpose(2, 0, 1, 3)

    attn, win, three = attention(context, out_proj, win, three)
    theirs = swap(three, 1)
    mixed = hidden_state.astype(f32) + attn
    inverse = lax.rsqrt(jnp.mean(mixed * mixed, axis=1, keepdims=True) + 1e-06)
    normed32 = mixed * inverse * norm_gain.astype(f32)
    normed = normed32.astype(bf)
    logits = jnp.dot(normed32, router_weight, precision=lax.Precision.HIGHEST)
    named = jnp.any(
        route_ids[:, :, None] == jnp.arange(experts, dtype=jnp.int32)[None, None, :], axis=1
    )
    highest = jnp.max(jnp.where(named, logits, -jnp.inf), axis=1, keepdims=True)
    raised = jnp.where(named, jnp.exp(logits - highest), 0.0)
    gates = raised / jnp.sum(raised, axis=1, keepdims=True)

    rest, parts = gates.T, []
    for _ in range(3):
        parts.append(lax.reduce_precision(rest, 8, 7))
        rest = rest - parts[-1]
    below = jnp.stack(parts).astype(bf).reshape(-1, half)
    extra = -(-below.shape[0] // 16) * 16
    below = jnp.pad(below, ((0, extra - below.shape[0]), (0, half)))
    blocks = along_z(jnp.concatenate([normed, below], axis=0), layers)

    each = half // rows
    chip_experts = (me, jnp.bitwise_xor(me, 1))
    idx = jnp.stack([v for e in chip_experts for v in (e // each, e % each)]).astype(jnp.int32)
    slots, span = 4 * cap, 4 * rows
    sds, dma = jax.ShapeDtypeStruct, pltpu.SemaphoreType.DMA
    xs = pltpu.VMEM((span, wide), bf)
    sent = pltpu.VMEM((4, extra, half), bf)

    def add_first(near_low, far_low, near_high, far_high):
        low = near_low + swap(far_low, 4).astype(f32)
        high = near_high + swap(far_high, 2).astype(f32)
        return low[:rows], low[rows:].astype(bf), high[:rows], high[rows:].astype(bf)

    order = [0] + sorted(range(1, layers), key=lambda k: (k != 1, -k))
    firsts, placed, once = {}, [], []

    def first(k, *others):
        if k not in firsts:
            firsts[k] = spread_first(tie(blocks[k], *others) if others else blocks[k], rows)
        return firsts[k]

    upcoming = spread_second(*first(0))
    for at, k in enumerate(order):
        pieces = upcoming
        after = [placed[-1][1]] if placed else [theirs]
        picked, lent = call(
            functools.partial(pick_kernel, cap, rows, experts, len(after)),
            [sds((slots, wide), bf)] * 2,
            "shhhh",
            (idx, *pieces),
            [
                xs,
                sent,
                pltpu.VMEM((2 * slots, span), bf),
                pltpu.VMEM((2 * slots, wide), bf),
                dma((8,)),
                dma((4,)),
                dma((2,)),
            ],
            after,
            False,
        )
        borrowed = swap(lent, 1)
        (hs,) = call(
            functools.partial(shared_kernel, rows, 1),
            [sds((span, 2 * hp), bf)],
            "hhhhhh",
            (three, theirs, *pieces),
            [xs, pltpu.VMEM((n, depth, 4 * hp), bf), dma((12,))],
            [lent],
        )
        after = [hs]
        if at + 1 < layers:
            after += first(order[at + 1], *([placed[0][1]] if at == 1 else []))
        done, back = call(
            functools.partial(expert_kernel, len(after)),
            [sds((slots, wide), bf)] * 2,
            "hhhh",
            (picked, borrowed, win, wout),
            [
                pltpu.VMEM((2 * slots, wide), bf),
                pltpu.VMEM((hidden // tile, wide // pack, pack, 2 * tile), bf),
                pltpu.VMEM((hidden, wide), bf),
                pltpu.VMEM((2 * slots, hidden), bf),
                pltpu.VMEM((2 * slots, wide), bf),
                dma((2,)),
                dma((2 * (hidden // tile) + 1,)),
                dma((2,)),
            ],
            after,
            False,
        )
        after = []
        if at + 1 < layers:
            upcoming = spread_second(*first(order[at + 1]))
            back = tie(back, upcoming[1], upcoming[3], *(blocks[2:3] if not at else []))
        if not at:
            for j in range(3, layers):
                if j & (j - 1):
                    blocks[j] = swap(tie(blocks[j & (j - 1)], done), LAYER * (j & -j))
        if placed:
            once.append(add_first(*placed[-1]))
            after = [once[-1][1], once[-1][3]]
        placed.append(
            call(
                functools.partial(place_kernel, cap, rows, experts, len(after)),
                [sds((2 * rows, half), t) for t in (f32, bf, f32, bf)],
                "svvvhhhh",
                (idx, done, swap(back, 1), hs, three, theirs, pieces[0], pieces[1]),
                [pltpu.VMEM((2 * rows, half), t) for t in (f32, bf, f32, bf)]
                + [
                    pltpu.VMEM((n, depth, 2 * hp), bf),
                    sent,
                    pltpu.VMEM((2, span, slots), bf),
                    pltpu.VMEM((2, span, LANES), f32),
                    dma((4,)),
                    dma((2,)),
                    dma((4,)),
                ],
                after,
                False,
            )
        )
    once.append(add_first(*placed[-1]))
    sums = {}
    for k, (low, far_low, high, far_high) in zip(order, once):
        low = low + swap(far_low, 2).astype(f32)
        high = high + swap(far_high, 4).astype(f32)
        sums[k] = jnp.concatenate([low, high], axis=1)
    for k in reversed(range(1, layers)):
        low = k & -k
        sums[k - low] = sums[k - low] + swap(sums[k].astype(bf), LAYER * low).astype(f32)
    return mixed + sums[0]


def solution(mesh):
    n, mp = mesh.shape["expert"], mesh.shape["mp"]
    fits = mp == 1 and n % LAYER == 0 and (n // LAYER) & (n // LAYER - 1) == 0
    per_device = whole_rows if fits else general
    return jax.shard_map(
        per_device,
        mesh=mesh,
        in_specs=(
            P("expert", "mp"),
            P("expert", "mp"),
            P("mp", "expert"),
            P("mp"),
            P("mp", None),
            P("expert", None, None, "mp"),
            P("expert", "mp", None),
            P("expert", None, "mp"),
            P("mp", "expert"),
            P("expert", None),
        ),
        out_specs=P("expert", "mp"),
        check_vma=False,
    )
```

```python
import functools

import jax
import jax.numpy as jnp
from jax import lax
from jax.experimental import pallas as pl
from jax.experimental.pallas import tpu as pltpu
from jax.sharding import PartitionSpec as P

LANES = 128
LAYER = 8


def capacity_of(rows, top, experts):
    return max(2, min(rows, rows * top // experts * 5 // 3))


def general(
    hidden_state,
    context,
    out_proj,
    norm_gain,
    router_weight,
    expert_in,
    expert_out,
    shared_in,
    shared_out,
    route_ids,
):
    rows_here, top = route_ids.shape
    experts = router_weight.shape[1]
    width = out_proj.shape[0] * lax.axis_size("mp")
    capacity = capacity_of(rows_here, top, experts)
    partial_attn = jnp.dot(
        context,
        lax.all_gather(out_proj, "expert", axis=1, tiled=True),
        preferred_element_type=jnp.float32,
    )
    attn = lax.psum_scatter(partial_attn, "mp", scatter_dimension=1, tiled=True)
    mixed = hidden_state.astype(jnp.float32) + attn
    gain = norm_gain.astype(jnp.float32)
    squares = lax.psum(jnp.sum(mixed * mixed, axis=1), "mp")
    inverse = lax.rsqrt(squares / width + 1e-06)[:, None]
    normed32 = mixed * inverse * gain
    logits = lax.psum(jnp.dot(normed32, router_weight, precision=lax.Precision.HIGHEST), "mp")
    normed = normed32.astype(jnp.bfloat16)
    gates = jax.nn.softmax(jnp.take_along_axis(logits, route_ids, axis=1), axis=1)
    full_rows = lax.all_gather(normed, "mp", axis=1, tiled=True)
    shared_width = shared_in.shape[2]
    piece = lax.all_gather(shared_in, "expert", axis=0, tiled=True)
    shared_both = jnp.dot(
        full_rows,
        piece.reshape(piece.shape[0], 2 * shared_width),
        preferred_element_type=jnp.float32,
    )
    shared_both = shared_both.reshape(rows_here, 2, shared_width)
    shared_hidden = (jax.nn.silu(shared_both[:, 0]) * shared_both[:, 1]).astype(jnp.bfloat16)
    shared_part = jnp.dot(
        shared_hidden,
        lax.all_gather(shared_out, "expert", axis=1, tiled=True),
        preferred_element_type=jnp.float32,
    )
    flat = route_ids.reshape(-1)
    onehot = (flat[:, None] == jnp.arange(experts, dtype=jnp.int32)[None, :]).astype(jnp.int32)
    position = jnp.sum(onehot * jnp.cumsum(onehot, axis=0), axis=1) - 1
    slot_of = flat * capacity + position
    source = (
        jnp.zeros((experts * capacity,), jnp.int32)
        .at[slot_of]
        .set(jnp.arange(flat.shape[0], dtype=jnp.int32) // top)
    )
    filled = jnp.zeros((experts * capacity,), jnp.bool_).at[slot_of].set(True)
    outgoing = jnp.where(filled[:, None], normed[source], jnp.zeros((), jnp.bfloat16)).reshape(
        experts, capacity, normed.shape[1]
    )
    quarter = expert_in.shape[3]
    weights_in = expert_in[0].reshape(width, 2 * quarter)
    incoming = lax.all_to_all(outgoing, "expert", split_axis=0, concat_axis=0, tiled=True)
    sources = incoming.shape[0]
    items = incoming.shape[1]
    gathered = lax.all_gather(incoming, "mp", axis=2, tiled=True).reshape(sources * items, width)
    inner = jnp.dot(gathered, weights_in, preferred_element_type=jnp.float32).reshape(
        -1, 2, quarter
    )
    hidden = (jax.nn.silu(inner[:, 0]) * inner[:, 1]).astype(jnp.bfloat16)
    partial_out = jnp.dot(hidden, expert_out[0], preferred_element_type=jnp.float32).astype(
        jnp.bfloat16
    )
    partial_out = partial_out.reshape(sources, items, width)
    result = lax.all_to_all(partial_out, "expert", split_axis=0, concat_axis=0, tiled=True)
    picked = result.reshape(experts * capacity, result.shape[2])[slot_of]
    slot_total = lax.psum_scatter(
        lax.optimization_barrier(picked).astype(jnp.float32).astype(jnp.bfloat16),
        "mp",
        scatter_dimension=1,
        tiled=True,
    )
    expert_sum = lax.optimization_barrier(slot_total).astype(jnp.float32)
    expert_sum = expert_sum.reshape(rows_here, top, expert_sum.shape[1])
    routed = jnp.sum(gates[:, :, None] * expert_sum, axis=1)
    shared = lax.psum_scatter(shared_part, "mp", scatter_dimension=1, tiled=True)
    return mixed + routed + shared


def swap(x, bit):
    n = lax.axis_size("expert")
    return lax.ppermute(x, "expert", [(i, i ^ bit) for i in range(n)])


def silu(v):
    return v / (1.0 + jnp.exp(-v))


def spread_first(block, rows):
    half = block.shape[1] // 2
    h0, h1 = block[:, :half], block[:rows, half:]
    return jnp.concatenate([h0, swap(h0, 2)], axis=0), jnp.concatenate([h1, swap(h1, 4)], axis=0)


def spread_second(l0, l1):
    return l0, swap(l0, 4), l1, swap(l1, 2)


def along_z(block, layers):
    blocks = [block]
    for k in range(1, layers):
        low = k & -k
        blocks.append(swap(blocks[k - low], LAYER * low))
    return blocks


def tie(x, *others):
    return lax.optimization_barrier((x, *others))[0]


class Copies:
    def __init__(self, sems):
        self.sems, self.all = sems, []

    def start(self, src, dst):
        c = pltpu.make_async_copy(src, dst, self.sems.at[len(self.all)])
        c.start()
        self.all.append(c)

    def wait(self):
        for c in self.all:
            c.wait()


PIECES = ((0, 0, (0, 1)), (1, 0, (2, 3)), (2, 1, (0, 2)), (3, 1, (1, 3)))


def fetch_rows(copies, pieces, rows, xs):
    half = xs.shape[1] // 2
    for n, h, chips in PIECES:
        stride = pieces[n].shape[0] // 2
        for a, q in enumerate(chips):
            copies.start(
                pieces[n].at[pl.ds(a * stride, rows)],
                xs.at[pl.ds(q * rows, rows), pl.ds(h * half, half)],
            )


def fetch_gates(copies, left, rows, to):
    for piece, (_, _, chips) in zip(left, PIECES):
        stride = piece.shape[0] // 2
        for a, q in enumerate(chips):
            copies.start(piece.at[pl.ds(a * stride + rows, stride - rows)], to.at[q])


def slots_of(sent, idx_ref, expert, experts, cap, rows):
    extra, half = sent.shape[1:]
    each = half // rows
    tall = experts // each
    line, column = idx_ref[2 * expert], idx_ref[2 * expert + 1]
    r = lax.broadcasted_iota(jnp.int32, (extra, half), 0)
    wanted = (r == line) | (r == line + tall) | (r == line + 2 * tall)
    found = []
    for q in range(4):
        parts = jnp.where(wanted, sent[q].astype(jnp.float32), 0.0)
        parts = jnp.sum(parts, axis=0, keepdims=True)
        g = jnp.zeros((1, rows), jnp.float32)
        for j in range(each):
            g = jnp.where(column == j, parts[:, j * rows : (j + 1) * rows], g)
        found.append(g)
    g = jnp.concatenate(found, axis=0)
    chosen = g > 0.0
    r_io = lax.broadcasted_iota(jnp.int32, (rows, rows), 0)
    c_io = lax.broadcasted_iota(jnp.int32, (rows, rows), 1)
    upto = jnp.where(r_io <= c_io, 1.0, 0.0).astype(jnp.bfloat16)
    count = jnp.dot(
        jnp.where(chosen, 1.0, 0.0).astype(jnp.bfloat16), upto, preferred_element_type=jnp.float32
    ).astype(jnp.int32)
    first = lax.broadcasted_iota(jnp.int32, (4, rows), 0) * cap
    return g, jnp.where(chosen, first + count - 1, -1)


def steps(total, most):
    step = min(most, total)
    return [(n, step) for n in range(0, total, step)]


def attention_kernel(groups, rows, idx_ref, mine_ref, other_ref, *rest):
    pieces, (keep_ref, send_ref, w_v, sems) = rest[: 4 * groups], rest[4 * groups :]
    half = w_v.shape[1] // 2
    count = pieces[0].shape[0] // (2 * rows)
    copies = Copies(sems)
    for g in range(groups):
        l0, r0, l1, r1 = pieces[4 * g : 4 * g + 4]
        for h, (near, far, first, second) in enumerate(((l0, r0, 1, 2), (l1, r1, 2, 1))):
            for piece, base in ((near, 0), (far, second)):
                for a, q in enumerate((base, base + first)):
                    for i in range(count):
                        chip = idx_ref[(g * count + i) * 4 + q]
                        to = pl.ds(pl.multiple_of(chip * rows, rows), rows)
                        copies.start(
                            piece.at[pl.ds((a * count + i) * rows, rows)],
                            w_v.at[to, pl.ds(h * half, half)],
                        )
    copies.wait()
    both = jnp.concatenate([mine_ref[...], other_ref[...]], axis=0)
    here = mine_ref.shape[0]
    for n, step in steps(w_v.shape[0], 512):
        part = lax.dot_general(
            both,
            w_v[pl.ds(n, step), :],
            (((1,), (1,)), ((), ())),
            preferred_element_type=jnp.float32,
        )
        keep_ref[:, pl.ds(n, step)] = part[:here]
        send_ref[:, pl.ds(n, step)] = part[here:]


def pick_kernel(cap, rows, experts, unused, idx_ref, *rest):
    pieces = rest[:4]
    mine_ref, other_ref, xs, sent, pick, out_v, x_sem, g_sem, o_sem = rest[4 + unused :]
    gates, copies = Copies(g_sem), Copies(x_sem)
    fetch_gates(gates, pieces[:2], rows, sent)
    fetch_rows(copies, pieces, rows, xs)
    slots = 4 * cap
    numbers = lax.broadcasted_iota(jnp.int32, (slots, rows), 0)
    gates.wait()
    for e in range(2):
        _, slot = slots_of(sent, idx_ref, e, experts, cap, rows)
        for q in range(4):
            pick[pl.ds(e * slots, slots), pl.ds(q * rows, rows)] = jnp.where(
                numbers == slot[q : q + 1, :], 1.0, 0.0
            ).astype(jnp.bfloat16)
    copies.wait()
    for n, step in steps(xs.shape[1], 512):
        out_v[:, pl.ds(n, step)] = jnp.dot(
            pick[...], xs[:, pl.ds(n, step)], preferred_element_type=jnp.float32
        ).astype(jnp.bfloat16)
    outs = Copies(o_sem)
    outs.start(out_v.at[pl.ds(slots, slots)], other_ref)
    outs.start(out_v.at[pl.ds(0, slots)], mine_ref)
    outs.wait()


def shared_kernel(rows, unused, three_ref, theirs_ref, *rest):
    pieces, (hs_ref, xs, w_v, x_sem) = rest[:4], rest[4 + unused :]
    hp = three_ref.shape[3]
    copies = Copies(x_sem)
    fetch_rows(copies, pieces, rows, xs)
    for e, ref in enumerate((three_ref, theirs_ref)):
        for h in range(2):
            copies.start(ref.at[:, h], w_v.at[:, :, pl.ds((2 * h + e) * hp, hp)])
    copies.wait()
    w = w_v[...].reshape(xs.shape[1], 4 * hp)
    for m, step in steps(4 * rows, 2 * rows):
        both = jnp.dot(xs[pl.ds(m, step), :], w, preferred_element_type=jnp.float32)
        hs_ref[pl.ds(m, step), :] = (silu(both[:, : 2 * hp]) * both[:, 2 * hp :]).astype(
            jnp.bfloat16
        )


def expert_kernel(unused, mine_ref, other_ref, win_ref, wout_ref, *rest):
    mine_out, other_out, x_v, win_v, wout_v, hid_v, y_v, x_sem, w_sem, o_sem = rest[unused:]
    slots, wide = mine_ref.shape
    tiles, tile = win_v.shape[0], win_v.shape[3] // 2
    rows = Copies(x_sem)
    rows.start(mine_ref, x_v.at[pl.ds(0, slots)])
    rows.start(other_ref, x_v.at[pl.ds(slots, slots)])
    copies = Copies(w_sem)
    for t in range(tiles):
        for h in range(2):
            copies.start(
                win_ref.at[:, h, :, pl.ds(t * tile, tile)],
                win_v.at[t, :, :, pl.ds(h * tile, tile)],
            )
    copies.start(wout_ref, wout_v)
    rows.wait()
    here = 0
    for t in range(tiles):
        if t == here:
            here = min(2 * here + 1, tiles)
            for c in copies.all[2 * t : 2 * here]:
                c.wait()
        both = jnp.dot(
            x_v[...], win_v[t].reshape(wide, 2 * tile), preferred_element_type=jnp.float32
        )
        hid_v[:, pl.ds(t * tile, tile)] = (silu(both[:, :tile]) * both[:, tile:]).astype(
            jnp.bfloat16
        )
    copies.all[2 * tiles].wait()
    outs = Copies(o_sem)
    for n, step in steps(wide, 512):
        y_v[:, pl.ds(n, step)] = jnp.dot(
            hid_v[...], wout_v[:, pl.ds(n, step)], preferred_element_type=jnp.float32
        ).astype(jnp.bfloat16)
    outs.start(y_v.at[pl.ds(slots, slots)], other_out)
    outs.start(y_v.at[pl.ds(0, slots)], mine_out)
    outs.wait()


def place_kernel(cap, rows, experts, unused, idx_ref, mine_ref, other_ref, hs_ref, *rest):
    three_ref, theirs_ref, l0, r0 = rest[:4]
    refs, rest = rest[4 + unused : 8 + unused], rest[8 + unused :]
    bufs, (w_v, sent, place, gate_col, g_sem, w_sem, o_sem) = rest[:4], rest[4:]
    near_low, far_low, near_high, far_high = bufs
    wide, half = mine_ref.shape[1], near_low.shape[1]
    hp = three_ref.shape[3]
    slots = 4 * cap
    f32 = jnp.float32
    gates, copies = Copies(g_sem), Copies(w_sem)
    fetch_gates(gates, (l0, r0), rows, sent)
    for e, ref in enumerate((three_ref, theirs_ref)):
        copies.start(ref.at[:, 2], w_v.at[:, :, pl.ds(e * hp, hp)])
    r_io = lax.broadcasted_iota(jnp.int32, (rows, rows), 0)
    c_io = lax.broadcasted_iota(jnp.int32, (rows, rows), 1)
    eye = r_io == c_io
    numbers = lax.broadcasted_iota(jnp.int32, (rows, slots), 1)
    gates.wait()
    for e in range(2):
        g, slot = slots_of(sent, idx_ref, e, experts, cap, rows)
        for q in range(4):
            at = pl.ds(q * rows, rows)
            col = jnp.sum(jnp.where(eye, slot[q : q + 1, :], 0), axis=1, keepdims=True)
            place[e, at, :] = jnp.where(numbers == col, 1.0, 0.0).astype(jnp.bfloat16)
            gcol = jnp.sum(jnp.where(eye, g[q : q + 1, :], 0.0), axis=1, keepdims=True)
            gate_col[e, at, :] = jnp.broadcast_to(gcol, (rows, LANES))
    copies.wait()
    depth = w_v.shape[1]
    outs = Copies(o_sem)
    for n, step in steps(wide, min(256, half)):
        cols = pl.ds(n, step)
        if step % depth == 0:
            down = w_v[pl.ds(n // depth, step // depth)].reshape(step, 2 * hp)
        else:
            down = w_v[...].reshape(wide, 2 * hp)[n : n + step]
        total = lax.dot_general(
            hs_ref[...], down, (((1,), (1,)), ((), ())), preferred_element_type=f32
        )
        for e, ref in enumerate((mine_ref, other_ref)):
            y = jnp.dot(place[e], ref[:, cols], preferred_element_type=f32)
            total = total + gate_col[e][:, 0:1] * y
        if n < half:
            near, far, order, at = near_low, far_low, (0, 1, 2, 3), pl.ds(n, step)
        else:
            near, far, order, at = near_high, far_high, (0, 2, 1, 3), pl.ds(n - half, step)
        for a in range(2):
            to = pl.ds(a * rows, rows)
            q = order[a] * rows
            near[to, at] = total[q : q + rows]
            q = order[2 + a] * rows
            far[to, at] = total[q : q + rows].astype(far.dtype)
        if (n + step) % half == 0:
            k = 2 * (n // half)
            outs.start(bufs[k + 1], refs[k + 1])
            outs.start(bufs[k], refs[k])
    outs.wait()


def call(body, out_shape, in_specs, args, scratch, after=(), outs_in_vmem=True):
    vmem = pl.BlockSpec(memory_space=pltpu.VMEM)
    hbm = pl.BlockSpec(memory_space=pl.ANY)
    kinds = {"s": pl.BlockSpec(memory_space=pltpu.SMEM), "v": vmem, "h": hbm}
    return pl.pallas_call(
        body,
        out_shape=out_shape,
        in_specs=[kinds[k] for k in in_specs] + [hbm] * len(after),
        out_specs=tuple([vmem if outs_in_vmem else hbm] * len(out_shape)),
        scratch_shapes=scratch,
        compiler_params=pltpu.CompilerParams(vmem_limit_bytes=48 * 1024 * 1024),
        cost_estimate=pl.CostEstimate(flops=1, bytes_accessed=1, transcendentals=0),
    )(*args, *after)


def attention(context, out_proj, before, exchange):
    bf, f32 = jnp.bfloat16, jnp.float32
    me = lax.axis_index("expert")
    layers = lax.axis_size("expert") // LAYER
    odd = me % 2 == 1
    wide = context.shape[1]
    half = wide // 2

    def halves(lo, hi):
        return jnp.where(odd, hi, lo), jnp.where(odd, lo, hi)

    turned = out_proj.T
    mine, other = halves(turned[:, :half], turned[:, half:])
    pair = jnp.concatenate(halves(mine, swap(other, 1)), axis=0)
    mine, other = halves(context[:, :half], context[:, half:])
    got = swap(other, 1)
    cut = pair.shape[0]
    blocks = along_z(pair, layers)
    twos = [list(range(i, min(i + 2, layers))) for i in range(0, layers, 2)]
    firsts = [
        spread_first(jnp.concatenate([blocks[k] for k in two], axis=0), cut * len(two))
        for two in twos
    ]
    pieces, chips = [], []
    for two, first in zip(twos, firsts):
        pieces += spread_second(*first)
        for k in two:
            layer = jnp.bitwise_xor(me // LAYER, k)
            chips += [layer * (LAYER // 2) + jnp.bitwise_xor(me % LAYER // 2, q) for q in range(4)]
    exchange = lax.all_to_all(
        tie(exchange, *pieces[:4], *firsts[-1]),
        "expert",
        split_axis=0,
        concat_axis=0,
        tiled=True,
    )
    mine, before = lax.optimization_barrier((mine, before))
    here = context.shape[0]
    keep, send = call(
        functools.partial(attention_kernel, len(twos), cut),
        [jax.ShapeDtypeStruct((here, wide), f32)] * 2,
        "svv" + "h" * len(pieces),
        (jnp.stack(chips).astype(jnp.int32), mine, got, *pieces),
        [
            pltpu.VMEM((out_proj.shape[1] * lax.axis_size("expert"), half), bf),
            pltpu.SemaphoreType.DMA((8 * layers,)),
        ],
    )
    return keep + swap(send, 1), before, exchange


def whole_rows(
    hidden_state,
    context,
    out_proj,
    norm_gain,
    router_weight,
    expert_in,
    expert_out,
    shared_in,
    shared_out,
    route_ids,
):
    bf, f32 = jnp.bfloat16, jnp.float32
    n = lax.axis_size("expert")
    layers = n // LAYER
    me = lax.axis_index("expert")
    odd = me % 2
    rows, top = route_ids.shape
    experts = router_weight.shape[1]
    wide = out_proj.shape[0]
    half = wide // 2
    cap = capacity_of(rows, top, experts)
    pack = 16
    win = expert_in[0].reshape(wide // pack, pack, 2, -1).transpose(0, 2, 1, 3)
    wout = expert_out[0]
    hidden = wout.shape[0]
    tile = LANES if hidden % LANES == 0 else hidden

    own = shared_in.shape[2] // n
    depth = shared_in.shape[0]
    hp = -(-own // LANES) * LANES
    three = jnp.concatenate([shared_in.transpose(1, 0, 2), shared_out.T[None]], axis=0)
    three = three.reshape(3, depth, n, own)
    three = jnp.pad(three, ((0, 0), (0, 0), (0, 0), (0, hp - own))).transpose(2, 0, 1, 3)

    attn, win, three = attention(context, out_proj, win, three)
    theirs = swap(three, 1)
    mixed = hidden_state.astype(f32) + attn
    inverse = lax.rsqrt(jnp.mean(mixed * mixed, axis=1, keepdims=True) + 1e-06)
    normed32 = mixed * inverse * norm_gain.astype(f32)
    normed = normed32.astype(bf)
    logits = jnp.dot(normed32, router_weight, precision=lax.Precision.HIGHEST)
    named = jnp.any(
        route_ids[:, :, None] == jnp.arange(experts, dtype=jnp.int32)[None, None, :], axis=1
    )
    highest = jnp.max(jnp.where(named, logits, -jnp.inf), axis=1, keepdims=True)
    raised = jnp.where(named, jnp.exp(logits - highest), 0.0)
    gates = raised / jnp.sum(raised, axis=1, keepdims=True)

    rest, parts = gates.T, []
    for _ in range(3):
        parts.append(lax.reduce_precision(rest, 8, 7))
        rest = rest - parts[-1]
    below = jnp.stack(parts).astype(bf).reshape(-1, half)
    extra = -(-below.shape[0] // 16) * 16
    below = jnp.pad(below, ((0, extra - below.shape[0]), (0, half)))
    blocks = along_z(jnp.concatenate([normed, below], axis=0), layers)

    each = half // rows
    chip_experts = (me, jnp.bitwise_xor(me, 1))
    idx = jnp.stack([v for e in chip_experts for v in (e // each, e % each)]).astype(jnp.int32)
    slots, span = 4 * cap, 4 * rows
    sds, dma = jax.ShapeDtypeStruct, pltpu.SemaphoreType.DMA
    xs = pltpu.VMEM((span, wide), bf)
    sent = pltpu.VMEM((4, extra, half), bf)

    def add_first(near_low, far_low, near_high, far_high):
        low = near_low + swap(far_low, 4).astype(f32)
        high = near_high + swap(far_high, 2).astype(f32)
        return low[:rows], low[rows:].astype(bf), high[:rows], high[rows:].astype(bf)

    order = [0] + sorted(range(1, layers), key=lambda k: (k != 1, -k))
    firsts, placed, once = {}, [], []

    def first(k):
        if k not in firsts:
            firsts[k] = spread_first(blocks[k], rows)
        return firsts[k]

    upcoming = spread_second(*first(0))
    for at, k in enumerate(order):
        pieces = upcoming
        after = [placed[-1][1]] if placed else [theirs]
        picked, lent = call(
            functools.partial(pick_kernel, cap, rows, experts, len(after)),
            [sds((slots, wide), bf)] * 2,
            "shhhh",
            (idx, *pieces),
            [
                xs,
                sent,
                pltpu.VMEM((2 * slots, span), bf),
                pltpu.VMEM((2 * slots, wide), bf),
                dma((8,)),
                dma((4,)),
                dma((2,)),
            ],
            after,
            False,
        )
        borrowed = swap(lent, 1)
        (hs,) = call(
            functools.partial(shared_kernel, rows, 1),
            [sds((span, 2 * hp), bf)],
            "hhhhhh",
            (three, theirs, *pieces),
            [xs, pltpu.VMEM((n, depth, 4 * hp), bf), dma((12,))],
            [lent],
        )
        after = [hs]
        if at + 1 < layers:
            after += first(order[at + 1])
        done, back = call(
            functools.partial(expert_kernel, len(after)),
            [sds((slots, wide), bf)] * 2,
            "hhhh",
            (picked, borrowed, win, wout),
            [
                pltpu.VMEM((2 * slots, wide), bf),
                pltpu.VMEM((hidden // tile, wide // pack, pack, 2 * tile), bf),
                pltpu.VMEM((hidden, wide), bf),
                pltpu.VMEM((2 * slots, hidden), bf),
                pltpu.VMEM((2 * slots, wide), bf),
                dma((2,)),
                dma((2 * (hidden // tile) + 1,)),
                dma((2,)),
            ],
            after,
            False,
        )
        after = []
        if at + 1 < layers:
            upcoming = spread_second(*first(order[at + 1]))
            back = tie(back, upcoming[1], upcoming[3])
        if placed:
            once.append(add_first(*placed[-1]))
            after = [once[-1][1], once[-1][3]]
        placed.append(
            call(
                functools.partial(place_kernel, cap, rows, experts, len(after)),
                [sds((2 * rows, half), t) for t in (f32, bf, f32, bf)],
                "svvvhhhh",
                (idx, done, swap(back, 1), hs, three, theirs, pieces[0], pieces[1]),
                [pltpu.VMEM((2 * rows, half), t) for t in (f32, bf, f32, bf)]
                + [
                    pltpu.VMEM((n, depth, 2 * hp), bf),
                    sent,
                    pltpu.VMEM((2, span, slots), bf),
                    pltpu.VMEM((2, span, LANES), f32),
                    dma((4,)),
                    dma((2,)),
                    dma((4,)),
                ],
                after,
                False,
            )
        )
    once.append(add_first(*placed[-1]))
    sums = {}
    for k, (low, far_low, high, far_high) in zip(order, once):
        low = low + swap(far_low, 2).astype(f32)
        high = high + swap(far_high, 4).astype(f32)
        sums[k] = jnp.concatenate([low, high], axis=1)
    for k in reversed(range(1, layers)):
        low = k & -k
        sums[k - low] = sums[k - low] + swap(sums[k].astype(bf), LAYER * low).astype(f32)
    return mixed + sums[0]


def solution(mesh):
    n, mp = mesh.shape["expert"], mesh.shape["mp"]
    fits = mp == 1 and n % LAYER == 0 and (n // LAYER) & (n // LAYER - 1) == 0
    per_device = whole_rows if fits else general
    return jax.shard_map(
        per_device,
        mesh=mesh,
        in_specs=(
            P("expert", "mp"),
            P("expert", "mp"),
            P("mp", "expert"),
            P("mp"),
            P("mp", None),
            P("expert", None, None, "mp"),
            P("expert", "mp", None),
            P("expert", None, "mp"),
            P("mp", "expert"),
            P("expert", None),
        ),
        out_specs=P("expert", "mp"),
        check_vma=False,
    )
```
